128 devices in a mesh: dp: 4 (over z_lo, core), fsdp: 32 (over z_hi, y, x).
Axes of the slice: x: 4, y: 4, z: 4 (z_hi: 2, z_lo: 2; z = z_hi * 2 + z_lo), core: 2. Of those that a mesh axis runs over, the one named last changes fastest.
Arguments:
- tokens: bfloat16 [32768, 640], P(('dp', 'fsdp')), may hold values from -6 to 6
- cotangent: bfloat16 [3, 32768, 640], P(None, ('dp', 'fsdp')), may hold values from -6 to 6
- segment_ids: int32 [16, 2048], P('dp'), may hold values from 0 to 2, as said below
- width_mask: int32 [16, 3], P('dp'), may hold values from 0 to 1, as said below
- q_codes: bfloat16 [640, 1024], P(('dp', 'fsdp')), may hold values from -128 to 127, as said below
- kv_codes: bfloat16 [640, 512], P(('dp', 'fsdp')), may hold values from -128 to 127, as said below
- o_codes: bfloat16 [1024, 640], P(('dp', 'fsdp')), may hold values from -128 to 127, as said below
- gate_codes: bfloat16 [640, 2048], P(('dp', 'fsdp')), may hold values from -128 to 127, as said below
- up_codes: bfloat16 [640, 2048], P(('dp', 'fsdp')), may hold values from -128 to 127, as said below
- down_codes: bfloat16 [2048, 640], P(('dp', 'fsdp')), may hold values from -128 to 127, as said below
- q_scale: float32 [1024], P(('dp', 'fsdp')), may hold values from 1 to 4
- kv_scale: float32 [512], P(('dp', 'fsdp')), may hold values from 1 to 4
- o_scale: float32 [640], P(('dp', 'fsdp')), may hold values from 1 to 4
- gate_scale: float32 [2048], P(('dp', 'fsdp')), may hold values from 1 to 4
- up_scale: float32 [2048], P(('dp', 'fsdp')), may hold values from 1 to 4
- down_scale: float32 [640], P(('dp', 'fsdp')), may hold values from 1 to 4
- norm_gains: float32 [640, 4], P(('dp', 'fsdp')), may hold values from 0.5 to 1.5
Outputs:
- outputs: float32 [3, 32768, 640], P(None, ('dp', 'fsdp'))
- grad_tokens: float32 [32768, 640], P(('dp', 'fsdp'))
- grad_q_codes: float32 [640, 1024], P(('dp', 'fsdp'))
- grad_kv_codes: float32 [640, 512], P(('dp', 'fsdp'))
- grad_o_codes: float32 [1024, 640], P(('dp', 'fsdp'))
- grad_gate_codes: float32 [640, 2048], P(('dp', 'fsdp'))
- grad_up_codes: float32 [640, 2048], P(('dp', 'fsdp'))
- grad_down_codes: float32 [2048, 640], P(('dp', 'fsdp'))
- grad_q_scale: float32 [1024], P(('dp', 'fsdp'))
- grad_kv_scale: float32 [512], P(('dp', 'fsdp'))
- grad_o_scale: float32 [640], P(('dp', 'fsdp'))
- grad_gate_scale: float32 [2048], P(('dp', 'fsdp'))
- grad_up_scale: float32 [2048], P(('dp', 'fsdp'))
- grad_down_scale: float32 [640], P(('dp', 'fsdp'))
- grad_norm_gains: float32 [640, 4], P(('dp', 'fsdp'))
The draws below stay inside these ranges and needn't reach their ends.
Inputs may be any that keep to these rules, and one draw needn't show every extreme that they name: `width_mask`: every sequence runs at least one width. `q_codes`: whole numbers. `kv_codes`: whole numbers. `o_codes`: whole numbers. `gate_codes`: whole numbers. `up_codes`: whole numbers. `down_codes`: whole numbers. `segment_ids`: each sequence's ids start at 0 and never fall.
All inputs are finite; a program needn't handle non-finite values.
Results may differ from the reference program's by a relative error of at most 0.024.
Values may be sent and summed in bfloat16 or wider, within the bound.
No kernel may reach another device: no remote copies, remote signals or barrier semaphores. Data moves between devices by JAX's collectives and lax.ppermute only.
A program may use at most 320 MiB of HBM per device.

```python
import math
import jax
import jax.numpy as jnp
from jax import lax

D = 640
HEADS = 4
HD = 256
FF = 2048
WINDOW = 512
LEN = 2048
SEQS = 16
TOKENS = 32768


def random_codes(key, rows, columns):
    return jax.random.randint(key, (rows, columns), -128, 128).astype(jnp.float32).astype(jnp.bfloat16)


def draw_width_mask(key, part):
    key = jax.random.fold_in(key, 17)
    ticket = jax.random.randint(key, (SEQS, 3), 0, 4)
    chosen = (ticket < jnp.array([3, 2, 1], jnp.int32)[None, :]).astype(jnp.int32)
    last_row = (jnp.arange(SEQS) == SEQS - 1)[:, None]
    third_column = (jnp.arange(3) == 2)[None, :]
    chosen = jnp.where(last_row & third_column, 0, chosen)
    empty_rows = jnp.sum(chosen, axis=1, keepdims=True) == 0
    first_column = (jnp.arange(3) == 0)[None, :]
    return jnp.where(empty_rows & first_column, 1, chosen).astype(jnp.int32)


def draw_segment_ids(key, part):
    key = jax.random.fold_in(key, 19)
    key_turn, key_count, key_first, key_second = jax.random.split(key, 4)
    block_total = SEQS // 4
    turn = jax.random.randint(key_turn, (block_total, 1), 0, 4)
    role = (jnp.arange(4)[None, :] - turn) % 4
    cuts = jax.random.randint(key_count, (block_total, 4), 1, 3)
    cuts = jnp.where(role == 0, 0, jnp.where(role == 1, 2, cuts)).reshape(SEQS)
    first_cut = jax.random.randint(key_first, (SEQS,), LEN // 8, LEN // 2)
    second_cut = jax.random.randint(key_second, (SEQS,), LEN // 2, 7 * LEN // 8)
    position = jnp.arange(LEN)[None, :]
    one_more = ((cuts[:, None] >= 1) & (position >= first_cut[:, None])).astype(jnp.int32)
    two_more = ((cuts[:, None] >= 2) & (position >= second_cut[:, None])).astype(jnp.int32)
    return (one_more + two_more).astype(jnp.int32)


def draw_q_codes(key, part):
    key = jax.random.fold_in(key, 21)
    return random_codes(key, D, HEADS * HD)


def draw_kv_codes(key, part):
    key = jax.random.fold_in(key, 22)
    return random_codes(key, D, 2 * HD)


def draw_o_codes(key, part):
    key = jax.random.fold_in(key, 23)
    return random_codes(key, HEADS * HD, D)


def draw_gate_codes(key, part):
    key = jax.random.fold_in(key, 24)
    return random_codes(key, D, FF)


def draw_up_codes(key, part):
    key = jax.random.fold_in(key, 25)
    return random_codes(key, D, FF)


def draw_down_codes(key, part):
    key = jax.random.fold_in(key, 26)
    return random_codes(key, FF, D)


def block_scale(key, dims, cuts, smallest, high):
    def one(dim, parts):
        steps = jax.random.uniform(jax.random.fold_in(jax.random.fold_in(key, 6), dim), (parts,), jnp.float32, smallest / len(cuts), high / len(cuts))
        return jnp.repeat(jnp.exp(steps), dims[dim] // parts).reshape((-1,) + (1,) * (len(dims) - dim - 1))

    gain = one(*cuts[0])
    for cut in cuts[1:]:
        gain = gain * one(*cut)
    return gain


def gaussian(rng, dims, spread, most, cuts=(), dtype=jnp.bfloat16):
    values = spread * jax.random.normal(rng, dims, jnp.float32)
    if cuts:
        values = values * block_scale(rng, dims, cuts, -0.22, 0.18)
    return jnp.clip(values, -most, most).astype(dtype)


def setup_inputs(seed: int = 0) -> dict:
    arg_keys = jax.random.split(jax.random.key(seed), 18)
    tokens = gaussian(arg_keys[0], (TOKENS, D), 1.0, 6.0, ((0, 128),))
    cotangent = gaussian(arg_keys[1], (3, TOKENS, D), 1.0, 6.0, ((1, 128),))
    segment_ids = draw_segment_ids(jax.random.fold_in(arg_keys[17], 71), 0)
    width_mask = draw_width_mask(jax.random.fold_in(arg_keys[17], 71), 0)
    q_codes = draw_q_codes(jax.random.fold_in(arg_keys[17], 71), 0)
    kv_codes = draw_kv_codes(jax.random.fold_in(arg_keys[17], 71), 0)
    o_codes = draw_o_codes(jax.random.fold_in(arg_keys[17], 71), 0)
    gate_codes = draw_gate_codes(jax.random.fold_in(arg_keys[17], 71), 0)
    up_codes = draw_up_codes(jax.random.fold_in(arg_keys[17], 71), 0)
    down_codes = draw_down_codes(jax.random.fold_in(arg_keys[17], 71), 0)
    q_scale = jnp.clip(jnp.exp(math.log(4.0) - 1.3862944 * jax.random.uniform(arg_keys[10], (HEADS * HD,), jnp.float32) ** block_scale(arg_keys[10], (HEADS * HD,), ((0, 128),), -0.2, 0.2)), 1.0, 4.0)
    kv_scale = jnp.clip(jnp.exp(math.log(4.0) - 1.3862944 * jax.random.uniform(arg_keys[11], (2 * HD,), jnp.float32) ** block_scale(arg_keys[11], (2 * HD,), ((0, 128),), -0.2, 0.2)), 1.0, 4.0)
    o_scale = jnp.clip(jnp.exp(math.log(4.0) - 1.3862944 * jax.random.uniform(arg_keys[12], (D,), jnp.float32) ** block_scale(arg_keys[12], (D,), ((0, 128),), -0.2, 0.2)), 1.0, 4.0)
    gate_scale = jnp.clip(jnp.exp(math.log(4.0) - 1.3862944 * jax.random.uniform(arg_keys[13], (FF,), jnp.float32) ** block_scale(arg_keys[13], (FF,), ((0, 128),), -0.2, 0.2)), 1.0, 4.0)
    up_scale = jnp.clip(jnp.exp(math.log(4.0) - 1.3862944 * jax.random.uniform(arg_keys[14], (FF,), jnp.float32) ** block_scale(arg_keys[14], (FF,), ((0, 128),), -0.2, 0.2)), 1.0, 4.0)
    down_scale = jnp.clip(jnp.exp(math.log(4.0) - 1.3862944 * jax.random.uniform(arg_keys[15], (D,), jnp.float32) ** block_scale(arg_keys[15], (D,), ((0, 128),), -0.2, 0.2)), 1.0, 4.0)
    norm_gains = jnp.clip(1.0 + 0.1 * jax.random.normal(arg_keys[16], (D, 4), jnp.float32), 0.5, 1.5)
    return dict(tokens=tokens, cotangent=cotangent, segment_ids=segment_ids, width_mask=width_mask, q_codes=q_codes, kv_codes=kv_codes, o_codes=o_codes, gate_codes=gate_codes, up_codes=up_codes, down_codes=down_codes, q_scale=q_scale, kv_scale=kv_scale, o_scale=o_scale, gate_scale=gate_scale, up_scale=up_scale, down_scale=down_scale, norm_gains=norm_gains)


@jax.custom_vjp
def low(v):
    return lax.optimization_barrier(v.astype(jnp.bfloat16)).astype(jnp.float32)

@jax.custom_vjp
def low_back(v):
    return v

def low_keep(v):
    return (low(v), None)

def low_pass(kept, grad):
    return (grad,)

def back_keep(v):
    return (v, None)

def back_low(kept, grad):
    return (low(grad),)
low.defvjp(low_keep, low_pass)
low_back.defvjp(back_keep, back_low)
epsilon = 1e-06
soft_cap = 50.0
masked_value = -1e+30
highest = lax.Precision.HIGHEST

def norm_rows(values, gain_row):
    return values * lax.rsqrt(lax.optimization_barrier(jnp.mean(values * values, axis=-1, keepdims=True)) + epsilon) * gain_row

def rotate(values, cosine, sine_table):
    half_size = values.shape[-1] // 2
    first_half = values[..., :half_size]
    second_half = values[..., half_size:]
    return jnp.concatenate([first_half * cosine - second_half * sine_table, second_half * cosine + first_half * sine_table], axis=-1)

def rotary_tables(length, head_size):
    position = jnp.arange(length).astype(jnp.float32)
    inverse = 10000.0 ** (-2.0 * jnp.arange(head_size // 2).astype(jnp.float32) / head_size)
    angles = position[:, None] * inverse[None, :]
    return (jnp.cos(angles), jnp.sin(angles))

def sliced(code_table, bit_count):
    step_size = 2.0 ** (8 - bit_count)
    return jnp.floor(code_table / step_size) * step_size + step_size / 2.0

def unit_scale(fan_in):
    return 1.0 / (128.0 * math.sqrt(fan_in))

def matmul(left, right):
    return jnp.dot(left, right, precision=highest)

def window_attention(queries, key_rows, value_rows, segments):
    groups, length = segments.shape
    pad_keys = jnp.pad(key_rows, ((0, 0), (WINDOW, 0), (0, 0)))
    pad_values = jnp.pad(value_rows, ((0, 0), (WINDOW, 0), (0, 0)))
    pad_segments = jnp.pad(segments, ((0, 0), (WINDOW, 0)), constant_values=-1)
    distance = jnp.arange(WINDOW)[:, None] - (jnp.arange(2 * WINDOW)[None, :] - WINDOW)
    inside = (distance >= 0) & (distance < WINDOW)
    blocks = []
    for block_index in range(length // WINDOW):
        block_start = block_index * WINDOW
        block_queries = queries[:, block_start:block_start + WINDOW]
        block_keys = pad_keys[:, block_start:block_start + 2 * WINDOW]
        block_values = pad_values[:, block_start:block_start + 2 * WINDOW]
        query_segments = segments[:, block_start:block_start + WINDOW]
        key_segments = pad_segments[:, block_start:block_start + 2 * WINDOW]
        allowed = (inside[None] & (query_segments[:, :, None] == key_segments[:, None, :]))[:, None]
        scores = low_back(jnp.einsum('gqhd,gkd->ghqk', block_queries, block_keys, precision=highest) * HD ** (-0.5))
        capped = jnp.where(allowed, soft_cap * jnp.tanh(scores / soft_cap), masked_value)
        weights_soft = low(jax.nn.softmax(capped, axis=-1))
        blocks.append(jnp.einsum('ghqk,gkd->gqhd', weights_soft, block_values, precision=highest))
    return jnp.concatenate(blocks, axis=1)

def block(tokens_f, segments, keep_rows, weights, gain_table, cosine, sine_table):
    groups, length, model_width = tokens_f.shape
    normed = low(norm_rows(tokens_f, gain_table[:, 0]))
    results = []
    for width_index in range(3):
        w_query, w_keyval, w_out, w_gate, w_up, w_down = weights[width_index]
        queries = low_back(matmul(normed, w_query)).reshape(groups, length, HEADS, HD)
        queries = low(rotate(queries, cosine[:, None, :], sine_table[:, None, :]))
        keyval = low_back(matmul(normed, w_keyval))
        key_rows = low(rotate(keyval[..., :HD], cosine, sine_table))
        value_rows = low(keyval[..., HD:])
        mixed = window_attention(queries, key_rows, value_rows, segments)
        mixed = low(low_back(mixed)).reshape(groups, length, HEADS * HD)
        attended = low_back(matmul(mixed, w_out))
        middle = tokens_f + norm_rows(attended, gain_table[:, 1])
        normed_two = low(norm_rows(middle, gain_table[:, 2]))
        gate_rows = low_back(matmul(normed_two, w_gate))
        up_rows = low_back(matmul(normed_two, w_up))
        hidden = low(jax.nn.gelu(gate_rows, approximate=True) * up_rows)
        branch = low_back(matmul(hidden, w_down))
        result = middle + norm_rows(branch, gain_table[:, 3])
        results.append(jnp.where(keep_rows[:, width_index][:, None, None] > 0, result, 0.0))
    return jnp.stack(results)

def reference(tokens, cotangent, segment_ids, width_mask, q_codes, kv_codes, o_codes, gate_codes, up_codes, down_codes, q_scale, kv_scale, o_scale, gate_scale, up_scale, down_scale, norm_gains):
    fan_list = [D, D, HEADS * HD, D, D, FF]
    code_list = [code_table.astype(jnp.float32) for code_table in (q_codes, kv_codes, o_codes, gate_codes, up_codes, down_codes)]
    scale_list = [q_scale, kv_scale, o_scale, gate_scale, up_scale, down_scale]
    offsets = [[sliced(code_table, bit_count) - code_table for code_table in code_list] for bit_count in (8, 4, 2)]
    cosine, sine_table = rotary_tables(LEN, HD)
    group_size = math.gcd(SEQS, max(1, 4096 // LEN))
    block_count = SEQS // group_size
    segment_blocks = segment_ids.reshape(block_count, group_size, LEN)
    keep_blocks = width_mask.reshape(block_count, group_size, 3)

    def forward(tokens_f, codes_f, scales_f, gain_table):
        weights = []
        for width_index in range(3):
            weights.append([low(scales_f[matrix_index][None, :] * (codes_f[matrix_index] + offsets[width_index][matrix_index]) * unit_scale(fan_list[matrix_index])) for matrix_index in range(6)])
        token_blocks = tokens_f.reshape(block_count, group_size, LEN, D)

        def step_block(carried, pieces):
            return (carried, block(pieces[0], pieces[1], pieces[2], weights, gain_table, cosine, sine_table))
        unused, stacked = lax.scan(jax.checkpoint(step_block), jnp.zeros((), jnp.float32), (token_blocks, segment_blocks, keep_blocks))
        return jnp.transpose(stacked, (1, 0, 2, 3, 4)).reshape(3, TOKENS, D)
    results, pullback = jax.vjp(forward, tokens.astype(jnp.float32), code_list, scale_list, norm_gains)
    grad_tokens, grad_codes, grad_scales, grad_gains = pullback(cotangent.astype(jnp.float32))
    return (results, grad_tokens, grad_codes[0], grad_codes[1], grad_codes[2], grad_codes[3], grad_codes[4], grad_codes[5], grad_scales[0], grad_scales[1], grad_scales[2], grad_scales[3], grad_scales[4], grad_scales[5], grad_gains)
```

```python
import functools
import itertools
import math

import jax
import jax.numpy as jnp
import numpy as np
from jax import lax
from jax.experimental import pallas as pl
from jax.experimental.pallas import tpu as pltpu
from jax.sharding import Mesh
from jax.sharding import PartitionSpec as P

AX = ("zl", "c", "zh", "y", "x")
F32 = jnp.float32
BF = jnp.bfloat16
EPS = 1e-6
D, HEADS, HD, FF, WINDOW = 640, 4, 256, 2048, 512
TOK = 256
WIN = 768
ORDER = (("x", "y", "z"), ("y", "z", "x"))
NA = 64
NB = 288
N = NA + NB
INT_A, INT_B = 64, 160
RA, RB = 16 * NA, 16 * NB
DOWN_ROW, O_ROW = 2560, 3840
NP = 9472
SEG = dict(q=(0, 1024, 8, 0), kv=(1024, 512, 4, 8), o=(1536, 640, 5, 12), gate=(2176, 2048, 16, 17),
           up=(4224, 2048, 16, 33), down=(6272, 640, 5, 49))
OQ, OKV, OO, OG, OU, OD, ON = 0, 1024, 1536, 2176, 4224, 6272, 6912
U_D = 1.0 / (128.0 * math.sqrt(D))
U_O = 1.0 / (128.0 * math.sqrt(HEADS * HD))
U_F = 1.0 / (128.0 * math.sqrt(FF))
VMEM = pl.BlockSpec(memory_space=pltpu.VMEM)
SMEM = pl.BlockSpec(memory_space=pltpu.SMEM)


def lane_tables():
    lane, dev = np.zeros((1, NP), np.int32), np.zeros((1, NP), np.int32)
    for at, size, each, first in SEG.values():
        c = np.arange(size)
        lane[0, at : at + size] = first + c % each
        dev[0, at : at + size] = c // each
    for g in range(4):
        c = np.arange(D)
        at = ON + g * D
        lane[0, at : at + D] = 54 + (c % 5) * 4 + g
        dev[0, at : at + D] = c // 5
    return lane, dev


def cost_of(us):
    return pl.CostEstimate(flops=int(us * 1e6) + 1000, bytes_accessed=1000, transcendentals=0)


def call(kernel, out_shape, ins, scratch=(), mem=62, us=1, in_specs=None, name=None):
    params = dict(vmem_limit_bytes=mem << 20)
    return pl.pallas_call(
        kernel,
        out_shape=out_shape,
        in_specs=in_specs or [VMEM] * len(ins),
        out_specs=jax.tree.map(lambda s: VMEM, out_shape),
        scratch_shapes=list(scratch),
        compiler_params=pltpu.CompilerParams(**params),
        cost_estimate=cost_of(us),
        name=name,
    )(*ins)


def sds(shape, dtype):
    return jax.ShapeDtypeStruct(shape, dtype)


def dot(a, b):
    return jnp.dot(a, b, preferred_element_type=F32)


def dot_t(a, b):
    return lax.dot_general(a, b, (((1,), (1,)), ((), ())), preferred_element_type=F32)


def t_dot(a, b):
    return lax.dot_general(a, b, (((0,), (0,)), ((), ())), preferred_element_type=F32)


def flat(c, x, y, z):
    return ((((z & 1) * 2 + c) * 2 + (z >> 1)) * 4 + y) * 4 + x


@functools.lru_cache(None)
def stage_pairs(stage, r):
    pairs = []
    for c, x, y, z in itertools.product(range(2), range(4), range(4), range(4)):
        at = dict(x=x, y=y, z=z)
        axis = ORDER[c][stage]
        at[axis] = (at[axis] + r) % 4
        pairs.append((flat(c, x, y, z), flat(c, **at)))
    return tuple(sorted(pairs))


def send(a, stage, r):
    return lax.ppermute(a, AX, stage_pairs(stage, r % 4))


def behind(k):
    return [(i, i + k) for i in range(16) if i % 8 + k < 8]


def other_core(a):
    return lax.ppermute(a, "c", [(0, 1), (1, 0)])


def swap_matrix():
    row = lax.broadcasted_iota(jnp.int32, (256, 256), 0)
    col = lax.broadcasted_iota(jnp.int32, (256, 256), 1)
    return ((row % 16) * 16 + row // 16 == col).astype(BF)


BLOCKS = ((224, 80, DOWN_ROW), (304, 48, O_ROW))


def asm_kernel(*refs):
    ins, out_a, out_b = refs[:4], refs[4], refs[5]
    swap = swap_matrix()
    for g in range((INT_A + INT_B) // 16):
        x = jnp.concatenate(
            [ins[s // 4][(s % 4) * N + 16 * g : (s % 4) * N + 16 * g + 16, :] for s in range(16)], axis=0
        )
        y = dot(swap, x).astype(BF)
        if g < 4:
            out_a[256 * g : 256 * g + 256, :] = y
        else:
            out_b[256 * (g - 4) : 256 * (g - 4) + 256, :] = y
    for first, lines, row in BLOCKS:
        for s in range(16):
            at = (s % 4) * N + first
            out_b[row + s * lines : row + (s + 1) * lines, :] = ins[s // 4][at : at + lines, :]


def join_kernel(a, b, c, d, out):
    for r, ref in enumerate((a, b, c, d)):
        out[r * RA : (r + 1) * RA, :] = ref[...]


def gather(shard, tokens, early):
    one = jnp.concatenate([shard] + [send(shard, 0, r) for r in (1, 2, 3)], axis=0)
    t1, t0 = (lax.ppermute(tokens, ("y", "x"), behind(k)) for k in (1, 2))
    two = [one] + [send(one, 1, r) for r in (1, 2, 3)]
    two[0], t0, t1, *early = lax.optimization_barrier((two[0], t0, t1, *early))
    piece_a, piece_b = call(asm_kernel, [sds((RA, 128), BF), sds((RB, 128), BF)], two, name="asm", us=0)
    mine_a = [piece_a] + [send(piece_a, 2, r) for r in (1, 2, 3)]
    mine_a = call(join_kernel, sds((4 * RA, 128), BF), mine_a, name="join", us=0)
    theirs_a = other_core(mine_a)
    mine_b = [piece_b] + [send(piece_b, 2, r) for r in (1, 2, 3)]
    return mine_a, theirs_a, mine_b, other_core(piece_b), t0, t1, early


def rs1_kernel(a, b, *outs):
    for r in range(4):
        outs[r][...] = (a[r].astype(F32) + b[r].astype(F32)).astype(BF)


def total4(refs, at, rows):
    t = refs[0][at : at + rows, :].astype(F32)
    for k in (1, 2, 3):
        t = t + refs[k][at : at + rows, :].astype(F32)
    return t


def rs2_kernel(*refs):
    a, b, outs = refs[:4], refs[4:8], refs[8:]
    swap = swap_matrix()
    for g in range((INT_A + INT_B) // 16):
        t = total4(a, 256 * g, 256) if g < 4 else total4(b, 256 * (g - 4), 256)
        y = dot(swap, t.astype(BF)).astype(BF)
        for s in range(16):
            at = (s % 4) * N + 16 * g
            outs[s // 4][at : at + 16, :] = y[16 * s : 16 * s + 16]
    for first, lines, row in BLOCKS:
        for s in range(16):
            at = (s % 4) * N + first
            outs[s // 4][at : at + lines, :] = total4(b, row + s * lines, lines).astype(BF)


def rs3_kernel(*refs):
    ins, outs = refs[:4], refs[4:]
    for r in range(4):
        outs[r][...] = total4(ins, r * N, N).astype(BF)


def rs4_kernel(a0, a1, a2, a3, q, kv, gate, up, down, o, *small):
    t = total4((a0, a1, a2, a3), 0, N)
    for cb in range(8):
        q[:, cb * 128 : cb * 128 + 128] = t[cb * 5 : cb * 5 + 5]
    for cb in range(4):
        kv[:, cb * 128 : cb * 128 + 128] = t[40 + cb * 5 : 45 + cb * 5]
    at = 0
    for ref in small[:6]:
        ref[...] = t[60, at : at + ref.shape[0]]
        at += ref.shape[0]
    for j in range(5):
        small[6][j : j + 1, :] = t[60:61, at + 4 * j : at + 4 * j + 4]
    for cb in range(16):
        gate[:, cb * 128 : cb * 128 + 128] = t[64 + cb * 5 : 69 + cb * 5]
        up[:, cb * 128 : cb * 128 + 128] = t[144 + cb * 5 : 149 + cb * 5]
    for cb in range(5):
        down[:, cb * 128 : cb * 128 + 128] = t[224 + cb * 16 : 240 + cb * 16]
        o[:, cb * 128 : cb * 128 + 128] = t[304 + cb * 8 : 312 + cb * 8]


def first_hop(mine, got, rows, grid, us):
    block = rows // grid
    parts = pl.pallas_call(
        rs1_kernel,
        grid=(grid,),
        out_shape=[sds((rows, 128), BF)] * 4,
        in_specs=[pl.BlockSpec((4, block, 128), lambda i: (0, i, 0))] * 2,
        out_specs=[pl.BlockSpec((block, 128), lambda i: (i, 0))] * 4,
        compiler_params=pltpu.CompilerParams(vmem_limit_bytes=24 << 20),
        cost_estimate=cost_of(us),
        name=f"rs1_{rows}",
    )(mine.reshape(4, rows, 128), got.reshape(4, rows, 128))
    return [parts[0]] + [send(parts[r], 2, -r) for r in (1, 2, 3)]


def scatter(a, b, out_shape):
    parts = call(rs2_kernel, [sds((4 * N, 128), BF)] * 4, a + b, name="rs2", mem=24, us=0)
    parts = [parts[0]] + [send(parts[r], 1, -r) for r in (1, 2, 3)]
    parts = call(rs3_kernel, [sds((N, 128), BF)] * 4, parts, name="rs3", mem=24, us=0)
    parts = [parts[0]] + [send(parts[r], 0, -r) for r in (1, 2, 3)]
    return call(rs4_kernel, out_shape, parts, name="rs4", mem=24, us=0)


def pack_kernel(q, kv, o, gate, up, down, sq, skv, so, sg, su, sd, gains, out, wide):
    for cb in range(8):
        wide[cb * 5 : cb * 5 + 5, :] = q[:, cb * 128 : cb * 128 + 128].astype(F32)
    for cb in range(4):
        wide[40 + cb * 5 : 45 + cb * 5, :] = kv[:, cb * 128 : cb * 128 + 128].astype(F32)
    row = [ref[...].reshape(1, -1) for ref in (sq, skv, so, sg, su, sd)] + [gains[j : j + 1, :] for j in range(5)]
    v = jnp.concatenate(row + [jnp.zeros((1, 54), F32)], axis=1)
    hi = v.astype(BF).astype(F32)
    mid = (v - hi).astype(BF).astype(F32)
    wide[60:61, :] = hi
    wide[61:62, :] = mid
    wide[62:63, :] = v - hi - mid
    wide[63:64, :] = jnp.zeros((1, 128), F32)
    for cb in range(16):
        wide[64 + cb * 5 : 69 + cb * 5, :] = gate[:, cb * 128 : cb * 128 + 128].astype(F32)
        wide[144 + cb * 5 : 149 + cb * 5, :] = up[:, cb * 128 : cb * 128 + 128].astype(F32)
    for cb in range(5):
        wide[224 + cb * 16 : 240 + cb * 16, :] = down[:, cb * 128 : cb * 128 + 128].astype(F32)
        wide[304 + cb * 8 : 312 + cb * 8, :] = o[:, cb * 128 : cb * 128 + 128].astype(F32)
    wide[344:352, :] = jnp.zeros((8, 128), F32)
    out[...] = wide[...].astype(BF)


def piece(mine, theirs, p, rows):
    return (mine if p < 4 else theirs), (p % 4) * rows


def perm_matrix(dk):
    return (lax.broadcasted_iota(jnp.int32, (D, D), 0) == dk).astype(BF)


def steps_of(b):
    step = jnp.where(b == 0, 1.0, jnp.where(b == 1, 16.0, 64.0)).astype(F32)
    inv = jnp.where(b == 0, 1.0, jnp.where(b == 1, 1.0 / 16, 1.0 / 64)).astype(F32)
    return step, inv


def level_maker(b, rows=16, dtype=BF):
    step, inv = steps_of(b)
    step_v = jnp.full((rows, 128), step, F32)
    inv_v = jnp.full((rows, 128), inv, F32).astype(dtype)
    half_v = (step_v * 0.5).astype(dtype)
    step_v = step_v.astype(dtype)
    return lambda c: jnp.floor(c * inv_v) * step_v + half_v


def dequant_a(b, mine, theirs, lq, lkv):
    level = level_maker(b)
    for p in range(8):
        ref, base = piece(mine, theirs, p, RA)
        for j in range(5):
            for cb in range(8):
                at = base + (cb * 5 + j) * 16
                lq[j * 128 + p * 16 : j * 128 + p * 16 + 16, cb * 128 : cb * 128 + 128] = level(ref[at : at + 16, :])
            for cb in range(4):
                at = base + (40 + cb * 5 + j) * 16
                lkv[j * 128 + p * 16 : j * 128 + p * 16 + 16, cb * 128 : cb * 128 + 128] = level(ref[at : at + 16, :])


def make_mask(segq, segk, mask):
    for t in range(2):
        r = lax.broadcasted_iota(jnp.int32, (128, 640), 0)
        c = lax.broadcasted_iota(jnp.int32, (128, 640), 1)
        ok = (c <= WINDOW + r) & (c > r)
        ok = ok & (segq[t * 128 : t * 128 + 128, :] == segk[:, t * 128 : t * 128 + 640])
        mask[t] = ok.astype(F32)


def rope(v, cos, sin):
    a, b = v[:, :128], v[:, 128:]
    return jnp.concatenate([a * cos - b * sin, b * cos + a * sin], axis=1)


def unrope(v, cos, sin):
    a, b = v[:, :128], v[:, 128:]
    return jnp.concatenate([a * cos + b * sin, b * cos - a * sin], axis=1)


TANH_IN = 1.0 / (16.0 * 50.0)
EXP2_IN = 50.0 * math.log2(math.e)


def first_kernel(
    run, mine, theirs, dev_col, lane_of, dev_of, t0, t1, t2, dk, cos, sin, segq, segk,
    par, h1p, q_out, kv_out, mix_out, lq, lkv, mask, sc, ex, tot,
):
    lines = []
    for l in (60, 61, 62):
        refs = [piece(mine, theirs, p, RA) for p in range(8)]
        lines.append(jnp.concatenate([ref[at + l * 16 : at + l * 16 + 16, :] for ref, at in refs], axis=0))
    lines = jnp.concatenate(lines, axis=1)
    devs = dev_col[...]
    row = lax.broadcasted_iota(jnp.int32, (128, 256), 0)
    for i in range(NP // 256):
        cols = slice(i * 256, i * 256 + 256)
        one_hot = (row == lane_of[:, cols]).astype(BF)
        t = dot(lines, jnp.concatenate([one_hot] * 3, axis=0))
        t = jnp.where(devs == dev_of[:, cols], t, 0.0)
        par[:, cols] = jnp.sum(t, axis=0, keepdims=True)
    perm = perm_matrix(dk[...])
    gain = par[:, ON : ON + D]
    for k, t in enumerate((t0, t1, t2)):
        v = t[...].astype(F32)
        h = v * lax.rsqrt(jnp.mean(v * v, axis=-1, keepdims=True) + EPS) * gain
        h1p[k * 256 : k * 256 + 256, :] = dot(h.astype(BF), perm).astype(BF)
    make_mask(segq, segk, mask)

    def width(b, carry):
        @pl.when(run[b] == 0)
        def _():
            mix_out[b] = jnp.zeros((TOK, HEADS * HD), BF)

        @pl.when(run[b] > 0)
        def _():
            dequant_a(b, mine, theirs, lq, lkv)
            own = h1p[512:768, :]
            co, so = cos[512:768, :], sin[512:768, :]
            for h in range(4):
                scale = par[:, OQ + h * 256 : OQ + h * 256 + 256] * U_D
                q = rope(dot(own, lq[:, h * 256 : h * 256 + 256]) * scale, co, so).astype(BF)
                for t in range(2):
                    q_out[b, t, h * 128 : h * 128 + 128, :] = q[t * 128 : t * 128 + 128]
            for k in range(3):
                rows = h1p[k * 256 : k * 256 + 256, :]
                cw, sw = cos[k * 256 : k * 256 + 256, :], sin[k * 256 : k * 256 + 256, :]
                key = dot(rows, lkv[:, :256]) * (par[:, OKV : OKV + 256] * U_D)
                kv_out[b, k * 256 : k * 256 + 256, 0:256] = rope(key, cw, sw).astype(BF)
                val = dot(rows, lkv[:, 256:]) * (par[:, OKV + 256 : OKV + 512] * U_D)
                kv_out[b, k * 256 : k * 256 + 256, 256:512] = val.astype(BF)
            for t in range(2):
                keys = kv_out[b, t * 128 : t * 128 + 640, 0:256]
                vals = kv_out[b, t * 128 : t * 128 + 640, 256:512]
                sc[...] = dot_t(q_out[b, t], keys)

                def soft(i, carry):
                    at = pl.multiple_of(i * 32, 32)
                    m = mask[t, pl.ds(pl.multiple_of((i % 4) * 32, 32), 32), :]
                    e = jnp.exp2(jnp.tanh(sc[pl.ds(at, 32), :] * TANH_IN) * EXP2_IN) * m
                    tot[pl.ds(at, 32), :] = jnp.broadcast_to(1.0 / jnp.sum(e, axis=1, keepdims=True), (32, 128))
                    ex[pl.ds(at, 32), :] = e.astype(BF)
                    return carry

                lax.fori_loop(0, 16, soft, 0, unroll=4)
                mixed = dot(ex[...], vals) * tot[:, 0:1]
                for h in range(4):
                    mix_out[b, t * 128 : t * 128 + 128, h * 256 : h * 256 + 256] = mixed[h * 128 : h * 128 + 128].astype(BF)

        return carry

    lax.fori_loop(0, 3, width, 0)


def mean_of(v):
    return jnp.mean(v, axis=-1, keepdims=True)


C_G = math.sqrt(2.0 / math.pi)
C_3 = C_G * 0.044715
PARTS = ((O_ROW, 768), (0, 2560), (DOWN_ROW, 1280))


def middle_kernel(
    run, inat, mix, tok, cot, b0, b1, b2, b3, b4, b5, b6, b7, par, dk,
    out, rest, gmix, g_mine, g_theirs, gpar,
    pcs, lgu, ld, lo, onat, gu32, gate, up, aa, bb, hid, gg, gu, h2s, gbr, gat, att, mid, acc, perm, outv,
    in_sem, gu_sem, do_sem, out_sem,
):
    dwd, dwo = ld, onat
    loads = [
        [
            pltpu.make_async_copy(ref.at[pl.ds(first, rows)], pcs.at[p, pl.ds(first, rows)], in_sem.at[k, p])
            for p, ref in enumerate((b0, b1, b2, b3, b4, b5, b6, b7))
        ]
        for k, (first, rows) in enumerate(PARTS)
    ]
    for group in loads:
        for copy in group:
            copy.start()
    perm[...] = perm_matrix(dk[...])
    rest[...] = jnp.zeros_like(rest)
    gpar[...] = jnp.zeros_like(gpar)
    for copy in loads[0]:
        copy.wait()
    for p in range(8):
        for s in range(16):
            at = O_ROW + s * 48
            block = pcs[p, at : at + 48, :].astype(F32)
            row = pl.multiple_of(inat[p * 16 + s] * 8, 8)
            for cb in range(5):
                onat[pl.ds(row, 8), cb * 128 : cb * 128 + 128] = block[cb * 8 : cb * 8 + 8]
    for copy in loads[1] + loads[2]:
        copy.wait()

    def width(b, carry):
        rows = pl.ds(pl.multiple_of(b * TOK, TOK), TOK)

        @pl.when(run[b] == 0)
        def _():
            outv[b] = jnp.zeros((TOK, D), F32)
            hid[rows, :] = jnp.zeros((TOK, FF), BF)
            gg[rows, :] = jnp.zeros((TOK, FF), BF)
            gu[rows, :] = jnp.zeros((TOK, FF), BF)
            h2s[rows, :] = jnp.zeros((TOK, D), BF)
            gbr[rows, :] = jnp.zeros((TOK, D), BF)
            gat[rows, :] = jnp.zeros((TOK, D), BF)

        @pl.when(run[b] > 0)
        def _():
            level = level_maker(b)
            wide = level_maker(b, 8, F32)
            for r in range(64):
                for cb in range(5):
                    two = [wide(onat[r * 16 + k * 8 : r * 16 + k * 8 + 8, cb * 128 : cb * 128 + 128]) for k in (0, 1)]
                    lo[r * 16 : r * 16 + 16, cb * 128 : cb * 128 + 128] = jnp.concatenate(two, axis=0).astype(BF)
            s_o = par[:, OO : OO + D] * U_O
            s_d = par[:, OD : OD + D] * U_F
            g1, g2, g3 = (par[:, ON + k * D : ON + (k + 1) * D] for k in (1, 2, 3))
            attended = dot(mix[b], lo[...]) * s_o
            att[...] = attended
            r1 = lax.rsqrt(mean_of(attended * attended) + EPS)
            middle = tok[...].astype(F32) + attended * r1 * g1
            mid[...] = middle
            r2 = lax.rsqrt(mean_of(middle * middle) + EPS)
            h2 = (middle * r2 * g2).astype(BF)
            h2p = dot(h2, perm[...]).astype(BF)
            h2s[rows, :] = h2p

            def gate_up(f):
                for half in range(2):
                    cb = f * 2 + half
                    for first, to in ((0, f * 512), (80, f * 512 + 256)):
                        for j in range(5):
                            for p in range(8):
                                at = (first + cb * 5 + j) * 16
                                k = j * 128 + p * 16
                                col = to + half * 128
                                lgu[k : k + 16, col : col + 128] = level(pcs[p, at : at + 16, :])
                gu32[f % 2] = dot(h2p, lgu[:, f * 512 : f * 512 + 512])

            gate_up(0)
            for p in range(8):
                for s in range(16):
                    row = pl.multiple_of(inat[p * 16 + s] * 16, 16)
                    for cb in range(5):
                        at = DOWN_ROW + s * 80 + cb * 16
                        ld[pl.ds(row, 16), cb * 128 : cb * 128 + 128] = level(pcs[p, at : at + 16, :])
            for f in range(8):
                if f < 7:
                    gate_up(f + 1)
                cols = slice(f * 256, f * 256 + 256)
                s_g, s_u = par[:, OG + f * 256 : OG + f * 256 + 256] * U_D, par[:, OU + f * 256 : OU + f * 256 + 256] * U_D
                parts = []
                for rc in range(8):
                    rr = slice(rc * 32, rc * 32 + 32)
                    x = gu32[f % 2, rr, 0:256] * s_g
                    u = gu32[f % 2, rr, 256:512] * s_u
                    gate[rr, cols] = x.astype(BF)
                    up[rr, cols] = u.astype(BF)
                    x2 = x * x
                    hf = 0.5 * jnp.tanh(x * (C_G + C_3 * x2)) + 0.5
                    gl = x * hf
                    aa[rr, cols] = u * (hf + (gl - gl * hf) * (2 * C_G + (6 * C_3) * x2))
                    bb[rr, cols] = gl
                    parts.append((gl * u).astype(BF))
                h = jnp.concatenate(parts, axis=0)
                hid[rows, cols] = h
                add = dot(h, ld[cols, :])
                acc[...] = add if f == 0 else acc[...] + add
            branch = acc[...] * s_d
            r3 = lax.rsqrt(mean_of(branch * branch) + EPS)
            outv[b] = mid[...] + branch * r3 * g3
            gy = cot[b].astype(F32)
            gpar[:, ON + 3 * D : ON + 4 * D] += jnp.sum(gy * branch * r3, axis=0, keepdims=True)
            w = g3 * gy
            gb = r3 * w - branch * (r3 * r3 * r3 * mean_of(w * branch))
            gpar[:, OD : OD + D] += jnp.sum(gb * branch, axis=0, keepdims=True)
            gb = (gb * s_d).astype(BF)
            gbr[rows, :] = gb

            def grad_hidden(f):
                gu32[f % 2, :, 0:256] = dot_t(gb, ld[f * 256 : f * 256 + 256, :])

            ones = jnp.ones((8, TOK), BF)
            grad_hidden(0)
            for f in range(8):
                if f < 7:
                    grad_hidden(f + 1)
                cols = slice(f * 256, f * 256 + 256)
                col_g, col_u = slice(OG + f * 256, OG + f * 256 + 256), slice(OU + f * 256, OU + f * 256 + 256)
                s_g, s_u = par[:, col_g] * U_D, par[:, col_u] * U_D
                parts, prods = [], []
                for rc in range(8):
                    rr = slice(rc * 32, rc * 32 + 32)
                    g = gu32[f % 2, rr, 0:256]
                    gg_b = (g * aa[rr, cols] * s_g).astype(BF)
                    gu_b = (g * bb[rr, cols] * s_u).astype(BF)
                    parts.append(jnp.concatenate([gg_b, gu_b], axis=1))
                    prods.append(jnp.concatenate([gg_b * gate[rr, cols], gu_b * up[rr, cols]], axis=1))
                both = jnp.concatenate(parts, axis=0)
                gg[rows, cols] = both[:, 0:256]
                gu[rows, cols] = both[:, 256:512]
                sums = dot(ones, jnp.concatenate(prods, axis=0))
                gpar[:, col_g] += sums[0:1, 0:256]
                gpar[:, col_u] += sums[0:1, 256:512]
                add = dot_t(both, lgu[:, f * 512 : f * 512 + 512])
                acc[...] = add if f == 0 else acc[...] + add
            g_h2 = acc[...]
            high = g_h2.astype(BF)
            low = (g_h2 - high.astype(F32)).astype(BF)
            g_h2 = dot_t(high, perm[...]) + dot_t(low, perm[...])
            middle = mid[...]
            attended = att[...]
            gpar[:, ON + 2 * D : ON + 3 * D] += jnp.sum(g_h2 * middle * r2, axis=0, keepdims=True)
            w = g2 * g_h2
            gmid = cot[b].astype(F32) + r2 * w - middle * (r2 * r2 * r2 * mean_of(w * middle))
            rest[...] += gmid
            gpar[:, ON + D : ON + 2 * D] += jnp.sum(gmid * attended * r1, axis=0, keepdims=True)
            w = g1 * gmid
            ga = r1 * w - attended * (r1 * r1 * r1 * mean_of(w * attended))
            gpar[:, OO : OO + D] += jnp.sum(ga * attended, axis=0, keepdims=True)
            ga = (ga * s_o).astype(BF)
            gat[rows, :] = ga
            gmix[b] = dot_t(ga, lo[...]).astype(BF)

        return carry

    lax.fori_loop(0, 3, width, 0)
    out_copy = pltpu.make_async_copy(outv, out, out_sem)
    out_copy.start()
    gpar[:, OO : OO + D] = gpar[:, OO : OO + D] / par[:, OO : OO + D]
    for at in (OG, OU):
        scale = par[:, at : at + FF]
        gpar[:, at : at + FF] = gpar[:, at : at + FF] / (scale * scale * U_D)
    gpar[:, OD : OD + D] = gpar[:, OD : OD + D] / par[:, OD : OD + D]

    stores = []

    def leave(p, first, rows, sem):
        to, base = piece(g_mine, g_theirs, p, RB)
        copy = pltpu.make_async_copy(pcs.at[p, pl.ds(first, rows)], to.at[pl.ds(base + first, rows)], sem)
        copy.start()
        stores.append(copy)

    g_all = gbr[...]
    for f in range(8):
        cols = slice(f * 256, f * 256 + 256)
        dwd[cols, :] = t_dot(hid[:, cols], g_all).astype(BF)
    for p in range(8):
        for s in range(16):
            row = pl.multiple_of(inat[p * 16 + s] * 16, 16)
            for cb in range(5):
                at = DOWN_ROW + s * 80 + cb * 16
                pcs[p, at : at + 16, :] = dwd[pl.ds(row, 16), cb * 128 : cb * 128 + 128]
        leave(p, DOWN_ROW, 1280, do_sem.at[0, p])
    for h in range(4):
        w = jnp.zeros((256, D), F32)
        for b in range(3):
            w = w + t_dot(mix[b, :, h * 256 : h * 256 + 256], gat[b * TOK : (b + 1) * TOK, :])
        dwo[h * 256 : h * 256 + 256, :] = w
    for p in range(8):
        for s in range(16):
            row = pl.multiple_of(inat[p * 16 + s] * 8, 8)
            parts = [dwo[pl.ds(row, 8), cb * 128 : cb * 128 + 128] for cb in range(5)] + [jnp.zeros((8, 128), F32)]
            at = O_ROW + s * 48
            pcs[p, at : at + 48, :] = jnp.concatenate(parts, axis=0).astype(BF)
        leave(p, O_ROW, 768, do_sem.at[1, p])
    h2t = h2s[...]
    for f in range(8):
        cols = slice(f * 256, f * 256 + 256)
        for k, (first, ref) in enumerate(((0, gg), (80, gu))):
            w = t_dot(h2t, ref[:, cols]).astype(BF)
            for half in range(2):
                for j in range(5):
                    for p in range(8):
                        at = (first + (f * 2 + half) * 5 + j) * 16
                        r = j * 128 + p * 16
                        pcs[p, at : at + 16, :] = w[r : r + 16, half * 128 : half * 128 + 128]
            if f % 2:
                for p in range(8):
                    leave(p, (first + (f - 1) * 10) * 16, 320, gu_sem.at[f // 2, k, p])
    for copy in stores:
        copy.wait()
    out_copy.wait()


def attn_back_kernel(
    first, count, run, par, cos, sin, segq, segk, q, kv, gmix, gpar2,
    gqb, gkvb, gpar,
    mask, sc, gp, pb, gz, gq, gkv,
):
    make_mask(segq, segk, mask)
    gpar[...] = gpar2[...]

    def width(k, carry):
        b = first + k
        @pl.when(run[b] > 0)
        def _():
            gkv[...] = jnp.zeros_like(gkv)
            for t in range(2):
                win = slice(t * 128, t * 128 + 640)
                keys = kv[b, win, 0:256]
                vals = kv[b, win, 256:512]
                gm = jnp.concatenate(
                    [gmix[b, t * 128 : t * 128 + 128, h * 256 : h * 256 + 256] for h in range(4)], axis=0
                )
                sc[...] = dot_t(q[b, t], keys)
                gp[...] = dot_t(gm, vals)

                def soft(i, carry):
                    at = pl.multiple_of(i * 16, 16)
                    m = mask[t, pl.ds(pl.multiple_of((i % 8) * 16, 16), 16), :]
                    th = jnp.tanh(sc[pl.ds(at, 16), :] * TANH_IN)
                    e = jnp.exp2(th * EXP2_IN) * m
                    p = e * (1.0 / jnp.sum(e, axis=1, keepdims=True))
                    pb[pl.ds(at, 16), :] = p.astype(BF)
                    pg = p * gp[pl.ds(at, 16), :]
                    dd = jnp.sum(pg, axis=1, keepdims=True)
                    gz[pl.ds(at, 16), :] = ((pg - p * dd) * (1.0 - th * th)).astype(BF)
                    return carry

                lax.fori_loop(0, 32, soft, 0, unroll=4)
                gkv[win, 256:512] += t_dot(pb[...], gm)
                gkv[win, 0:256] += t_dot(gz[...], q[b, t]) * (1.0 / 16)
                gq[t] = dot(gz[...], keys) * (1.0 / 16)
            co, so = cos[512:768, :], sin[512:768, :]
            for h in range(4):
                cols = slice(h * 256, h * 256 + 256)
                g = unrope(jnp.concatenate([gq[t, h * 128 : h * 128 + 128, :] for t in (0, 1)], axis=0), co, so)
                raw = jnp.concatenate([q[b, t, h * 128 : h * 128 + 128, :] for t in (0, 1)], axis=0)
                raw = unrope(raw.astype(F32), co, so)
                gpar[:, OQ + h * 256 : OQ + h * 256 + 256] += jnp.sum(g * raw, axis=0, keepdims=True)
                g = g * (par[:, OQ + h * 256 : OQ + h * 256 + 256] * U_D)
                gqb[k, :, cols] = g.astype(BF)
            for w in range(3):
                rows = slice(w * 256, w * 256 + 256)
                cw, sw = cos[rows, :], sin[rows, :]
                for half in range(2):
                    cols = slice(half * 256, half * 256 + 256)
                    g = gkv[rows, cols]
                    raw = kv[b, rows, cols].astype(F32)
                    if half == 0:
                        g, raw = unrope(g, cw, sw), unrope(raw, cw, sw)
                    at = OKV + half * 256
                    gpar[:, at : at + 256] += jnp.sum(g * raw, axis=0, keepdims=True)
                    g = g * (par[:, at : at + 256] * U_D)
                    gkvb[k, rows, cols] = g.astype(BF)

        return carry

    lax.fori_loop(0, count, width, 0)


def last_kernel(
    run, h1p, mine, theirs, gqb0, gkvb0, gqb1, gkvb1, par, gpar_in, dk, dev_col, lane_of, dev_of, t0, t1, t2,
    own, back1, back2, g_mine, g_theirs,
    lq, lkv, gh1, gpar, gq_sum, gkv_sum, gqs, gkvs,
):
    gh1[...] = jnp.zeros_like(gh1)
    gpar[...] = gpar_in[...]
    gpar[:, OQ : OQ + 1536] = gpar[:, OQ : OQ + 1536] / par[:, OQ : OQ + 1536]
    gq_sum[...] = jnp.zeros_like(gq_sum)
    gkv_sum[...] = jnp.zeros_like(gkv_sum)
    for b, (gqb, gkvb, at) in enumerate(((gqb0, gkvb0, 0), (gqb1, gkvb1, 0), (gqb1, gkvb1, 1))):

        @pl.when(run[b] > 0)
        def _(gqb=gqb, gkvb=gkvb, at=at):
            gq_sum[...] += gqb[at].astype(F32)
            gkv_sum[...] += gkvb[at].astype(F32)

    gqs[...] = gq_sum[...].astype(BF)
    gkvs[...] = gkv_sum[...].astype(BF)

    def put(w, first):
        for half in range(2):
            for j in range(5):
                for p in range(8):
                    to, base = piece(g_mine, g_theirs, p, RA)
                    at = base + (first + half * 5 + j) * 16
                    k = j * 128 + p * 16
                    to[at : at + 16, :] = w[k : k + 16, half * 128 : half * 128 + 128]

    for f in range(4):
        put(t_dot(h1p[512:768, :], gqs[:, f * 256 : f * 256 + 256]).astype(BF), f * 10)
    for f in range(2):
        put(t_dot(h1p[...], gkvs[:, f * 256 : f * 256 + 256]).astype(BF), 40 + f * 10)

    for b, (gqb, gkvb, at) in enumerate(((gqb0, gkvb0, 0), (gqb1, gkvb1, 0), (gqb1, gkvb1, 1))):

        @pl.when(run[b] > 0)
        def _(b=b, gqb=gqb, gkvb=gkvb, at=at):
            dequant_a(b, mine, theirs, lq, lkv)
            gh1[512:768, :] += dot_t(gqb[at], lq[...])
            for k in range(3):
                gh1[k * 256 : k * 256 + 256, :] += dot_t(gkvb[at, k * 256 : k * 256 + 256, :], lkv[...])

    perm = perm_matrix(dk[...])
    gain_sum = jnp.zeros((1, D), F32)
    for k, (t, to) in enumerate(((t0, back2), (t1, back1), (t2, own))):
        g = gh1[k * 256 : k * 256 + 256, :]
        high = g.astype(BF)
        low = (g - high.astype(F32)).astype(BF)
        g = dot_t(high, perm) + dot_t(low, perm)
        v = t[...].astype(F32)
        r = lax.rsqrt(mean_of(v * v) + EPS)
        gain_sum = gain_sum + jnp.sum(g * v * r, axis=0, keepdims=True)
        to[...] = g.astype(to.dtype)
    gpar[:, ON : ON + D] = gain_sum

    devs = dev_col[...]
    sums = jnp.zeros((128, 128), F32)
    row = lax.broadcasted_iota(jnp.int32, (128, 256), 0)
    for i in range(NP // 256):
        cols = slice(i * 256, i * 256 + 256)
        one_hot = (row == lane_of[:, cols]).astype(BF)
        sums = sums + dot_t(jnp.where(devs == dev_of[:, cols], gpar[:, cols], 0.0).astype(BF), one_hot)
    sums = sums.astype(BF)
    for p in range(8):
        to, base = piece(g_mine, g_theirs, p, RA)
        to[base + 960 : base + 976, :] = sums[p * 16 : p * 16 + 16]
        to[base + 976 : base + 1024, :] = jnp.zeros((48, 128), BF)


def end_kernel(own, got1, got2, tok, rest, par, out):
    g = own[...] + got1[...].astype(F32) + got2[...].astype(F32)
    v = tok[...].astype(F32)
    r = lax.rsqrt(mean_of(v * v) + EPS)
    w = par[:, ON : ON + D] * g
    out[...] = rest[...] + r * w - v * (r * r * r * mean_of(w * v))


def run_first(args):
    return call(
        first_kernel,
        [
            sds((1, NP), F32), sds((WIN, D), BF),
            sds((3, 2, 512, HD), BF), sds((3, WIN, 2 * HD), BF), sds((3, TOK, HEADS * HD), BF),
        ],
        args,
        scratch=[
            pltpu.VMEM((D, 1024), BF), pltpu.VMEM((D, 512), BF), pltpu.VMEM((2, 128, 640), F32),
            pltpu.VMEM((512, 640), F32), pltpu.VMEM((512, 640), BF), pltpu.VMEM((512, 128), F32),
        ],
        in_specs=[SMEM] + [VMEM] * 13, name="first", us=20,
    )


def run_middle(args):
    out_shape = [
        sds((3, TOK, D), F32), sds((TOK, D), F32), sds((3, TOK, HEADS * HD), BF),
        sds((4 * RB, 128), BF), sds((4 * RB, 128), BF), sds((1, NP), F32),
    ]
    any_ = pl.BlockSpec(memory_space=pl.ANY)
    return pl.pallas_call(
        middle_kernel,
        out_shape=out_shape,
        in_specs=[SMEM, SMEM] + [VMEM] * 3 + [any_] * 8 + [VMEM] * 2,
        out_specs=[any_, VMEM, VMEM, any_, any_, VMEM],
        scratch_shapes=[
            pltpu.VMEM((8, RB, 128), BF), pltpu.VMEM((D, 2 * FF), BF), pltpu.VMEM((FF, D), BF), pltpu.VMEM((1024, D), BF),
            pltpu.VMEM((1024, D), F32), pltpu.VMEM((2, TOK, 512), F32),
            pltpu.VMEM((TOK, FF), BF), pltpu.VMEM((TOK, FF), BF), pltpu.VMEM((TOK, FF), F32), pltpu.VMEM((TOK, FF), F32),
            pltpu.VMEM((3 * TOK, FF), BF), pltpu.VMEM((3 * TOK, FF), BF), pltpu.VMEM((3 * TOK, FF), BF),
            pltpu.VMEM((3 * TOK, D), BF), pltpu.VMEM((3 * TOK, D), BF), pltpu.VMEM((3 * TOK, D), BF),
            pltpu.VMEM((TOK, D), F32), pltpu.VMEM((TOK, D), F32), pltpu.VMEM((TOK, D), F32),
            pltpu.VMEM((D, D), BF), pltpu.VMEM((3, TOK, D), F32),
            pltpu.SemaphoreType.DMA((3, 8)), pltpu.SemaphoreType.DMA((4, 2, 8)), pltpu.SemaphoreType.DMA((2, 8)),
            pltpu.SemaphoreType.DMA,
        ],
        compiler_params=pltpu.CompilerParams(vmem_limit_bytes=62 << 20),
        cost_estimate=cost_of(70),
        name="middle",
    )(*args)


def run_attnb(first, count, args):
    return call(
        functools.partial(attn_back_kernel, first, count),
        [sds((count, TOK, 1024), BF), sds((count, WIN, 512), BF), sds((1, NP), F32)],
        args,
        scratch=[
            pltpu.VMEM((2, 128, 640), F32), pltpu.VMEM((512, 640), F32), pltpu.VMEM((512, 640), F32),
            pltpu.VMEM((512, 640), BF), pltpu.VMEM((512, 640), BF),
            pltpu.VMEM((2, 512, HD), F32), pltpu.VMEM((WIN, 512), F32),
        ],
        in_specs=[SMEM] + [VMEM] * 9, mem=28, name=f"attnb{first}", us=8 * count,
    )


def run_last(args):
    return call(
        last_kernel,
        [
            sds((TOK, D), F32), sds((TOK, D), BF), sds((TOK, D), BF),
            sds((4 * RA, 128), BF), sds((4 * RA, 128), BF),
        ],
        args,
        scratch=[
            pltpu.VMEM((D, 1024), BF), pltpu.VMEM((D, 512), BF),
            pltpu.VMEM((WIN, D), F32), pltpu.VMEM((1, NP), F32),
            pltpu.VMEM((TOK, 1024), F32), pltpu.VMEM((WIN, 512), F32), pltpu.VMEM((TOK, 1024), BF), pltpu.VMEM((WIN, 512), BF),
        ],
        in_specs=[SMEM] + [VMEM] * 16, mem=28, name="last", us=14,
    )


def per_device(
    tokens, cotangent, segment_ids, width_mask,
    q_codes, kv_codes, o_codes, gate_codes, up_codes, down_codes,
    q_scale, kv_scale, o_scale, gate_scale, up_scale, down_scale, norm_gains,
):
    c, x, y = lax.axis_index("c"), lax.axis_index("x"), lax.axis_index("y")
    zl, zh = lax.axis_index("zl"), lax.axis_index("zh")
    z = zh * 2 + zl
    lane_of, dev_of = lane_tables()

    p, s = jnp.arange(128, dtype=jnp.int32) // 16, jnp.arange(128, dtype=jnp.int32) % 16
    shift = (s % 4, s // 4, p % 4)
    core = jnp.where(p < 4, c, 1 - c)
    sx, sy, sz = (
        (at - jnp.where(core == 0, shift[ORDER[0].index(a)], shift[ORDER[1].index(a)])) % 4 for at, a in ((x, "x"), (y, "y"), (z, "z"))
    )
    inat = ((((sz % 2) * 2 + core) * 2 + sz // 2) * 4 + sy) * 4 + sx
    dk = (5 * inat[None, :] + jnp.arange(5, dtype=jnp.int32)[:, None]).reshape(1, D)
    dev_col = inat[:, None]

    place = (y % 2) * 4 + x
    seq = zh * 2 + y // 2
    segs = lax.dynamic_slice_in_dim(segment_ids, seq, 1, 0)
    run = lax.dynamic_slice_in_dim(width_mask, seq, 1, 0)[0]
    padded = jnp.concatenate([jnp.full((1, WINDOW), -1, jnp.int32), segs], axis=1)
    segk = lax.dynamic_slice_in_dim(padded, place * TOK, WIN, 1)
    segq = segk[0, WINDOW:][:, None]
    pos = (place * TOK - WINDOW + jnp.arange(WIN, dtype=jnp.int32)).astype(F32)
    inverse = 10000.0 ** (-2.0 * jnp.arange(HD // 2).astype(F32) / HD)
    angles = pos[:, None] * inverse[None, :]
    cos, sin = jnp.cos(angles), jnp.sin(angles)

    shard = call(
        pack_kernel, sds((N, 128), BF),
        (q_codes, kv_codes, o_codes, gate_codes, up_codes, down_codes, q_scale, kv_scale, o_scale, gate_scale, up_scale, down_scale, norm_gains),
        scratch=[pltpu.VMEM((N, 128), F32)], name="pack", us=0,
    )
    early = (run, inat, dk, dev_col, segq, segk, cos, sin)
    mine_a, theirs_a, mine_b, their_first, t0, t1, early = gather(shard, tokens, early)
    run, inat, dk, dev_col, segq, segk, cos, sin = early

    par, h1p, q, kv, mix = run_first((run, mine_a, theirs_a, dev_col, lane_of, dev_of, t0, t1, tokens, dk, cos, sin, segq, segk))
    mix, *late = lax.optimization_barrier((mix, *mine_b[1:]))
    pieces_b = [mine_b[0], *late, their_first] + [other_core(b) for b in late]
    out, rest, gmix, gm_b, gt_b, gpar = run_middle((run, inat, mix, tokens, cotangent, *pieces_b, par, dk))
    got_b = other_core(gt_b)
    gqb, gkvb = [], []
    for first, count in ((0, 1), (1, 2)):
        got = run_attnb(first, count, (run, par, cos, sin, segq, segk, q, kv, gmix, gpar))
        gqb.append(got[0])
        gkvb.append(got[1])
        gpar = got[2]
        if first == 0:
            gpar, got_b = lax.optimization_barrier((gpar, got_b))
            parts_b = first_hop(gm_b, got_b, RB, 2, 0)
            gpar, parts_b[0] = lax.optimization_barrier((gpar, parts_b[0]))
    own, back1, back2, gm_a, gt_a = run_last(
        (run, h1p, mine_a, theirs_a, gqb[0], gkvb[0], gqb[1], gkvb[1], par, gpar, dk, dev_col, lane_of, dev_of, t0, t1, tokens)
    )
    gt_a, *parts_b = lax.optimization_barrier((gt_a, *parts_b))
    parts_a = first_hop(gm_a, other_core(gt_a), RA, 1, 0)
    gq, gkv, gate, up, down, o, *small = scatter(
        parts_a, parts_b,
        [sds((5, 1024), F32), sds((5, 512), F32), sds((5, FF), F32), sds((5, FF), F32), sds((16, D), F32), sds((8, D), F32),
         sds((8,), F32), sds((4,), F32), sds((5,), F32), sds((16,), F32), sds((16,), F32), sds((5,), F32), sds((5, 4), F32)],
    )
    forth = lambda k: [(j, i) for i, j in behind(k)]
    got1 = lax.ppermute(back1, ("y", "x"), forth(1))
    got2 = lax.ppermute(back2, ("y", "x"), forth(2))
    grad_tokens = call(end_kernel, sds((TOK, D), F32), (own, got1, got2, tokens, rest, par), name="end", mem=24, us=0)

    return (out, grad_tokens, gq, gkv, o, gate, up, down, *small)


def solution(mesh):
    fine = Mesh(mesh.devices.reshape(2, 2, 2, 4, 4), AX)
    rows, seqs = P(AX, None), P(("zl", "c"), None)
    wide = P(None, AX, None)
    return jax.shard_map(
        per_device,
        mesh=fine,
        in_specs=(rows, wide, seqs, seqs) + (rows,) * 6 + (P(AX),) * 6 + (rows,),
        out_specs=(wide, rows) + (rows,) * 6 + (P(AX),) * 6 + (rows,),
        check_vma=False,
    )
```

```python
import functools
import itertools
import math

import jax
import jax.numpy as jnp
import numpy as np
from jax import lax
from jax.experimental import pallas as pl
from jax.experimental.pallas import tpu as pltpu
from jax.sharding import Mesh
from jax.sharding import PartitionSpec as P

AX = ("zl", "c", "zh", "y", "x")
F32 = jnp.float32
BF = jnp.bfloat16
EPS = 1e-6
D, HEADS, HD, FF, WINDOW = 640, 4, 256, 2048, 512
TOK = 256
WIN = 768
ORDER = (("x", "y", "z"), ("y", "z", "x"))
NA = 64
NB = 288
N = NA + NB
INT_A, INT_B = 64, 160
RA, RB = 16 * NA, 16 * NB
DOWN_ROW, O_ROW = 2560, 3840
NP = 9472
SEG = dict(q=(0, 1024, 8, 0), kv=(1024, 512, 4, 8), o=(1536, 640, 5, 12), gate=(2176, 2048, 16, 17),
           up=(4224, 2048, 16, 33), down=(6272, 640, 5, 49))
OQ, OKV, OO, OG, OU, OD, ON = 0, 1024, 1536, 2176, 4224, 6272, 6912
U_D = 1.0 / (128.0 * math.sqrt(D))
U_O = 1.0 / (128.0 * math.sqrt(HEADS * HD))
U_F = 1.0 / (128.0 * math.sqrt(FF))
VMEM = pl.BlockSpec(memory_space=pltpu.VMEM)
SMEM = pl.BlockSpec(memory_space=pltpu.SMEM)


def lane_tables():
    lane, dev = np.zeros((1, NP), np.int32), np.zeros((1, NP), np.int32)
    for at, size, each, first in SEG.values():
        c = np.arange(size)
        lane[0, at : at + size] = first + c % each
        dev[0, at : at + size] = c // each
    for g in range(4):
        c = np.arange(D)
        at = ON + g * D
        lane[0, at : at + D] = 54 + g * 5 + c % 5
        dev[0, at : at + D] = c // 5
    return lane, dev


def cost_of(us):
    return pl.CostEstimate(flops=int(us * 1e6) + 1000, bytes_accessed=1000, transcendentals=0)


def call(kernel, out_shape, ins, scratch=(), mem=62, us=1, in_specs=None, name=None):
    params = dict(vmem_limit_bytes=mem << 20)
    return pl.pallas_call(
        kernel,
        out_shape=out_shape,
        in_specs=in_specs or [VMEM] * len(ins),
        out_specs=jax.tree.map(lambda s: VMEM, out_shape),
        scratch_shapes=list(scratch),
        compiler_params=pltpu.CompilerParams(**params),
        cost_estimate=cost_of(us),
        name=name,
    )(*ins)


def sds(shape, dtype):
    return jax.ShapeDtypeStruct(shape, dtype)


def dot(a, b):
    return jnp.dot(a, b, preferred_element_type=F32)


def dot_t(a, b):
    return lax.dot_general(a, b, (((1,), (1,)), ((), ())), preferred_element_type=F32)


def t_dot(a, b):
    return lax.dot_general(a, b, (((0,), (0,)), ((), ())), preferred_element_type=F32)


def flat(c, x, y, z):
    return ((((z & 1) * 2 + c) * 2 + (z >> 1)) * 4 + y) * 4 + x


@functools.lru_cache(None)
def stage_pairs(stage, r):
    pairs = []
    for c, x, y, z in itertools.product(range(2), range(4), range(4), range(4)):
        at = dict(x=x, y=y, z=z)
        axis = ORDER[c][stage]
        at[axis] = (at[axis] + r) % 4
        pairs.append((flat(c, x, y, z), flat(c, **at)))
    return tuple(sorted(pairs))


def send(a, stage, r):
    return lax.ppermute(a, AX, stage_pairs(stage, r % 4))


def behind(k):
    return [(i, i + k) for i in range(16) if i % 8 + k < 8]


def other_core(a):
    return lax.ppermute(a, "c", [(0, 1), (1, 0)])


def swap_matrix():
    row = lax.broadcasted_iota(jnp.int32, (256, 256), 0)
    col = lax.broadcasted_iota(jnp.int32, (256, 256), 1)
    return ((row % 16) * 16 + row // 16 == col).astype(BF)


BLOCKS = ((224, 80, DOWN_ROW), (304, 48, O_ROW))


def asm_kernel(*refs):
    ins, out_a, out_b = refs[:4], refs[4], refs[5]
    swap = swap_matrix()
    for g in range((INT_A + INT_B) // 16):
        x = jnp.concatenate(
            [ins[s // 4][(s % 4) * N + 16 * g : (s % 4) * N + 16 * g + 16, :] for s in range(16)], axis=0
        )
        y = dot(swap, x).astype(BF)
        if g < 4:
            out_a[256 * g : 256 * g + 256, :] = y
        else:
            out_b[256 * (g - 4) : 256 * (g - 4) + 256, :] = y
    for first, lines, row in BLOCKS:
        for s in range(16):
            at = (s % 4) * N + first
            out_b[row + s * lines : row + (s + 1) * lines, :] = ins[s // 4][at : at + lines, :]


def join_kernel(a, b, c, d, out):
    for r, ref in enumerate((a, b, c, d)):
        out[r * RA : (r + 1) * RA, :] = ref[...]


def gather(shard, tokens, early):
    one = jnp.concatenate([shard] + [send(shard, 0, r) for r in (1, 2, 3)], axis=0)
    t1, t0 = (lax.ppermute(tokens, ("y", "x"), behind(k)) for k in (1, 2))
    two = [one] + [send(one, 1, r) for r in (1, 2, 3)]
    two[0], t0, t1, *early = lax.optimization_barrier((two[0], t0, t1, *early))
    piece_a, piece_b = call(asm_kernel, [sds((RA, 128), BF), sds((RB, 128), BF)], two, name="asm", us=0)
    mine_a = [piece_a] + [send(piece_a, 2, r) for r in (1, 2, 3)]
    mine_a = call(join_kernel, sds((4 * RA, 128), BF), mine_a, name="join", us=0)
    theirs_a = other_core(mine_a)
    mine_b = [piece_b] + [send(piece_b, 2, r) for r in (1, 2, 3)]
    return mine_a, theirs_a, mine_b, other_core(piece_b), t0, t1, early


def rs1_kernel(a, b, *outs):
    for r in range(4):
        outs[r][...] = (a[r].astype(F32) + b[r].astype(F32)).astype(BF)


def total4(refs, at, rows):
    t = refs[0][at : at + rows, :].astype(F32)
    for ref in refs[1:]:
        t = t + ref[at : at + rows, :].astype(F32)
    return t


def add_kernel(a, b, out):
    out[...] = (a[...].astype(F32) + b[...].astype(F32)).astype(BF)


def rs2_kernel(*refs):
    a, b, outs = refs[:4], refs[4:9], refs[9:]
    swap = swap_matrix()
    for g in range((INT_A + INT_B) // 16):
        t = total4(a, 256 * g, 256) if g < 4 else total4(b, 256 * (g - 4), 256)
        y = dot(swap, t.astype(BF)).astype(BF)
        for s in range(16):
            at = (s % 4) * N + 16 * g
            outs[s // 4][at : at + 16, :] = y[16 * s : 16 * s + 16]
    for first, lines, row in BLOCKS:
        for s in range(16):
            at = (s % 4) * N + first
            outs[s // 4][at : at + lines, :] = total4(b, row + s * lines, lines).astype(BF)


def rs3_kernel(*refs):
    ins, outs = refs[:4], refs[4:]
    for r in range(4):
        outs[r][...] = total4(ins, r * N, N).astype(BF)


def rs4_kernel(a0, a1, a2, a3, q, kv, gate, up, down, o, *small):
    t = total4((a0, a1, a2, a3), 0, N)
    for cb in range(8):
        q[:, cb * 128 : cb * 128 + 128] = t[cb * 5 : cb * 5 + 5]
    for cb in range(4):
        kv[:, cb * 128 : cb * 128 + 128] = t[40 + cb * 5 : 45 + cb * 5]
    at = 0
    for ref in small[:6]:
        ref[...] = t[60, at : at + ref.shape[0]]
        at += ref.shape[0]
    for g in range(4):
        small[6][g : g + 1, :] = t[60:61, at + 5 * g : at + 5 * g + 5]
    for cb in range(16):
        gate[:, cb * 128 : cb * 128 + 128] = t[64 + cb * 5 : 69 + cb * 5]
        up[:, cb * 128 : cb * 128 + 128] = t[144 + cb * 5 : 149 + cb * 5]
    for cb in range(5):
        down[:, cb * 128 : cb * 128 + 128] = t[224 + cb * 16 : 240 + cb * 16]
        o[:, cb * 128 : cb * 128 + 128] = t[304 + cb * 8 : 312 + cb * 8]


def first_hop(mine, got, rows, grid, us):
    block = rows // grid
    parts = pl.pallas_call(
        rs1_kernel,
        grid=(grid,),
        out_shape=[sds((rows, 128), BF)] * 4,
        in_specs=[pl.BlockSpec((4, block, 128), lambda i: (0, i, 0))] * 2,
        out_specs=[pl.BlockSpec((block, 128), lambda i: (i, 0))] * 4,
        compiler_params=pltpu.CompilerParams(vmem_limit_bytes=24 << 20),
        cost_estimate=cost_of(us),
        name=f"rs1_{rows}",
    )(mine.reshape(4, rows, 128), got.reshape(4, rows, 128))
    return [parts[0]] + [send(parts[r], 2, -r) for r in (1, 2, 3)]


def scatter(a, b, out_shape):
    parts = call(rs2_kernel, [sds((4 * N, 128), BF)] * 4, a + b, name="rs2", mem=24, us=0)
    parts = [parts[0]] + [send(parts[r], 1, -r) for r in (1, 2, 3)]
    parts = call(rs3_kernel, [sds((N, 128), BF)] * 4, parts, name="rs3", mem=24, us=0)
    parts = [parts[0]] + [send(parts[r], 0, -r) for r in (1, 2, 3)]
    return call(rs4_kernel, out_shape, parts, name="rs4", mem=24, us=0)


def pack_kernel(q, kv, o, gate, up, down, sq, skv, so, sg, su, sd, gains, out, wide):
    for cb in range(8):
        wide[cb * 5 : cb * 5 + 5, :] = q[:, cb * 128 : cb * 128 + 128].astype(F32)
    for cb in range(4):
        wide[40 + cb * 5 : 45 + cb * 5, :] = kv[:, cb * 128 : cb * 128 + 128].astype(F32)
    row = [ref[...].reshape(1, -1) for ref in (sq, skv, so, sg, su, sd)] + [gains[g : g + 1, :] for g in range(4)]
    v = jnp.concatenate(row + [jnp.zeros((1, 54), F32)], axis=1)
    hi = v.astype(BF).astype(F32)
    mid = (v - hi).astype(BF).astype(F32)
    wide[60:61, :] = hi
    wide[61:62, :] = mid
    wide[62:63, :] = v - hi - mid
    wide[63:64, :] = jnp.zeros((1, 128), F32)
    for cb in range(16):
        wide[64 + cb * 5 : 69 + cb * 5, :] = gate[:, cb * 128 : cb * 128 + 128].astype(F32)
        wide[144 + cb * 5 : 149 + cb * 5, :] = up[:, cb * 128 : cb * 128 + 128].astype(F32)
    for cb in range(5):
        wide[224 + cb * 16 : 240 + cb * 16, :] = down[:, cb * 128 : cb * 128 + 128].astype(F32)
        wide[304 + cb * 8 : 312 + cb * 8, :] = o[:, cb * 128 : cb * 128 + 128].astype(F32)
    wide[344:352, :] = jnp.zeros((8, 128), F32)
    out[...] = wide[...].astype(BF)


def piece(mine, theirs, p, rows):
    return (mine if p < 4 else theirs), (p % 4) * rows


def perm_matrix(dk):
    return (lax.broadcasted_iota(jnp.int32, (D, D), 0) == dk).astype(BF)


def steps_of(b):
    step = jnp.where(b == 0, 1.0, jnp.where(b == 1, 16.0, 64.0)).astype(F32)
    inv = jnp.where(b == 0, 1.0, jnp.where(b == 1, 1.0 / 16, 1.0 / 64)).astype(F32)
    return step, inv


def level_maker(b, rows=16, dtype=BF):
    step, inv = steps_of(b)
    step_v = jnp.full((rows, 128), step, F32)
    inv_v = jnp.full((rows, 128), inv, F32).astype(dtype)
    half_v = (step_v * 0.5).astype(dtype)
    step_v = step_v.astype(dtype)
    return lambda c: jnp.floor(c * inv_v) * step_v + half_v


def dequant_a(b, mine, theirs, lq, lkv):
    level = level_maker(b)
    for p in range(8):
        ref, base = piece(mine, theirs, p, RA)
        for j in range(5):
            for cb in range(8):
                at = base + (cb * 5 + j) * 16
                lq[j * 128 + p * 16 : j * 128 + p * 16 + 16, cb * 128 : cb * 128 + 128] = level(ref[at : at + 16, :])
            for cb in range(4):
                at = base + (40 + cb * 5 + j) * 16
                lkv[j * 128 + p * 16 : j * 128 + p * 16 + 16, cb * 128 : cb * 128 + 128] = level(ref[at : at + 16, :])


def column(row):
    n = row.shape[1]
    eye = lax.broadcasted_iota(jnp.int32, (n, n), 0) == lax.broadcasted_iota(jnp.int32, (n, n), 1)
    return jnp.sum(jnp.where(eye, row.astype(F32), 0.0), axis=1, keepdims=True).astype(jnp.int32)


def make_mask(segk, mask):
    for t in range(2):
        mine = column(segk[:, WINDOW + t * 128 : WINDOW + t * 128 + 128])
        r = lax.broadcasted_iota(jnp.int32, (128, 640), 0)
        c = lax.broadcasted_iota(jnp.int32, (128, 640), 1)
        ok = (c <= WINDOW + r) & (c > r)
        ok = ok & (mine == segk[:, t * 128 : t * 128 + 640])
        mask[t] = ok.astype(F32)


def rope(v, cos, sin):
    a, b = v[:, :128], v[:, 128:]
    return jnp.concatenate([a * cos - b * sin, b * cos + a * sin], axis=1)


def unrope(v, cos, sin):
    a, b = v[:, :128], v[:, 128:]
    return jnp.concatenate([a * cos + b * sin, b * cos - a * sin], axis=1)


TANH_IN = 1.0 / (16.0 * 50.0)
EXP2_IN = 50.0 * math.log2(math.e)


def first_kernel(
    run, mine, theirs, dev_row, lane_of, dev_of, t0, t1, t2, dk, cos, sin, segk,
    par, h1p, q_out, kv_out, mix_out, lq, lkv, mask, sc, ex,
):
    lines = []
    for l in (60, 61, 62):
        refs = [piece(mine, theirs, p, RA) for p in range(8)]
        lines.append(jnp.concatenate([ref[at + l * 16 : at + l * 16 + 16, :] for ref, at in refs], axis=0))
    lines = jnp.concatenate(lines, axis=1)
    devs = column(dev_row[...])
    row = lax.broadcasted_iota(jnp.int32, (128, 256), 0)
    for i in range(NP // 256):
        cols = slice(i * 256, i * 256 + 256)
        one_hot = (row == lane_of[:, cols]).astype(BF)
        t = dot(lines, jnp.concatenate([one_hot] * 3, axis=0))
        t = jnp.where(devs == dev_of[:, cols], t, 0.0)
        par[:, cols] = jnp.sum(t, axis=0, keepdims=True)
    perm = perm_matrix(dk[...])
    gain = par[:, ON : ON + D]
    for k, t in enumerate((t0, t1, t2)):
        v = t[...].astype(F32)
        h = v * lax.rsqrt(jnp.mean(v * v, axis=-1, keepdims=True) + EPS) * gain
        h1p[k * 256 : k * 256 + 256, :] = dot(h.astype(BF), perm).astype(BF)
    make_mask(segk, mask)

    def width(b, carry):
        @pl.when(run[b] == 0)
        def _():
            mix_out[b] = jnp.zeros((TOK, HEADS * HD), BF)

        @pl.when(run[b] > 0)
        def _():
            dequant_a(b, mine, theirs, lq, lkv)
            own = h1p[512:768, :]
            co, so = cos[512:768, :], sin[512:768, :]
            for h in range(4):
                scale = par[:, OQ + h * 256 : OQ + h * 256 + 256] * U_D
                q = rope(dot(own, lq[:, h * 256 : h * 256 + 256]) * scale, co, so).astype(BF)
                for t in range(2):
                    q_out[b, t, h * 128 : h * 128 + 128, :] = q[t * 128 : t * 128 + 128]
            for k in range(3):
                rows = h1p[k * 256 : k * 256 + 256, :]
                cw, sw = cos[k * 256 : k * 256 + 256, :], sin[k * 256 : k * 256 + 256, :]
                key = dot(rows, lkv[:, :256]) * (par[:, OKV : OKV + 256] * U_D)
                kv_out[b, k * 256 : k * 256 + 256, 0:256] = rope(key, cw, sw).astype(BF)
                val = dot(rows, lkv[:, 256:]) * (par[:, OKV + 256 : OKV + 512] * U_D)
                kv_out[b, k * 256 : k * 256 + 256, 256:512] = val.astype(BF)
            ones = jnp.ones((640, 128), BF)
            for t in range(2):
                sc[t] = dot_t(q_out[b, t], kv_out[b, t * 128 : t * 128 + 640, 0:256])
            for t in range(2):
                for i in range(16):
                    rows = slice(i * 32, i * 32 + 32)
                    m = mask[t, (i % 4) * 32 : (i % 4) * 32 + 32, :]
                    ex[t, rows, :] = (jnp.exp2(jnp.tanh(sc[t, rows, :] * TANH_IN) * EXP2_IN) * m).astype(BF)
                e = ex[t]
                inv = 1.0 / dot(e, ones)
                mixed = dot(e, kv_out[b, t * 128 : t * 128 + 640, 256:512]) * jnp.concatenate([inv, inv], axis=1)
                for h in range(4):
                    mix_out[b, t * 128 : t * 128 + 128, h * 256 : h * 256 + 256] = mixed[h * 128 : h * 128 + 128].astype(BF)

        return carry

    lax.fori_loop(0, 3, width, 0)


def mean_of(v):
    return jnp.mean(v, axis=-1, keepdims=True)


C_G = math.sqrt(2.0 / math.pi)
C_3 = C_G * 0.044715
PARTS = ((O_ROW, 768), (0, 2560), (DOWN_ROW, 1280))


def middle_kernel(
    run, inat, mix, tok, cot, b0, b1, b2, b3, b4, b5, b6, b7, par, dk,
    out, rest, gmix, g0, g1_, g2_, g3_, g4, g5, g6, g7, gpar,
    pcs, lgu, ld, lo, onat, gu32, gate, up, aa, bb, hid, gg, gu, h2s, gbr, gat, att, mid, acc, perm, outv,
    in_sem, gu_sem, do_sem, out_sem,
):
    dwd, dwo = ld, onat
    loads = [
        [
            pltpu.make_async_copy(ref.at[pl.ds(first, rows)], pcs.at[p, pl.ds(first, rows)], in_sem.at[k, p])
            for p, ref in enumerate((b0, b1, b2, b3, b4, b5, b6, b7))
        ]
        for k, (first, rows) in enumerate(PARTS)
    ]
    for group in loads:
        for copy in group:
            copy.start()
    perm[...] = perm_matrix(dk[...])
    rest[...] = jnp.zeros_like(rest)
    gpar[...] = jnp.zeros_like(gpar)
    for copy in loads[0]:
        copy.wait()
    for p in range(8):
        for s in range(16):
            at = O_ROW + s * 48
            block = pcs[p, at : at + 48, :].astype(F32)
            row = pl.multiple_of(inat[p * 16 + s] * 8, 8)
            for cb in range(5):
                onat[pl.ds(row, 8), cb * 128 : cb * 128 + 128] = block[cb * 8 : cb * 8 + 8]
    def width(b, carry):
        rows = pl.ds(pl.multiple_of(b * TOK, TOK), TOK)

        @pl.when(run[b] == 0)
        def _():
            outv[b] = jnp.zeros((TOK, D), F32)
            hid[rows, :] = jnp.zeros((TOK, FF), BF)
            gg[rows, :] = jnp.zeros((TOK, FF), BF)
            gu[rows, :] = jnp.zeros((TOK, FF), BF)
            h2s[rows, :] = jnp.zeros((TOK, D), BF)
            gbr[rows, :] = jnp.zeros((TOK, D), BF)
            gat[rows, :] = jnp.zeros((TOK, D), BF)

        @pl.when(run[b] > 0)
        def _():
            level = level_maker(b)
            wide = level_maker(b, 8, F32)
            for r in range(64):
                for cb in range(5):
                    two = [wide(onat[r * 16 + k * 8 : r * 16 + k * 8 + 8, cb * 128 : cb * 128 + 128]) for k in (0, 1)]
                    lo[r * 16 : r * 16 + 16, cb * 128 : cb * 128 + 128] = jnp.concatenate(two, axis=0).astype(BF)
            s_o = par[:, OO : OO + D] * U_O
            s_d = par[:, OD : OD + D] * U_F
            g1, g2, g3 = (par[:, ON + k * D : ON + (k + 1) * D] for k in (1, 2, 3))
            attended = dot(mix[b], lo[...]) * s_o
            att[...] = attended
            r1 = lax.rsqrt(mean_of(attended * attended) + EPS)
            middle = tok[...].astype(F32) + attended * r1 * g1
            mid[...] = middle
            r2 = lax.rsqrt(mean_of(middle * middle) + EPS)
            h2 = (middle * r2 * g2).astype(BF)
            h2p = dot(h2, perm[...]).astype(BF)
            h2s[rows, :] = h2p

            @pl.when(carry == 0)
            def _():
                for copy in loads[1] + loads[2]:
                    copy.wait()

            def gate_up(f):
                for half in range(2):
                    cb = f * 2 + half
                    for first, to in ((0, f * 512), (80, f * 512 + 256)):
                        for j in range(5):
                            for p in range(8):
                                at = (first + cb * 5 + j) * 16
                                k = j * 128 + p * 16
                                col = to + half * 128
                                lgu[k : k + 16, col : col + 128] = level(pcs[p, at : at + 16, :])
                gu32[f % 2] = dot(h2p, lgu[:, f * 512 : f * 512 + 512])

            gate_up(0)
            for p in range(8):
                for s in range(16):
                    row = pl.multiple_of(inat[p * 16 + s] * 16, 16)
                    for cb in range(5):
                        at = DOWN_ROW + s * 80 + cb * 16
                        ld[pl.ds(row, 16), cb * 128 : cb * 128 + 128] = level(pcs[p, at : at + 16, :])
            for f in range(8):
                if f < 7:
                    gate_up(f + 1)
                cols = slice(f * 256, f * 256 + 256)
                s_g, s_u = par[:, OG + f * 256 : OG + f * 256 + 256] * U_D, par[:, OU + f * 256 : OU + f * 256 + 256] * U_D
                parts = []
                for rc in range(8):
                    rr = slice(rc * 32, rc * 32 + 32)
                    x = gu32[f % 2, rr, 0:256] * s_g
                    u = gu32[f % 2, rr, 256:512] * s_u
                    gate[rr, cols] = x.astype(BF)
                    up[rr, cols] = u.astype(BF)
                    x2 = x * x
                    hf = 0.5 * jnp.tanh(x * (C_G + C_3 * x2)) + 0.5
                    gl = x * hf
                    aa[rr, cols] = u * (hf + (gl - gl * hf) * (2 * C_G + (6 * C_3) * x2))
                    bb[rr, cols] = gl
                    parts.append((gl * u).astype(BF))
                h = jnp.concatenate(parts, axis=0)
                hid[rows, cols] = h
                add = dot(h, ld[cols, :])
                acc[...] = add if f == 0 else acc[...] + add
            branch = acc[...] * s_d
            r3 = lax.rsqrt(mean_of(branch * branch) + EPS)
            outv[b] = mid[...] + branch * r3 * g3
            gy = cot[b].astype(F32)
            gpar[:, ON + 3 * D : ON + 4 * D] += jnp.sum(gy * branch * r3, axis=0, keepdims=True)
            w = g3 * gy
            gb = r3 * w - branch * (r3 * r3 * r3 * mean_of(w * branch))
            gpar[:, OD : OD + D] += jnp.sum(gb * branch, axis=0, keepdims=True)
            gb = (gb * s_d).astype(BF)
            gbr[rows, :] = gb

            def grad_hidden(f):
                gu32[f % 2, :, 0:256] = dot_t(gb, ld[f * 256 : f * 256 + 256, :])

            ones = jnp.ones((8, TOK), BF)
            grad_hidden(0)
            for f in range(8):
                if f < 7:
                    grad_hidden(f + 1)
                cols = slice(f * 256, f * 256 + 256)
                col_g, col_u = slice(OG + f * 256, OG + f * 256 + 256), slice(OU + f * 256, OU + f * 256 + 256)
                s_g, s_u = par[:, col_g] * U_D, par[:, col_u] * U_D
                parts, prods = [], []
                for rc in range(8):
                    rr = slice(rc * 32, rc * 32 + 32)
                    g = gu32[f % 2, rr, 0:256]
                    gg_b = (g * aa[rr, cols] * s_g).astype(BF)
                    gu_b = (g * bb[rr, cols] * s_u).astype(BF)
                    parts.append(jnp.concatenate([gg_b, gu_b], axis=1))
                    prods.append(jnp.concatenate([gg_b * gate[rr, cols], gu_b * up[rr, cols]], axis=1))
                both = jnp.concatenate(parts, axis=0)
                gg[rows, cols] = both[:, 0:256]
                gu[rows, cols] = both[:, 256:512]
                sums = dot(ones, jnp.concatenate(prods, axis=0))
                gpar[:, col_g] += sums[0:1, 0:256]
                gpar[:, col_u] += sums[0:1, 256:512]
                add = dot_t(both, lgu[:, f * 512 : f * 512 + 512])
                acc[...] = add if f == 0 else acc[...] + add
            g_h2 = dot_t(acc[...].astype(BF), perm[...])
            middle = mid[...]
            attended = att[...]
            gpar[:, ON + 2 * D : ON + 3 * D] += jnp.sum(g_h2 * middle * r2, axis=0, keepdims=True)
            w = g2 * g_h2
            gmid = cot[b].astype(F32) + r2 * w - middle * (r2 * r2 * r2 * mean_of(w * middle))
            rest[...] += gmid
            gpar[:, ON + D : ON + 2 * D] += jnp.sum(gmid * attended * r1, axis=0, keepdims=True)
            w = g1 * gmid
            ga = r1 * w - attended * (r1 * r1 * r1 * mean_of(w * attended))
            gpar[:, OO : OO + D] += jnp.sum(ga * attended, axis=0, keepdims=True)
            ga = (ga * s_o).astype(BF)
            gat[rows, :] = ga
            gmix[b] = dot_t(ga, lo[...]).astype(BF)

        return carry + run[b]

    lax.fori_loop(0, 3, width, 0)
    out_copy = pltpu.make_async_copy(outv, out, out_sem)
    out_copy.start()
    gpar[:, OO : OO + D] = gpar[:, OO : OO + D] / par[:, OO : OO + D]
    for at in (OG, OU):
        scale = par[:, at : at + FF]
        gpar[:, at : at + FF] = gpar[:, at : at + FF] / (scale * scale * U_D)
    gpar[:, OD : OD + D] = gpar[:, OD : OD + D] / par[:, OD : OD + D]

    stores = []

    def leave(p, first, rows, sem):
        to = (g0, g1_, g2_, g3_, g4, g5, g6, g7)[p]
        copy = pltpu.make_async_copy(pcs.at[p, pl.ds(first, rows)], to.at[pl.ds(first, rows)], sem)
        copy.start()
        stores.append(copy)

    g_all = gbr[...]
    for f in range(8):
        cols = slice(f * 256, f * 256 + 256)
        dwd[cols, :] = t_dot(hid[:, cols], g_all).astype(BF)
    for p in range(8):
        for s in range(16):
            row = pl.multiple_of(inat[p * 16 + s] * 16, 16)
            for cb in range(5):
                at = DOWN_ROW + s * 80 + cb * 16
                pcs[p, at : at + 16, :] = dwd[pl.ds(row, 16), cb * 128 : cb * 128 + 128]
        leave(p, DOWN_ROW, 1280, do_sem.at[0, p])
    for h in range(4):
        w = jnp.zeros((256, D), F32)
        for b in range(3):
            w = w + t_dot(mix[b, :, h * 256 : h * 256 + 256], gat[b * TOK : (b + 1) * TOK, :])
        dwo[h * 256 : h * 256 + 256, :] = w
    for p in range(8):
        for s in range(16):
            row = pl.multiple_of(inat[p * 16 + s] * 8, 8)
            parts = [dwo[pl.ds(row, 8), cb * 128 : cb * 128 + 128] for cb in range(5)] + [jnp.zeros((8, 128), F32)]
            at = O_ROW + s * 48
            pcs[p, at : at + 48, :] = jnp.concatenate(parts, axis=0).astype(BF)
        leave(p, O_ROW, 768, do_sem.at[1, p])
    h2t = h2s[...]
    for f in range(8):
        cols = slice(f * 256, f * 256 + 256)
        for k, (first, ref) in enumerate(((0, gg), (80, gu))):
            w = t_dot(h2t, ref[:, cols]).astype(BF)
            for half in range(2):
                for j in range(5):
                    for p in range(8):
                        at = (first + (f * 2 + half) * 5 + j) * 16
                        r = j * 128 + p * 16
                        pcs[p, at : at + 16, :] = w[r : r + 16, half * 128 : half * 128 + 128]
            if f % 2:
                for p in range(8):
                    leave(p, (first + (f - 1) * 10) * 16, 320, gu_sem.at[f // 2, k, p])
    for copy in stores:
        copy.wait()
    out_copy.wait()


def back_kernel(
    run, par, cos, sin, segk, gpar_in, dk, dev_row, lane_of, dev_of,
    q_far, kv_far, gmix_far, mine_far, theirs_far, h1p_far, t0_far, t1_far, t2_far,
    own, back1, back2, g_mine, g_theirs,
    q, kv, gmix, mine, theirs, h1p, toks, mask, sc, gp, ex, wt, pb, gz, gq, gkv, gq_sum, gkv_sum, gqb, gkvb, lq, lkv, gh1, gpar,
    sem, sem_late,
):
    loads = [
        [pltpu.make_async_copy(far.at[b], near.at[b], sem.at[b, k]) for k, (far, near) in enumerate(((q_far, q), (kv_far, kv), (gmix_far, gmix)))]
        for b in range(3)
    ]
    late = [
        pltpu.make_async_copy(far, near, sem_late.at[k])
        for k, (far, near) in enumerate(((mine_far, mine), (theirs_far, theirs), (h1p_far, h1p)))
    ]
    last = [pltpu.make_async_copy(far, toks.at[k], sem_late.at[3 + k]) for k, far in enumerate((t0_far, t1_far, t2_far))]
    for copy in loads[0] + late + loads[1] + loads[2] + last:
        copy.start()
    for t in range(2):
        k = lax.broadcasted_iota(jnp.int32, (640, 128), 0)
        r = lax.broadcasted_iota(jnp.int32, (640, 128), 1)
        ok = (k <= WINDOW + r) & (k > r)
        keys = jnp.concatenate([column(segk[:, (t + i) * 128 : (t + i + 1) * 128]) for i in range(5)], axis=0)
        ok = ok & (keys == segk[:, WINDOW + t * 128 : WINDOW + t * 128 + 128])
        mask[t] = ok.astype(F32)
    gpar[...] = gpar_in[...]
    gh1[...] = jnp.zeros_like(gh1)
    gq_sum[...] = jnp.zeros_like(gq_sum)
    gkv_sum[...] = jnp.zeros_like(gkv_sum)

    def width(b, seen):
        for k, (far, near) in enumerate(((q_far, q), (kv_far, kv), (gmix_far, gmix))):
            pltpu.make_async_copy(far.at[b], near.at[b], sem.at[b, k]).wait()

        @pl.when(run[b] > 0)
        def _():
            gkv[...] = jnp.zeros_like(gkv)
            gms = []
            for t in range(2):
                gm = jnp.concatenate(
                    [gmix[b, t * 128 : t * 128 + 128, h * 256 : h * 256 + 256] for h in range(4)], axis=0
                )
                gms.append(gm)
                sc[t] = dot_t(kv[b, t * 128 : t * 128 + 640, 0:256], q[b, t])
                gp[t] = dot_t(kv[b, t * 128 : t * 128 + 640, 256:512], gm)
            for t in range(2):
                for h in range(4):
                    cols = slice(h * 128, h * 128 + 128)
                    total, dot_sum = jnp.zeros((16, 128), F32), jnp.zeros((16, 128), F32)
                    for i in range(40):
                        rows = slice(i * 16, i * 16 + 16)
                        th = jnp.tanh(sc[t, rows, cols] * TANH_IN)
                        e = jnp.exp2(th * EXP2_IN) * mask[t, rows, :]
                        ex[t, rows, cols] = e
                        wt[t, rows, cols] = 1.0 - th * th
                        total = total + e
                        dot_sum = dot_sum + e * gp[t, rows, cols]
                    inv = 1.0 / jnp.sum(total, axis=0, keepdims=True)
                    dd = jnp.sum(dot_sum, axis=0, keepdims=True) * inv
                    inv, dd = jnp.broadcast_to(inv, (16, 128)), jnp.broadcast_to(dd, (16, 128))
                    for i in range(40):
                        rows = slice(i * 16, i * 16 + 16)
                        p = ex[t, rows, cols] * inv
                        pb[t, rows, cols] = p.astype(BF)
                        gz[t, rows, cols] = (p * (gp[t, rows, cols] - dd) * wt[t, rows, cols]).astype(BF)
                win = slice(t * 128, t * 128 + 640)
                gkv[win, 256:512] += dot(pb[t], gms[t])
                gkv[win, 0:256] += dot(gz[t], q[b, t]) * (1.0 / 16)
                gq[t] = t_dot(gz[t], kv[b, win, 0:256]) * (1.0 / 16)

            @pl.when(seen == 0)
            def _():
                for copy in late:
                    copy.wait()

            dequant_a(b, mine, theirs, lq, lkv)
            co, so = cos[512:768, :], sin[512:768, :]
            for h in range(4):
                cols = slice(h * 256, h * 256 + 256)
                g = unrope(jnp.concatenate([gq[t, h * 128 : h * 128 + 128, :] for t in (0, 1)], axis=0), co, so)
                raw = jnp.concatenate([q[b, t, h * 128 : h * 128 + 128, :] for t in (0, 1)], axis=0)
                raw = unrope(raw.astype(F32), co, so)
                gpar[:, OQ + h * 256 : OQ + h * 256 + 256] += jnp.sum(g * raw, axis=0, keepdims=True)
                g = g * (par[:, OQ + h * 256 : OQ + h * 256 + 256] * U_D)
                gq_sum[:, cols] += g
                gqb[:, cols] = g.astype(BF)
            for w in range(3):
                rows = slice(w * 256, w * 256 + 256)
                cw, sw = cos[rows, :], sin[rows, :]
                for half in range(2):
                    cols = slice(half * 256, half * 256 + 256)
                    g = gkv[rows, cols]
                    raw = kv[b, rows, cols].astype(F32)
                    if half == 0:
                        g, raw = unrope(g, cw, sw), unrope(raw, cw, sw)
                    at = OKV + half * 256
                    gpar[:, at : at + 256] += jnp.sum(g * raw, axis=0, keepdims=True)
                    g = g * (par[:, at : at + 256] * U_D)
                    gkv_sum[rows, cols] += g
                    gkvb[rows, cols] = g.astype(BF)
            gh1[512:768, :] += dot_t(gqb[...], lq[...])
            for k in range(3):
                gh1[k * 256 : k * 256 + 256, :] += dot_t(gkvb[k * 256 : k * 256 + 256, :], lkv[...])

        return seen + run[b]

    lax.fori_loop(0, 3, width, 0)
    gpar[:, OQ : OQ + 1536] = gpar[:, OQ : OQ + 1536] / par[:, OQ : OQ + 1536]

    def put(w, first):
        for half in range(2):
            for j in range(5):
                for p in range(8):
                    to, base = piece(g_mine, g_theirs, p, RA)
                    at = base + (first + half * 5 + j) * 16
                    k = j * 128 + p * 16
                    to[at : at + 16, :] = w[k : k + 16, half * 128 : half * 128 + 128]

    gqb[...] = gq_sum[...].astype(BF)
    gkvb[...] = gkv_sum[...].astype(BF)
    for f in range(4):
        put(t_dot(h1p[512:768, :], gqb[:, f * 256 : f * 256 + 256]).astype(BF), f * 10)
    for f in range(2):
        put(t_dot(h1p[...], gkvb[:, f * 256 : f * 256 + 256]).astype(BF), 40 + f * 10)

    for copy in last:
        copy.wait()
    perm = perm_matrix(dk[...])
    gain_sum = jnp.zeros((1, D), F32)
    for k, to in enumerate((back2, back1, own)):
        g = dot_t(gh1[k * 256 : k * 256 + 256, :].astype(BF), perm)
        v = toks[k].astype(F32)
        r = lax.rsqrt(mean_of(v * v) + EPS)
        gain_sum = gain_sum + jnp.sum(g * v * r, axis=0, keepdims=True)
        to[...] = g.astype(to.dtype)
    gpar[:, ON : ON + D] = gain_sum

    devs = column(dev_row[...])
    sums = jnp.zeros((128, 128), F32)
    row = lax.broadcasted_iota(jnp.int32, (128, 256), 0)
    for i in range(NP // 256):
        cols = slice(i * 256, i * 256 + 256)
        one_hot = (row == lane_of[:, cols]).astype(BF)
        sums = sums + dot_t(jnp.where(devs == dev_of[:, cols], gpar[:, cols], 0.0).astype(BF), one_hot)
    sums = sums.astype(BF)
    for p in range(8):
        to, base = piece(g_mine, g_theirs, p, RA)
        to[base + 960 : base + 976, :] = sums[p * 16 : p * 16 + 16]
        to[base + 976 : base + 1024, :] = jnp.zeros((48, 128), BF)


def end_kernel(own, got1, got2, tok, rest, par, out):
    g = own[...] + got1[...].astype(F32) + got2[...].astype(F32)
    v = tok[...].astype(F32)
    r = lax.rsqrt(mean_of(v * v) + EPS)
    w = par[:, ON : ON + D] * g
    out[...] = rest[...] + r * w - v * (r * r * r * mean_of(w * v))


def run_first(args):
    return call(
        first_kernel,
        [
            sds((1, NP), F32), sds((WIN, D), BF),
            sds((3, 2, 512, HD), BF), sds((3, WIN, 2 * HD), BF), sds((3, TOK, HEADS * HD), BF),
        ],
        args,
        scratch=[
            pltpu.VMEM((D, 1024), BF), pltpu.VMEM((D, 512), BF), pltpu.VMEM((2, 128, 640), F32),
            pltpu.VMEM((2, 512, 640), F32), pltpu.VMEM((2, 512, 640), BF),
        ],
        in_specs=[SMEM] + [VMEM] * 12, name="first", us=20,
    )


def run_middle(args):
    out_shape = [
        sds((3, TOK, D), F32), sds((TOK, D), F32), sds((3, TOK, HEADS * HD), BF),
        *[sds((RB, 128), BF)] * 8, sds((1, NP), F32),
    ]
    any_ = pl.BlockSpec(memory_space=pl.ANY)
    return pl.pallas_call(
        middle_kernel,
        out_shape=out_shape,
        in_specs=[SMEM, SMEM] + [VMEM] * 3 + [any_] * 8 + [VMEM] * 2,
        out_specs=[any_, VMEM, VMEM] + [any_] * 8 + [VMEM],
        scratch_shapes=[
            pltpu.VMEM((8, RB, 128), BF), pltpu.VMEM((D, 2 * FF), BF), pltpu.VMEM((FF, D), BF), pltpu.VMEM((1024, D), BF),
            pltpu.VMEM((1024, D), F32), pltpu.VMEM((2, TOK, 512), F32),
            pltpu.VMEM((TOK, FF), BF), pltpu.VMEM((TOK, FF), BF), pltpu.VMEM((TOK, FF), F32), pltpu.VMEM((TOK, FF), F32),
            pltpu.VMEM((3 * TOK, FF), BF), pltpu.VMEM((3 * TOK, FF), BF), pltpu.VMEM((3 * TOK, FF), BF),
            pltpu.VMEM((3 * TOK, D), BF), pltpu.VMEM((3 * TOK, D), BF), pltpu.VMEM((3 * TOK, D), BF),
            pltpu.VMEM((TOK, D), F32), pltpu.VMEM((TOK, D), F32), pltpu.VMEM((TOK, D), F32),
            pltpu.VMEM((D, D), BF), pltpu.VMEM((3, TOK, D), F32),
            pltpu.SemaphoreType.DMA((3, 8)), pltpu.SemaphoreType.DMA((4, 2, 8)), pltpu.SemaphoreType.DMA((2, 8)),
            pltpu.SemaphoreType.DMA,
        ],
        compiler_params=pltpu.CompilerParams(vmem_limit_bytes=55 << 20),
        cost_estimate=cost_of(70),
        name="middle",
    )(*args)


def run_back(args):
    return call(
        back_kernel,
        [
            sds((TOK, D), F32), sds((TOK, D), BF), sds((TOK, D), BF),
            sds((4 * RA, 128), BF), sds((4 * RA, 128), BF),
        ],
        args,
        scratch=[
            pltpu.VMEM((3, 2, 512, HD), BF), pltpu.VMEM((3, WIN, 512), BF), pltpu.VMEM((3, TOK, 1024), BF),
            pltpu.VMEM((4 * RA, 128), BF), pltpu.VMEM((4 * RA, 128), BF), pltpu.VMEM((WIN, D), BF), pltpu.VMEM((3, TOK, D), BF),
            pltpu.VMEM((2, 640, 128), F32), pltpu.VMEM((2, 640, 512), F32), pltpu.VMEM((2, 640, 512), F32),
            pltpu.VMEM((2, 640, 512), F32), pltpu.VMEM((2, 640, 512), F32),
            pltpu.VMEM((2, 640, 512), BF), pltpu.VMEM((2, 640, 512), BF),
            pltpu.VMEM((2, 512, HD), F32), pltpu.VMEM((WIN, 512), F32),
            pltpu.VMEM((TOK, 1024), F32), pltpu.VMEM((WIN, 512), F32), pltpu.VMEM((TOK, 1024), BF), pltpu.VMEM((WIN, 512), BF),
            pltpu.VMEM((D, 1024), BF), pltpu.VMEM((D, 512), BF), pltpu.VMEM((WIN, D), F32), pltpu.VMEM((1, NP), F32),
            pltpu.SemaphoreType.DMA((3, 3)), pltpu.SemaphoreType.DMA((6,)),
        ],
        in_specs=[SMEM] + [VMEM] * 9 + [pl.BlockSpec(memory_space=pl.ANY)] * 9, mem=46, name="back", us=30,
    )


def per_device(
    tokens, cotangent, segment_ids, width_mask,
    q_codes, kv_codes, o_codes, gate_codes, up_codes, down_codes,
    q_scale, kv_scale, o_scale, gate_scale, up_scale, down_scale, norm_gains,
):
    c, x, y = lax.axis_index("c"), lax.axis_index("x"), lax.axis_index("y")
    zl, zh = lax.axis_index("zl"), lax.axis_index("zh")
    z = zh * 2 + zl
    lane_of, dev_of = lane_tables()

    p, s = jnp.arange(128, dtype=jnp.int32) // 16, jnp.arange(128, dtype=jnp.int32) % 16
    shift = (s % 4, s // 4, p % 4)
    core = jnp.where(p < 4, c, 1 - c)
    sx, sy, sz = (
        (at - jnp.where(core == 0, shift[ORDER[0].index(a)], shift[ORDER[1].index(a)])) % 4 for at, a in ((x, "x"), (y, "y"), (z, "z"))
    )
    inat = ((((sz % 2) * 2 + core) * 2 + sz // 2) * 4 + sy) * 4 + sx
    dk = (5 * inat[None, :] + jnp.arange(5, dtype=jnp.int32)[:, None]).reshape(1, D)
    dev_row = inat[None, :]

    place = (y % 2) * 4 + x
    seq = zh * 2 + y // 2
    segs = lax.dynamic_slice_in_dim(segment_ids, seq, 1, 0)
    run = lax.dynamic_slice_in_dim(width_mask, seq, 1, 0)[0]
    padded = jnp.concatenate([jnp.full((1, WINDOW), -1, jnp.int32), segs], axis=1)
    segk = lax.dynamic_slice_in_dim(padded, place * TOK, WIN, 1)
    pos = (place * TOK - WINDOW + jnp.arange(WIN, dtype=jnp.int32)).astype(F32)
    inverse = 10000.0 ** (-2.0 * jnp.arange(HD // 2).astype(F32) / HD)
    angles = pos[:, None] * inverse[None, :]
    cos, sin = jnp.cos(angles), jnp.sin(angles)

    shard = call(
        pack_kernel, sds((N, 128), BF),
        (q_codes, kv_codes, o_codes, gate_codes, up_codes, down_codes, q_scale, kv_scale, o_scale, gate_scale, up_scale, down_scale, norm_gains.T),
        scratch=[pltpu.VMEM((N, 128), F32)], name="pack", us=0,
    )
    early = (run, inat, dk, dev_row, segk, cos, sin)
    mine_a, theirs_a, mine_b, their_first, t0, t1, early = gather(shard, tokens, early)
    run, inat, dk, dev_row, segk, cos, sin = early

    par, h1p, q, kv, mix = run_first((run, mine_a, theirs_a, dev_row, lane_of, dev_of, t0, t1, tokens, dk, cos, sin, segk))
    mix, *late = lax.optimization_barrier((mix, *mine_b[1:]))
    pieces_b = [mine_b[0], *late, their_first] + [other_core(b) for b in late]
    out, rest, gmix, *g_b, gpar = run_middle((run, inat, mix, tokens, cotangent, *pieces_b, par, dk))
    got_b = {r: other_core(g_b[4 + r]) for r in (2, 1, 3, 0)}
    hop = {r: call(add_kernel, sds((RB, 128), BF), (g_b[r], got_b[r]), name=f"add{r}", mem=24, us=0) for r in (2, 1, 3)}
    gpar, *hops = lax.optimization_barrier((gpar, hop[1], hop[2], hop[3]))
    hops = [send(a, 2, -r) for r, a in zip((1, 2, 3), hops)]
    own, back1, back2, gm_a, gt_a = run_back(
        (run, par, cos, sin, segk, gpar, dk, dev_row, lane_of, dev_of, q, kv, gmix, mine_a, theirs_a, h1p, t0, t1, tokens)
    )
    forth = lambda k: [(j, i) for i, j in behind(k)]
    gt_a, *hops = lax.optimization_barrier((gt_a, *hops))
    got1 = lax.ppermute(back1, ("y", "x"), forth(1))
    got2 = lax.ppermute(back2, ("y", "x"), forth(2))
    parts_a = first_hop(gm_a, other_core(gt_a), RA, 1, 0)
    gq, gkv, gate, up, down, o, *small = scatter(
        parts_a, [g_b[0], got_b[0], *hops],
        [sds((5, 1024), F32), sds((5, 512), F32), sds((5, FF), F32), sds((5, FF), F32), sds((16, D), F32), sds((8, D), F32),
         sds((8,), F32), sds((4,), F32), sds((5,), F32), sds((16,), F32), sds((16,), F32), sds((5,), F32), sds((4, 5), F32)],
    )
    grad_tokens = call(end_kernel, sds((TOK, D), F32), (own, got1, got2, tokens, rest, par), name="end", mem=24, us=0)

    return (out, grad_tokens, gq, gkv, o, gate, up, down, *small[:6], small[6].T)


def solution(mesh):
    fine = Mesh(mesh.devices.reshape(2, 2, 2, 4, 4), AX)
    rows, seqs = P(AX, None), P(("zl", "c"), None)
    wide = P(None, AX, None)
    return jax.shard_map(
        per_device,
        mesh=fine,
        in_specs=(rows, wide, seqs, seqs) + (rows,) * 6 + (P(AX),) * 6 + (rows,),
        out_specs=(wide, rows) + (rows,) * 6 + (P(AX),) * 6 + (rows,),
        check_vma=False,
    )
```

```python
import functools
import itertools
import math

import jax
import jax.numpy as jnp
import numpy as np
from jax import lax
from jax.experimental import pallas as pl
from jax.experimental.pallas import tpu as pltpu
from jax.sharding import Mesh
from jax.sharding import PartitionSpec as P

AX = ("zl", "c", "zh", "y", "x")
F32 = jnp.float32
BF = jnp.bfloat16
EPS = 1e-6
D, HEADS, HD, FF, WINDOW = 640, 4, 256, 2048, 512
TOK = 256
WIN = 768
ORDER = (("x", "y", "z"), ("y", "z", "x"))
NA = 64
NB = 288
N = NA + NB
INT_A, INT_B = 64, 160
RA, RB = 16 * NA, 16 * NB
DOWN_ROW, O_ROW = 2560, 3840
NP = 9472
SEG = dict(q=(0, 1024, 8, 0), kv=(1024, 512, 4, 8), o=(1536, 640, 5, 12), gate=(2176, 2048, 16, 17),
           up=(4224, 2048, 16, 33), down=(6272, 640, 5, 49))
OQ, OKV, OO, OG, OU, OD, ON = 0, 1024, 1536, 2176, 4224, 6272, 6912
U_D = 1.0 / (128.0 * math.sqrt(D))
U_O = 1.0 / (128.0 * math.sqrt(HEADS * HD))
U_F = 1.0 / (128.0 * math.sqrt(FF))
VMEM = pl.BlockSpec(memory_space=pltpu.VMEM)
SMEM = pl.BlockSpec(memory_space=pltpu.SMEM)


def lane_tables():
    lane, dev = np.zeros((1, NP), np.int32), np.zeros((1, NP), np.int32)
    for at, size, each, first in SEG.values():
        c = np.arange(size)
        lane[0, at : at + size] = first + c % each
        dev[0, at : at + size] = c // each
    for g in range(4):
        c = np.arange(D)
        at = ON + g * D
        lane[0, at : at + D] = 54 + g * 5 + c % 5
        dev[0, at : at + D] = c // 5
    return lane, dev


def cost_of(us):
    return pl.CostEstimate(flops=int(us * 1e6) + 1000, bytes_accessed=1000, transcendentals=0)


def call(kernel, out_shape, ins, scratch=(), mem=62, us=1, in_specs=None, name=None):
    params = dict(vmem_limit_bytes=mem << 20)
    return pl.pallas_call(
        kernel,
        out_shape=out_shape,
        in_specs=in_specs or [VMEM] * len(ins),
        out_specs=jax.tree.map(lambda s: VMEM, out_shape),
        scratch_shapes=list(scratch),
        compiler_params=pltpu.CompilerParams(**params),
        cost_estimate=cost_of(us),
        name=name,
    )(*ins)


def sds(shape, dtype):
    return jax.ShapeDtypeStruct(shape, dtype)


def dot(a, b):
    return jnp.dot(a, b, preferred_element_type=F32)


def dot_t(a, b):
    return lax.dot_general(a, b, (((1,), (1,)), ((), ())), preferred_element_type=F32)


def t_dot(a, b):
    return lax.dot_general(a, b, (((0,), (0,)), ((), ())), preferred_element_type=F32)


def flat(c, x, y, z):
    return ((((z & 1) * 2 + c) * 2 + (z >> 1)) * 4 + y) * 4 + x


@functools.lru_cache(None)
def stage_pairs(stage, r):
    pairs = []
    for c, x, y, z in itertools.product(range(2), range(4), range(4), range(4)):
        at = dict(x=x, y=y, z=z)
        axis = ORDER[c][stage]
        at[axis] = (at[axis] + r) % 4
        pairs.append((flat(c, x, y, z), flat(c, **at)))
    return tuple(sorted(pairs))


def send(a, stage, r):
    return lax.ppermute(a, AX, stage_pairs(stage, r % 4))


def behind(k):
    return [(i, i + k) for i in range(16) if i % 8 + k < 8]


def other_core(a):
    return lax.ppermute(a, "c", [(0, 1), (1, 0)])


def swap_matrix():
    row = lax.broadcasted_iota(jnp.int32, (256, 256), 0)
    col = lax.broadcasted_iota(jnp.int32, (256, 256), 1)
    return ((row % 16) * 16 + row // 16 == col).astype(BF)


BLOCKS = ((224, 80, DOWN_ROW), (304, 48, O_ROW))


def asm_kernel(*refs):
    ins, out_a, out_b = refs[:4], refs[4], refs[5]
    swap = swap_matrix()
    for g in range((INT_A + INT_B) // 16):
        x = jnp.concatenate(
            [ins[s // 4][(s % 4) * N + 16 * g : (s % 4) * N + 16 * g + 16, :] for s in range(16)], axis=0
        )
        y = dot(swap, x).astype(BF)
        if g < 4:
            out_a[256 * g : 256 * g + 256, :] = y
        else:
            out_b[256 * (g - 4) : 256 * (g - 4) + 256, :] = y
    for first, lines, row in BLOCKS:
        for s in range(16):
            at = (s % 4) * N + first
            out_b[row + s * lines : row + (s + 1) * lines, :] = ins[s // 4][at : at + lines, :]


def join_kernel(a, b, c, d, out):
    for r, ref in enumerate((a, b, c, d)):
        out[r * RA : (r + 1) * RA, :] = ref[...]


def gather(shard, tokens, early):
    one = jnp.concatenate([shard] + [send(shard, 0, r) for r in (1, 2, 3)], axis=0)
    t1, t0 = (lax.ppermute(tokens, ("y", "x"), behind(k)) for k in (1, 2))
    two = [one] + [send(one, 1, r) for r in (1, 2, 3)]
    two[0], t0, t1, *early = lax.optimization_barrier((two[0], t0, t1, *early))
    piece_a, piece_b = call(asm_kernel, [sds((RA, 128), BF), sds((RB, 128), BF)], two, name="asm", mem=24, us=0)
    mine_a = [piece_a] + [send(piece_a, 2, r) for r in (1, 2, 3)]
    mine_a = call(join_kernel, sds((4 * RA, 128), BF), mine_a, name="join", mem=24, us=0)
    theirs_a = other_core(mine_a)
    mine_b = [piece_b] + [send(piece_b, 2, r) for r in (1, 2, 3)]
    return mine_a, theirs_a, mine_b, other_core(piece_b), t0, t1, early


def rs1_kernel(a, b, *outs):
    for r in range(4):
        outs[r][...] = (a[r].astype(F32) + b[r].astype(F32)).astype(BF)


def total4(refs, at, rows):
    t = refs[0][at : at + rows, :].astype(F32)
    for ref in refs[1:]:
        t = t + ref[at : at + rows, :].astype(F32)
    return t


def add_kernel(a, b, out):
    out[...] = (a[...].astype(F32) + b[...].astype(F32)).astype(BF)


def rs2_kernel(*refs):
    a, b, outs = refs[:4], refs[4:9], refs[9:]
    swap = swap_matrix()
    for g in range((INT_A + INT_B) // 16):
        t = total4(a, 256 * g, 256) if g < 4 else total4(b, 256 * (g - 4), 256)
        y = dot(swap, t.astype(BF)).astype(BF)
        for s in range(16):
            at = (s % 4) * N + 16 * g
            outs[s // 4][at : at + 16, :] = y[16 * s : 16 * s + 16]
    for first, lines, row in BLOCKS:
        for s in range(16):
            at = (s % 4) * N + first
            outs[s // 4][at : at + lines, :] = total4(b, row + s * lines, lines).astype(BF)


def rs3_kernel(*refs):
    ins, outs = refs[:4], refs[4:]
    for r in range(4):
        outs[r][...] = total4(ins, r * N, N).astype(BF)


def rs4_kernel(a0, a1, a2, a3, q, kv, gate, up, down, o, *small):
    t = total4((a0, a1, a2, a3), 0, N)
    for cb in range(8):
        q[:, cb * 128 : cb * 128 + 128] = t[cb * 5 : cb * 5 + 5]
    for cb in range(4):
        kv[:, cb * 128 : cb * 128 + 128] = t[40 + cb * 5 : 45 + cb * 5]
    at = 0
    for ref in small[:6]:
        ref[...] = t[60, at : at + ref.shape[0]]
        at += ref.shape[0]
    for g in range(4):
        small[6][g : g + 1, :] = t[60:61, at + 5 * g : at + 5 * g + 5]
    for cb in range(16):
        gate[:, cb * 128 : cb * 128 + 128] = t[64 + cb * 5 : 69 + cb * 5]
        up[:, cb * 128 : cb * 128 + 128] = t[144 + cb * 5 : 149 + cb * 5]
    for cb in range(5):
        down[:, cb * 128 : cb * 128 + 128] = t[224 + cb * 16 : 240 + cb * 16]
        o[:, cb * 128 : cb * 128 + 128] = t[304 + cb * 8 : 312 + cb * 8]


def first_hop(mine, got, rows, grid, us):
    block = rows // grid
    parts = pl.pallas_call(
        rs1_kernel,
        grid=(grid,),
        out_shape=[sds((rows, 128), BF)] * 4,
        in_specs=[pl.BlockSpec((4, block, 128), lambda i: (0, i, 0))] * 2,
        out_specs=[pl.BlockSpec((block, 128), lambda i: (i, 0))] * 4,
        compiler_params=pltpu.CompilerParams(vmem_limit_bytes=24 << 20),
        cost_estimate=cost_of(us),
        name=f"rs1_{rows}",
    )(mine.reshape(4, rows, 128), got.reshape(4, rows, 128))
    return [parts[0]] + [send(parts[r], 2, -r) for r in (1, 2, 3)]


def scatter(a, b, out_shape):
    parts = call(rs2_kernel, [sds((4 * N, 128), BF)] * 4, a + b, name="rs2", mem=24, us=0)
    parts = [parts[0]] + [send(parts[r], 1, -r) for r in (1, 2, 3)]
    parts = call(rs3_kernel, [sds((N, 128), BF)] * 4, parts, name="rs3", mem=24, us=0)
    parts = [parts[0]] + [send(parts[r], 0, -r) for r in (1, 2, 3)]
    return call(rs4_kernel, out_shape, parts, name="rs4", mem=24, us=0)


def pack_kernel(q, kv, o, gate, up, down, sq, skv, so, sg, su, sd, gains, out, wide):
    for cb in range(8):
        wide[cb * 5 : cb * 5 + 5, :] = q[:, cb * 128 : cb * 128 + 128].astype(F32)
    for cb in range(4):
        wide[40 + cb * 5 : 45 + cb * 5, :] = kv[:, cb * 128 : cb * 128 + 128].astype(F32)
    row = [ref[...].reshape(1, -1) for ref in (sq, skv, so, sg, su, sd)] + [gains[g : g + 1, :] for g in range(4)]
    v = jnp.concatenate(row + [jnp.zeros((1, 54), F32)], axis=1)
    hi = v.astype(BF).astype(F32)
    mid = (v - hi).astype(BF).astype(F32)
    wide[60:61, :] = hi
    wide[61:62, :] = mid
    wide[62:63, :] = v - hi - mid
    wide[63:64, :] = jnp.zeros((1, 128), F32)
    for cb in range(16):
        wide[64 + cb * 5 : 69 + cb * 5, :] = gate[:, cb * 128 : cb * 128 + 128].astype(F32)
        wide[144 + cb * 5 : 149 + cb * 5, :] = up[:, cb * 128 : cb * 128 + 128].astype(F32)
    for cb in range(5):
        wide[224 + cb * 16 : 240 + cb * 16, :] = down[:, cb * 128 : cb * 128 + 128].astype(F32)
        wide[304 + cb * 8 : 312 + cb * 8, :] = o[:, cb * 128 : cb * 128 + 128].astype(F32)
    wide[344:352, :] = jnp.zeros((8, 128), F32)
    out[...] = wide[...].astype(BF)


def piece(mine, theirs, p, rows):
    return (mine if p < 4 else theirs), (p % 4) * rows


def perm_matrix(dk):
    return (lax.broadcasted_iota(jnp.int32, (D, D), 0) == dk).astype(BF)


def steps_of(b):
    step = jnp.where(b == 0, 1.0, jnp.where(b == 1, 16.0, 64.0)).astype(F32)
    inv = jnp.where(b == 0, 1.0, jnp.where(b == 1, 1.0 / 16, 1.0 / 64)).astype(F32)
    return step, inv


def level_maker(b, rows=16, dtype=BF):
    step, inv = steps_of(b)
    step_v = jnp.full((rows, 128), step, F32)
    inv_v = jnp.full((rows, 128), inv, F32).astype(dtype)
    half_v = (step_v * 0.5).astype(dtype)
    step_v = step_v.astype(dtype)
    return lambda c: jnp.floor(c * inv_v) * step_v + half_v


def dequant_a(b, mine, theirs, lq, lkv):
    level = level_maker(b)
    for p in range(8):
        ref, base = piece(mine, theirs, p, RA)
        for j in range(5):
            for cb in range(8):
                at = base + (cb * 5 + j) * 16
                lq[j * 128 + p * 16 : j * 128 + p * 16 + 16, cb * 128 : cb * 128 + 128] = level(ref[at : at + 16, :])
            for cb in range(4):
                at = base + (40 + cb * 5 + j) * 16
                lkv[j * 128 + p * 16 : j * 128 + p * 16 + 16, cb * 128 : cb * 128 + 128] = level(ref[at : at + 16, :])


def column(row):
    n = row.shape[1]
    eye = lax.broadcasted_iota(jnp.int32, (n, n), 0) == lax.broadcasted_iota(jnp.int32, (n, n), 1)
    return jnp.sum(jnp.where(eye, row.astype(F32), 0.0), axis=1, keepdims=True).astype(jnp.int32)


def make_mask(segk, mask):
    for t in range(2):
        mine = column(segk[:, WINDOW + t * 128 : WINDOW + t * 128 + 128])
        r = lax.broadcasted_iota(jnp.int32, (128, 640), 0)
        c = lax.broadcasted_iota(jnp.int32, (128, 640), 1)
        ok = (c <= WINDOW + r) & (c > r)
        ok = ok & (mine == segk[:, t * 128 : t * 128 + 640])
        mask[t] = ok.astype(F32)


def rope(v, cos, sin):
    a, b = v[:, :128], v[:, 128:]
    return jnp.concatenate([a * cos - b * sin, b * cos + a * sin], axis=1)


def unrope(v, cos, sin):
    a, b = v[:, :128], v[:, 128:]
    return jnp.concatenate([a * cos + b * sin, b * cos - a * sin], axis=1)


TANH_IN = 1.0 / (16.0 * 50.0)
EXP2_IN = 50.0 * math.log2(math.e)


def first_kernel(
    run, mine, theirs, dev_row, lane_of, dev_of, t0, t1, t2, dk, cos, sin, segk,
    par, h1p, q_out, kv_out, mix_out, lq, lkv, mask, sc, ex,
):
    lines = []
    for l in (60, 61, 62):
        refs = [piece(mine, theirs, p, RA) for p in range(8)]
        lines.append(jnp.concatenate([ref[at + l * 16 : at + l * 16 + 16, :] for ref, at in refs], axis=0))
    lines = jnp.concatenate(lines, axis=1)
    devs = column(dev_row[...])
    row = lax.broadcasted_iota(jnp.int32, (128, 256), 0)
    for i in range(NP // 256):
        cols = slice(i * 256, i * 256 + 256)
        one_hot = (row == lane_of[:, cols]).astype(BF)
        t = dot(lines, jnp.concatenate([one_hot] * 3, axis=0))
        t = jnp.where(devs == dev_of[:, cols], t, 0.0)
        par[:, cols] = jnp.sum(t, axis=0, keepdims=True)
    perm = perm_matrix(dk[...])
    gain = par[:, ON : ON + D]
    for k, t in enumerate((t0, t1, t2)):
        v = t[...].astype(F32)
        h = v * lax.rsqrt(jnp.mean(v * v, axis=-1, keepdims=True) + EPS) * gain
        h1p[k * 256 : k * 256 + 256, :] = dot(h.astype(BF), perm).astype(BF)
    make_mask(segk, mask)

    def width(b, carry):
        @pl.when(run[b] == 0)
        def _():
            mix_out[b] = jnp.zeros((TOK, HEADS * HD), BF)

        @pl.when(run[b] > 0)
        def _():
            dequant_a(b, mine, theirs, lq, lkv)
            own = h1p[512:768, :]
            co, so = cos[512:768, :], sin[512:768, :]
            for h in range(4):
                scale = par[:, OQ + h * 256 : OQ + h * 256 + 256] * U_D
                q = rope(dot(own, lq[:, h * 256 : h * 256 + 256]) * scale, co, so).astype(BF)
                for t in range(2):
                    q_out[b, t, h * 128 : h * 128 + 128, :] = q[t * 128 : t * 128 + 128]
            for k in range(3):
                rows = h1p[k * 256 : k * 256 + 256, :]
                cw, sw = cos[k * 256 : k * 256 + 256, :], sin[k * 256 : k * 256 + 256, :]
                key = dot(rows, lkv[:, :256]) * (par[:, OKV : OKV + 256] * U_D)
                kv_out[b, k * 256 : k * 256 + 256, 0:256] = rope(key, cw, sw).astype(BF)
                val = dot(rows, lkv[:, 256:]) * (par[:, OKV + 256 : OKV + 512] * U_D)
                kv_out[b, k * 256 : k * 256 + 256, 256:512] = val.astype(BF)
            ones = jnp.ones((640, 128), BF)
            for t in range(2):
                sc[t] = dot_t(q_out[b, t], kv_out[b, t * 128 : t * 128 + 640, 0:256])
            for t in range(2):
                for i in range(16):
                    rows = slice(i * 32, i * 32 + 32)
                    m = mask[t, (i % 4) * 32 : (i % 4) * 32 + 32, :]
                    ex[t, rows, :] = (jnp.exp2(jnp.tanh(sc[t, rows, :] * TANH_IN) * EXP2_IN) * m).astype(BF)
                e = ex[t]
                inv = 1.0 / dot(e, ones)
                mixed = dot(e, kv_out[b, t * 128 : t * 128 + 640, 256:512]) * jnp.concatenate([inv, inv], axis=1)
                for h in range(4):
                    mix_out[b, t * 128 : t * 128 + 128, h * 256 : h * 256 + 256] = mixed[h * 128 : h * 128 + 128].astype(BF)

        return carry

    lax.fori_loop(0, 3, width, 0)


def mean_of(v):
    return jnp.mean(v, axis=-1, keepdims=True)


C_G = math.sqrt(2.0 / math.pi)
C_3 = C_G * 0.044715
PARTS = ((O_ROW, 768), (0, 2560), (DOWN_ROW, 1280))


def middle_kernel(
    run, inat, mix, tok, cot, b0, b1, b2, b3, b4, b5, b6, b7, par, dk,
    out, rest, gmix, g0, g1_, g2_, g3_, g4, g5, g6, g7, gpar,
    pcs, lgu, ld, lo, onat, gu32, gate, up, aa, bb, hid, gg, gu, h2s, gbr, gat, att, mid, acc, perm, outv,
    in_sem, gu_sem, do_sem, out_sem,
):
    dwd, dwo = ld, onat
    loads = [
        [
            pltpu.make_async_copy(ref.at[pl.ds(first, rows)], pcs.at[p, pl.ds(first, rows)], in_sem.at[k, p])
            for p, ref in enumerate((b0, b1, b2, b3, b4, b5, b6, b7))
        ]
        for k, (first, rows) in enumerate(PARTS)
    ]
    for group in loads:
        for copy in group:
            copy.start()
    perm[...] = perm_matrix(dk[...])
    rest[...] = jnp.zeros_like(rest)
    gpar[...] = jnp.zeros_like(gpar)
    for copy in loads[0]:
        copy.wait()
    for p in range(8):
        for s in range(16):
            at = O_ROW + s * 48
            block = pcs[p, at : at + 48, :].astype(F32)
            row = pl.multiple_of(inat[p * 16 + s] * 8, 8)
            for cb in range(5):
                onat[pl.ds(row, 8), cb * 128 : cb * 128 + 128] = block[cb * 8 : cb * 8 + 8]
    def width(b, carry):
        rows = pl.ds(pl.multiple_of(b * TOK, TOK), TOK)

        @pl.when(run[b] == 0)
        def _():
            outv[b] = jnp.zeros((TOK, D), F32)
            hid[rows, :] = jnp.zeros((TOK, FF), BF)
            gg[rows, :] = jnp.zeros((TOK, FF), BF)
            gu[rows, :] = jnp.zeros((TOK, FF), BF)
            h2s[rows, :] = jnp.zeros((TOK, D), BF)
            gbr[rows, :] = jnp.zeros((TOK, D), BF)
            gat[rows, :] = jnp.zeros((TOK, D), BF)

        @pl.when(run[b] > 0)
        def _():
            level = level_maker(b)
            wide = level_maker(b, 8, F32)
            for r in range(64):
                for cb in range(5):
                    two = [wide(onat[r * 16 + k * 8 : r * 16 + k * 8 + 8, cb * 128 : cb * 128 + 128]) for k in (0, 1)]
                    lo[r * 16 : r * 16 + 16, cb * 128 : cb * 128 + 128] = jnp.concatenate(two, axis=0).astype(BF)
            s_o = par[:, OO : OO + D] * U_O
            s_d = par[:, OD : OD + D] * U_F
            g1, g2, g3 = (par[:, ON + k * D : ON + (k + 1) * D] for k in (1, 2, 3))
            attended = dot(mix[b], lo[...]) * s_o
            att[...] = attended
            r1 = lax.rsqrt(mean_of(attended * attended) + EPS)
            middle = tok[...].astype(F32) + attended * r1 * g1
            mid[...] = middle
            r2 = lax.rsqrt(mean_of(middle * middle) + EPS)
            h2 = (middle * r2 * g2).astype(BF)
            h2p = dot(h2, perm[...]).astype(BF)
            h2s[rows, :] = h2p

            @pl.when(carry == 0)
            def _():
                for copy in loads[1] + loads[2]:
                    copy.wait()

            def gate_up(f):
                for half in range(2):
                    cb = f * 2 + half
                    for first, to in ((0, f * 512), (80, f * 512 + 256)):
                        for j in range(5):
                            for p in range(8):
                                at = (first + cb * 5 + j) * 16
                                k = j * 128 + p * 16
                                col = to + half * 128
                                lgu[k : k + 16, col : col + 128] = level(pcs[p, at : at + 16, :])
                gu32[f % 2] = dot(h2p, lgu[:, f * 512 : f * 512 + 512])

            gate_up(0)
            for p in range(8):
                for s in range(16):
                    row = pl.multiple_of(inat[p * 16 + s] * 16, 16)
                    for cb in range(5):
                        at = DOWN_ROW + s * 80 + cb * 16
                        ld[pl.ds(row, 16), cb * 128 : cb * 128 + 128] = level(pcs[p, at : at + 16, :])
            for f in range(8):
                if f < 7:
                    gate_up(f + 1)
                cols = slice(f * 256, f * 256 + 256)
                s_g, s_u = par[:, OG + f * 256 : OG + f * 256 + 256] * U_D, par[:, OU + f * 256 : OU + f * 256 + 256] * U_D
                parts = []
                for rc in range(8):
                    rr = slice(rc * 32, rc * 32 + 32)
                    x = gu32[f % 2, rr, 0:256] * s_g
                    u = gu32[f % 2, rr, 256:512] * s_u
                    gate[rr, cols] = x.astype(BF)
                    up[rr, cols] = u.astype(BF)
                    x2 = x * x
                    hf = 0.5 * jnp.tanh(x * (C_G + C_3 * x2)) + 0.5
                    gl = x * hf
                    aa[rr, cols] = u * (hf + (gl - gl * hf) * (2 * C_G + (6 * C_3) * x2))
                    bb[rr, cols] = gl
                    parts.append((gl * u).astype(BF))
                h = jnp.concatenate(parts, axis=0)
                hid[rows, cols] = h
                add = dot(h, ld[cols, :])
                acc[...] = add if f == 0 else acc[...] + add
            branch = acc[...] * s_d
            r3 = lax.rsqrt(mean_of(branch * branch) + EPS)
            outv[b] = mid[...] + branch * r3 * g3
            gy = cot[b].astype(F32)
            gpar[:, ON + 3 * D : ON + 4 * D] += jnp.sum(gy * branch * r3, axis=0, keepdims=True)
            w = g3 * gy
            gb = r3 * w - branch * (r3 * r3 * r3 * mean_of(w * branch))
            gpar[:, OD : OD + D] += jnp.sum(gb * branch, axis=0, keepdims=True)
            gb = (gb * s_d).astype(BF)
            gbr[rows, :] = gb

            def grad_hidden(f):
                gu32[f % 2, :, 0:256] = dot_t(gb, ld[f * 256 : f * 256 + 256, :])

            ones = jnp.ones((8, TOK), BF)
            grad_hidden(0)
            for f in range(8):
                if f < 7:
                    grad_hidden(f + 1)
                cols = slice(f * 256, f * 256 + 256)
                col_g, col_u = slice(OG + f * 256, OG + f * 256 + 256), slice(OU + f * 256, OU + f * 256 + 256)
                s_g, s_u = par[:, col_g] * U_D, par[:, col_u] * U_D
                parts, prods = [], []
                for rc in range(8):
                    rr = slice(rc * 32, rc * 32 + 32)
                    g = gu32[f % 2, rr, 0:256]
                    gg_b = (g * aa[rr, cols] * s_g).astype(BF)
                    gu_b = (g * bb[rr, cols] * s_u).astype(BF)
                    parts.append(jnp.concatenate([gg_b, gu_b], axis=1))
                    prods.append(jnp.concatenate([gg_b * gate[rr, cols], gu_b * up[rr, cols]], axis=1))
                both = jnp.concatenate(parts, axis=0)
                gg[rows, cols] = both[:, 0:256]
                gu[rows, cols] = both[:, 256:512]
                sums = dot(ones, jnp.concatenate(prods, axis=0))
                gpar[:, col_g] += sums[0:1, 0:256]
                gpar[:, col_u] += sums[0:1, 256:512]
                add = dot_t(both, lgu[:, f * 512 : f * 512 + 512])
                acc[...] = add if f == 0 else acc[...] + add
            g_h2 = dot_t(acc[...].astype(BF), perm[...])
            middle = mid[...]
            attended = att[...]
            gpar[:, ON + 2 * D : ON + 3 * D] += jnp.sum(g_h2 * middle * r2, axis=0, keepdims=True)
            w = g2 * g_h2
            gmid = cot[b].astype(F32) + r2 * w - middle * (r2 * r2 * r2 * mean_of(w * middle))
            rest[...] += gmid
            gpar[:, ON + D : ON + 2 * D] += jnp.sum(gmid * attended * r1, axis=0, keepdims=True)
            w = g1 * gmid
            ga = r1 * w - attended * (r1 * r1 * r1 * mean_of(w * attended))
            gpar[:, OO : OO + D] += jnp.sum(ga * attended, axis=0, keepdims=True)
            ga = (ga * s_o).astype(BF)
            gat[rows, :] = ga
            gmix[b] = dot_t(ga, lo[...]).astype(BF)

        return carry + run[b]

    lax.fori_loop(0, 3, width, 0)
    out_copy = pltpu.make_async_copy(outv, out, out_sem)
    out_copy.start()
    gpar[:, OO : OO + D] = gpar[:, OO : OO + D] / par[:, OO : OO + D]
    for at in (OG, OU):
        scale = par[:, at : at + FF]
        gpar[:, at : at + FF] = gpar[:, at : at + FF] / (scale * scale * U_D)
    gpar[:, OD : OD + D] = gpar[:, OD : OD + D] / par[:, OD : OD + D]

    stores = []

    def leave(p, first, rows, sem):
        to = (g0, g1_, g2_, g3_, g4, g5, g6, g7)[p]
        copy = pltpu.make_async_copy(pcs.at[p, pl.ds(first, rows)], to.at[pl.ds(first, rows)], sem)
        copy.start()
        stores.append(copy)

    g_all = gbr[...]
    for f in range(8):
        cols = slice(f * 256, f * 256 + 256)
        dwd[cols, :] = t_dot(hid[:, cols], g_all).astype(BF)
    for p in range(8):
        for s in range(16):
            row = pl.multiple_of(inat[p * 16 + s] * 16, 16)
            for cb in range(5):
                at = DOWN_ROW + s * 80 + cb * 16
                pcs[p, at : at + 16, :] = dwd[pl.ds(row, 16), cb * 128 : cb * 128 + 128]
        leave(p, DOWN_ROW, 1280, do_sem.at[0, p])
    for h in range(4):
        w = jnp.zeros((256, D), F32)
        for b in range(3):
            w = w + t_dot(mix[b, :, h * 256 : h * 256 + 256], gat[b * TOK : (b + 1) * TOK, :])
        dwo[h * 256 : h * 256 + 256, :] = w
    for p in range(8):
        for s in range(16):
            row = pl.multiple_of(inat[p * 16 + s] * 8, 8)
            parts = [dwo[pl.ds(row, 8), cb * 128 : cb * 128 + 128] for cb in range(5)] + [jnp.zeros((8, 128), F32)]
            at = O_ROW + s * 48
            pcs[p, at : at + 48, :] = jnp.concatenate(parts, axis=0).astype(BF)
        leave(p, O_ROW, 768, do_sem.at[1, p])
    h2t = h2s[...]
    for f in range(8):
        cols = slice(f * 256, f * 256 + 256)
        for k, (first, ref) in enumerate(((0, gg), (80, gu))):
            w = t_dot(h2t, ref[:, cols]).astype(BF)
            for half in range(2):
                for j in range(5):
                    for p in range(8):
                        at = (first + (f * 2 + half) * 5 + j) * 16
                        r = j * 128 + p * 16
                        pcs[p, at : at + 16, :] = w[r : r + 16, half * 128 : half * 128 + 128]
            if f % 2:
                for p in range(8):
                    leave(p, (first + (f - 1) * 10) * 16, 320, gu_sem.at[f // 2, k, p])
    for copy in stores:
        copy.wait()
    out_copy.wait()


def back_kernel(
    run, par, cos, sin, segk, gpar_in, dk, dev_row, lane_of, dev_of,
    q_far, kv_far, gmix_far, mine_far, theirs_far, h1p_far, t0_far, t1_far, t2_far,
    own, back1, back2, g_mine, g_theirs,
    q, kv, gmix, mine, theirs, h1p, toks, mask, sc, gp, ex, wt, pb, gz, gq, gkv, gq_sum, gkv_sum, gqb, gkvb, lq, lkv, gh1, gpar,
    sem, sem_late,
):
    loads = [
        [pltpu.make_async_copy(far.at[b], near.at[b], sem.at[b, k]) for k, (far, near) in enumerate(((q_far, q), (kv_far, kv), (gmix_far, gmix)))]
        for b in range(3)
    ]
    late = [
        pltpu.make_async_copy(far, near, sem_late.at[k])
        for k, (far, near) in enumerate(((mine_far, mine), (theirs_far, theirs), (h1p_far, h1p)))
    ]
    last = [pltpu.make_async_copy(far, toks.at[k], sem_late.at[3 + k]) for k, far in enumerate((t0_far, t1_far, t2_far))]
    for copy in loads[0] + late + loads[1] + loads[2] + last:
        copy.start()
    for t in range(2):
        k = lax.broadcasted_iota(jnp.int32, (640, 128), 0)
        r = lax.broadcasted_iota(jnp.int32, (640, 128), 1)
        ok = (k <= WINDOW + r) & (k > r)
        keys = jnp.concatenate([column(segk[:, (t + i) * 128 : (t + i + 1) * 128]) for i in range(5)], axis=0)
        ok = ok & (keys == segk[:, WINDOW + t * 128 : WINDOW + t * 128 + 128])
        mask[t] = ok.astype(F32)
    gpar[...] = gpar_in[...]
    gh1[...] = jnp.zeros_like(gh1)
    gq_sum[...] = jnp.zeros_like(gq_sum)
    gkv_sum[...] = jnp.zeros_like(gkv_sum)

    def width(b, seen):
        for k, (far, near) in enumerate(((q_far, q), (kv_far, kv), (gmix_far, gmix))):
            pltpu.make_async_copy(far.at[b], near.at[b], sem.at[b, k]).wait()

        @pl.when(run[b] > 0)
        def _():
            gkv[...] = jnp.zeros_like(gkv)
            gms = []
            for t in range(2):
                gm = jnp.concatenate(
                    [gmix[b, t * 128 : t * 128 + 128, h * 256 : h * 256 + 256] for h in range(4)], axis=0
                )
                gms.append(gm)
                sc[t] = dot_t(kv[b, t * 128 : t * 128 + 640, 0:256], q[b, t])
                gp[t] = dot_t(kv[b, t * 128 : t * 128 + 640, 256:512], gm)
            for t in range(2):
                for h in range(4):
                    cols = slice(h * 128, h * 128 + 128)
                    total, dot_sum = jnp.zeros((16, 128), F32), jnp.zeros((16, 128), F32)
                    for i in range(40):
                        rows = slice(i * 16, i * 16 + 16)
                        th = jnp.tanh(sc[t, rows, cols] * TANH_IN)
                        e = jnp.exp2(th * EXP2_IN) * mask[t, rows, :]
                        ex[t, rows, cols] = e
                        wt[t, rows, cols] = 1.0 - th * th
                        total = total + e
                        dot_sum = dot_sum + e * gp[t, rows, cols]
                    inv = 1.0 / jnp.sum(total, axis=0, keepdims=True)
                    dd = jnp.sum(dot_sum, axis=0, keepdims=True) * inv
                    inv, dd = jnp.broadcast_to(inv, (16, 128)), jnp.broadcast_to(dd, (16, 128))
                    for i in range(40):
                        rows = slice(i * 16, i * 16 + 16)
                        p = ex[t, rows, cols] * inv
                        pb[t, rows, cols] = p.astype(BF)
                        gz[t, rows, cols] = (p * (gp[t, rows, cols] - dd) * wt[t, rows, cols]).astype(BF)
                win = slice(t * 128, t * 128 + 640)
                gkv[win, 256:512] += dot(pb[t], gms[t])
                gkv[win, 0:256] += dot(gz[t], q[b, t]) * (1.0 / 16)
                gq[t] = t_dot(gz[t], kv[b, win, 0:256]) * (1.0 / 16)

            @pl.when(seen == 0)
            def _():
                for copy in late:
                    copy.wait()

            dequant_a(b, mine, theirs, lq, lkv)
            co, so = cos[512:768, :], sin[512:768, :]
            for h in range(4):
                cols = slice(h * 256, h * 256 + 256)
                g = unrope(jnp.concatenate([gq[t, h * 128 : h * 128 + 128, :] for t in (0, 1)], axis=0), co, so)
                raw = jnp.concatenate([q[b, t, h * 128 : h * 128 + 128, :] for t in (0, 1)], axis=0)
                raw = unrope(raw.astype(F32), co, so)
                gpar[:, OQ + h * 256 : OQ + h * 256 + 256] += jnp.sum(g * raw, axis=0, keepdims=True)
                g = g * (par[:, OQ + h * 256 : OQ + h * 256 + 256] * U_D)
                gq_sum[:, cols] += g
                gqb[:, cols] = g.astype(BF)
            for w in range(3):
                rows = slice(w * 256, w * 256 + 256)
                cw, sw = cos[rows, :], sin[rows, :]
                for half in range(2):
                    cols = slice(half * 256, half * 256 + 256)
                    g = gkv[rows, cols]
                    raw = kv[b, rows, cols].astype(F32)
                    if half == 0:
                        g, raw = unrope(g, cw, sw), unrope(raw, cw, sw)
                    at = OKV + half * 256
                    gpar[:, at : at + 256] += jnp.sum(g * raw, axis=0, keepdims=True)
                    g = g * (par[:, at : at + 256] * U_D)
                    gkv_sum[rows, cols] += g
                    gkvb[rows, cols] = g.astype(BF)
            gh1[512:768, :] += dot_t(gqb[...], lq[...])
            for k in range(3):
                gh1[k * 256 : k * 256 + 256, :] += dot_t(gkvb[k * 256 : k * 256 + 256, :], lkv[...])

        return seen + run[b]

    lax.fori_loop(0, 3, width, 0)
    gpar[:, OQ : OQ + 1536] = gpar[:, OQ : OQ + 1536] / par[:, OQ : OQ + 1536]

    def put(w, first):
        for half in range(2):
            for j in range(5):
                for p in range(8):
                    to, base = piece(g_mine, g_theirs, p, RA)
                    at = base + (first + half * 5 + j) * 16
                    k = j * 128 + p * 16
                    to[at : at + 16, :] = w[k : k + 16, half * 128 : half * 128 + 128]

    gqb[...] = gq_sum[...].astype(BF)
    gkvb[...] = gkv_sum[...].astype(BF)
    for f in range(4):
        put(t_dot(h1p[512:768, :], gqb[:, f * 256 : f * 256 + 256]).astype(BF), f * 10)
    for f in range(2):
        put(t_dot(h1p[...], gkvb[:, f * 256 : f * 256 + 256]).astype(BF), 40 + f * 10)

    for copy in last:
        copy.wait()
    perm = perm_matrix(dk[...])
    gain_sum = jnp.zeros((1, D), F32)
    for k, to in enumerate((back2, back1, own)):
        g = dot_t(gh1[k * 256 : k * 256 + 256, :].astype(BF), perm)
        v = toks[k].astype(F32)
        r = lax.rsqrt(mean_of(v * v) + EPS)
        gain_sum = gain_sum + jnp.sum(g * v * r, axis=0, keepdims=True)
        to[...] = g.astype(to.dtype)
    gpar[:, ON : ON + D] = gain_sum

    devs = column(dev_row[...])
    sums = jnp.zeros((128, 128), F32)
    row = lax.broadcasted_iota(jnp.int32, (128, 256), 0)
    for i in range(NP // 256):
        cols = slice(i * 256, i * 256 + 256)
        one_hot = (row == lane_of[:, cols]).astype(BF)
        sums = sums + dot_t(jnp.where(devs == dev_of[:, cols], gpar[:, cols], 0.0).astype(BF), one_hot)
    sums = sums.astype(BF)
    for p in range(8):
        to, base = piece(g_mine, g_theirs, p, RA)
        to[base + 960 : base + 976, :] = sums[p * 16 : p * 16 + 16]
        to[base + 976 : base + 1024, :] = jnp.zeros((48, 128), BF)


def end_kernel(own, got1, got2, tok, rest, par, out):
    g = own[...] + got1[...].astype(F32) + got2[...].astype(F32)
    v = tok[...].astype(F32)
    r = lax.rsqrt(mean_of(v * v) + EPS)
    w = par[:, ON : ON + D] * g
    out[...] = rest[...] + r * w - v * (r * r * r * mean_of(w * v))


def run_first(args):
    return call(
        first_kernel,
        [
            sds((1, NP), F32), sds((WIN, D), BF),
            sds((3, 2, 512, HD), BF), sds((3, WIN, 2 * HD), BF), sds((3, TOK, HEADS * HD), BF),
        ],
        args,
        scratch=[
            pltpu.VMEM((D, 1024), BF), pltpu.VMEM((D, 512), BF), pltpu.VMEM((2, 128, 640), F32),
            pltpu.VMEM((2, 512, 640), F32), pltpu.VMEM((2, 512, 640), BF),
        ],
        in_specs=[SMEM] + [VMEM] * 12, mem=30, name="first", us=20,
    )


def run_middle(args):
    out_shape = [
        sds((3, TOK, D), F32), sds((TOK, D), F32), sds((3, TOK, HEADS * HD), BF),
        *[sds((RB, 128), BF)] * 8, sds((1, NP), F32),
    ]
    any_ = pl.BlockSpec(memory_space=pl.ANY)
    return pl.pallas_call(
        middle_kernel,
        out_shape=out_shape,
        in_specs=[SMEM, SMEM] + [VMEM] * 3 + [any_] * 8 + [VMEM] * 2,
        out_specs=[any_, VMEM, VMEM] + [any_] * 8 + [VMEM],
        scratch_shapes=[
            pltpu.VMEM((8, RB, 128), BF), pltpu.VMEM((D, 2 * FF), BF), pltpu.VMEM((FF, D), BF), pltpu.VMEM((1024, D), BF),
            pltpu.VMEM((1024, D), F32), pltpu.VMEM((2, TOK, 512), F32),
            pltpu.VMEM((TOK, FF), BF), pltpu.VMEM((TOK, FF), BF), pltpu.VMEM((TOK, FF), F32), pltpu.VMEM((TOK, FF), F32),
            pltpu.VMEM((3 * TOK, FF), BF), pltpu.VMEM((3 * TOK, FF), BF), pltpu.VMEM((3 * TOK, FF), BF),
            pltpu.VMEM((3 * TOK, D), BF), pltpu.VMEM((3 * TOK, D), BF), pltpu.VMEM((3 * TOK, D), BF),
            pltpu.VMEM((TOK, D), F32), pltpu.VMEM((TOK, D), F32), pltpu.VMEM((TOK, D), F32),
            pltpu.VMEM((D, D), BF), pltpu.VMEM((3, TOK, D), F32),
            pltpu.SemaphoreType.DMA((3, 8)), pltpu.SemaphoreType.DMA((4, 2, 8)), pltpu.SemaphoreType.DMA((2, 8)),
            pltpu.SemaphoreType.DMA,
        ],
        compiler_params=pltpu.CompilerParams(vmem_limit_bytes=55 << 20),
        cost_estimate=cost_of(70),
        name="middle",
    )(*args)


def run_back(args):
    return call(
        back_kernel,
        [
            sds((TOK, D), F32), sds((TOK, D), BF), sds((TOK, D), BF),
            sds((4 * RA, 128), BF), sds((4 * RA, 128), BF),
        ],
        args,
        scratch=[
            pltpu.VMEM((3, 2, 512, HD), BF), pltpu.VMEM((3, WIN, 512), BF), pltpu.VMEM((3, TOK, 1024), BF),
            pltpu.VMEM((4 * RA, 128), BF), pltpu.VMEM((4 * RA, 128), BF), pltpu.VMEM((WIN, D), BF), pltpu.VMEM((3, TOK, D), BF),
            pltpu.VMEM((2, 640, 128), F32), pltpu.VMEM((2, 640, 512), F32), pltpu.VMEM((2, 640, 512), F32),
            pltpu.VMEM((2, 640, 512), F32), pltpu.VMEM((2, 640, 512), F32),
            pltpu.VMEM((2, 640, 512), BF), pltpu.VMEM((2, 640, 512), BF),
            pltpu.VMEM((2, 512, HD), F32), pltpu.VMEM((WIN, 512), F32),
            pltpu.VMEM((TOK, 1024), F32), pltpu.VMEM((WIN, 512), F32), pltpu.VMEM((TOK, 1024), BF), pltpu.VMEM((WIN, 512), BF),
            pltpu.VMEM((D, 1024), BF), pltpu.VMEM((D, 512), BF), pltpu.VMEM((WIN, D), F32), pltpu.VMEM((1, NP), F32),
            pltpu.SemaphoreType.DMA((3, 3)), pltpu.SemaphoreType.DMA((6,)),
        ],
        in_specs=[SMEM] + [VMEM] * 9 + [pl.BlockSpec(memory_space=pl.ANY)] * 9, mem=46, name="back", us=30,
    )


def per_device(
    tokens, cotangent, segment_ids, width_mask,
    q_codes, kv_codes, o_codes, gate_codes, up_codes, down_codes,
    q_scale, kv_scale, o_scale, gate_scale, up_scale, down_scale, norm_gains,
):
    c, x, y = lax.axis_index("c"), lax.axis_index("x"), lax.axis_index("y")
    zl, zh = lax.axis_index("zl"), lax.axis_index("zh")
    z = zh * 2 + zl
    lane_of, dev_of = lane_tables()

    p, s = jnp.arange(128, dtype=jnp.int32) // 16, jnp.arange(128, dtype=jnp.int32) % 16
    shift = (s % 4, s // 4, p % 4)
    core = jnp.where(p < 4, c, 1 - c)
    sx, sy, sz = (
        (at - jnp.where(core == 0, shift[ORDER[0].index(a)], shift[ORDER[1].index(a)])) % 4 for at, a in ((x, "x"), (y, "y"), (z, "z"))
    )
    inat = ((((sz % 2) * 2 + core) * 2 + sz // 2) * 4 + sy) * 4 + sx
    dk = (5 * inat[None, :] + jnp.arange(5, dtype=jnp.int32)[:, None]).reshape(1, D)
    dev_row = inat[None, :]

    place = (y % 2) * 4 + x
    seq = zh * 2 + y // 2
    segs = lax.dynamic_slice_in_dim(segment_ids, seq, 1, 0)
    run = lax.dynamic_slice_in_dim(width_mask, seq, 1, 0)[0]
    padded = jnp.concatenate([jnp.full((1, WINDOW), -1, jnp.int32), segs], axis=1)
    segk = lax.dynamic_slice_in_dim(padded, place * TOK, WIN, 1)
    pos = (place * TOK - WINDOW + jnp.arange(WIN, dtype=jnp.int32)).astype(F32)
    inverse = 10000.0 ** (-2.0 * jnp.arange(HD // 2).astype(F32) / HD)
    angles = pos[:, None] * inverse[None, :]
    cos, sin = jnp.cos(angles), jnp.sin(angles)

    shard = call(
        pack_kernel, sds((N, 128), BF),
        (q_codes, kv_codes, o_codes, gate_codes, up_codes, down_codes, q_scale, kv_scale, o_scale, gate_scale, up_scale, down_scale, norm_gains.T),
        scratch=[pltpu.VMEM((N, 128), F32)], name="pack", us=0,
    )
    early = (run, inat, dk, dev_row, segk, cos, sin)
    mine_a, theirs_a, mine_b, their_first, t0, t1, early = gather(shard, tokens, early)
    run, inat, dk, dev_row, segk, cos, sin = early

    par, h1p, q, kv, mix = run_first((run, mine_a, theirs_a, dev_row, lane_of, dev_of, t0, t1, tokens, dk, cos, sin, segk))
    mix, *late = lax.optimization_barrier((mix, *mine_b[1:]))
    pieces_b = [mine_b[0], *late, their_first] + [other_core(b) for b in late]
    out, rest, gmix, *g_b, gpar = run_middle((run, inat, mix, tokens, cotangent, *pieces_b, par, dk))
    got_b = {r: other_core(g_b[4 + r]) for r in (2, 1, 3, 0)}
    hop = {r: call(add_kernel, sds((RB, 128), BF), (g_b[r], got_b[r]), name=f"add{r}", mem=24, us=0) for r in (2, 1, 3)}
    gpar, *hops = lax.optimization_barrier((gpar, hop[1], hop[2], hop[3]))
    hops = [send(a, 2, -r) for r, a in zip((1, 2, 3), hops)]
    own, back1, back2, gm_a, gt_a = run_back(
        (run, par, cos, sin, segk, gpar, dk, dev_row, lane_of, dev_of, q, kv, gmix, mine_a, theirs_a, h1p, t0, t1, tokens)
    )
    forth = lambda k: [(j, i) for i, j in behind(k)]
    gt_a, *hops = lax.optimization_barrier((gt_a, *hops))
    got1 = lax.ppermute(back1, ("y", "x"), forth(1))
    got2 = lax.ppermute(back2, ("y", "x"), forth(2))
    parts_a = first_hop(gm_a, other_core(gt_a), RA, 1, 0)
    gq, gkv, gate, up, down, o, *small = scatter(
        parts_a, [g_b[0], got_b[0], *hops],
        [sds((5, 1024), F32), sds((5, 512), F32), sds((5, FF), F32), sds((5, FF), F32), sds((16, D), F32), sds((8, D), F32),
         sds((8,), F32), sds((4,), F32), sds((5,), F32), sds((16,), F32), sds((16,), F32), sds((5,), F32), sds((4, 5), F32)],
    )
    grad_tokens = call(end_kernel, sds((TOK, D), F32), (own, got1, got2, tokens, rest, par), name="end", mem=24, us=0)

    return (out, grad_tokens, gq, gkv, o, gate, up, down, *small[:6], small[6].T)


def solution(mesh):
    fine = Mesh(mesh.devices.reshape(2, 2, 2, 4, 4), AX)
    rows, seqs = P(AX, None), P(("zl", "c"), None)
    wide = P(None, AX, None)
    return jax.shard_map(
        per_device,
        mesh=fine,
        in_specs=(rows, wide, seqs, seqs) + (rows,) * 6 + (P(AX),) * 6 + (rows,),
        out_specs=(wide, rows) + (rows,) * 6 + (P(AX),) * 6 + (rows,),
        check_vma=False,
    )
```

```python
import functools
import itertools
import math

import jax
import jax.numpy as jnp
import numpy as np
from jax import lax
from jax.experimental import pallas as pl
from jax.experimental.pallas import tpu as pltpu
from jax.sharding import Mesh
from jax.sharding import PartitionSpec as P

AX = ("zl", "c", "zh", "y", "x")
F32 = jnp.float32
BF = jnp.bfloat16
EPS = 1e-6
D, HEADS, HD, FF, WINDOW = 640, 4, 256, 2048, 512
TOK = 256
WIN = 768
ORDER = (("x", "y", "z"), ("y", "z", "x"))
NA = 64
NB = 288
N = NA + NB
INT_A, INT_B = 64, 160
RA, RB = 16 * NA, 16 * NB
DOWN_ROW, O_ROW = 2560, 3840
NP = 9472
SEG = dict(q=(0, 1024, 8, 0), kv=(1024, 512, 4, 8), o=(1536, 640, 5, 12), gate=(2176, 2048, 16, 17),
           up=(4224, 2048, 16, 33), down=(6272, 640, 5, 49))
OQ, OKV, OO, OG, OU, OD, ON = 0, 1024, 1536, 2176, 4224, 6272, 6912
U_D = 1.0 / (128.0 * math.sqrt(D))
U_O = 1.0 / (128.0 * math.sqrt(HEADS * HD))
U_F = 1.0 / (128.0 * math.sqrt(FF))
VMEM = pl.BlockSpec(memory_space=pltpu.VMEM)
SMEM = pl.BlockSpec(memory_space=pltpu.SMEM)


def lane_tables():
    lane, dev = np.zeros((1, NP), np.int32), np.zeros((1, NP), np.int32)
    for at, size, each, first in SEG.values():
        c = np.arange(size)
        lane[0, at : at + size] = first + c % each
        dev[0, at : at + size] = c // each
    for g in range(4):
        c = np.arange(D)
        at = ON + g * D
        lane[0, at : at + D] = 54 + g * 5 + c % 5
        dev[0, at : at + D] = c // 5
    return lane, dev


def cost_of(us):
    return pl.CostEstimate(flops=int(us * 1e6) + 1000, bytes_accessed=1000, transcendentals=0)


def call(kernel, out_shape, ins, scratch=(), mem=62, us=1, in_specs=None, name=None):
    params = dict(vmem_limit_bytes=mem << 20)
    return pl.pallas_call(
        kernel,
        out_shape=out_shape,
        in_specs=in_specs or [VMEM] * len(ins),
        out_specs=jax.tree.map(lambda s: VMEM, out_shape),
        scratch_shapes=list(scratch),
        compiler_params=pltpu.CompilerParams(**params),
        cost_estimate=cost_of(us),
        name=name,
    )(*ins)


def sds(shape, dtype):
    return jax.ShapeDtypeStruct(shape, dtype)


def dot(a, b):
    return jnp.dot(a, b, preferred_element_type=F32)


def dot_t(a, b):
    return lax.dot_general(a, b, (((1,), (1,)), ((), ())), preferred_element_type=F32)


def t_dot(a, b):
    return lax.dot_general(a, b, (((0,), (0,)), ((), ())), preferred_element_type=F32)


def flat(c, x, y, z):
    return ((((z & 1) * 2 + c) * 2 + (z >> 1)) * 4 + y) * 4 + x


@functools.lru_cache(None)
def stage_pairs(stage, r):
    pairs = []
    for c, x, y, z in itertools.product(range(2), range(4), range(4), range(4)):
        at = dict(x=x, y=y, z=z)
        axis = ORDER[c][stage]
        at[axis] = (at[axis] + r) % 4
        pairs.append((flat(c, x, y, z), flat(c, **at)))
    return tuple(sorted(pairs))


def send(a, stage, r):
    return lax.ppermute(a, AX, stage_pairs(stage, r % 4))


def behind(k):
    return [(i, i + k) for i in range(16) if i % 8 + k < 8]


def other_core(a):
    return lax.ppermute(a, "c", [(0, 1), (1, 0)])


def swap_matrix():
    row = lax.broadcasted_iota(jnp.int32, (256, 256), 0)
    col = lax.broadcasted_iota(jnp.int32, (256, 256), 1)
    return ((row % 16) * 16 + row // 16 == col).astype(BF)


BLOCKS = ((224, 80, DOWN_ROW), (304, 48, O_ROW))


def asm_kernel(*refs):
    ins, out_a, out_b = refs[:4], refs[4], refs[5]
    swap = swap_matrix()
    for g in range((INT_A + INT_B) // 16):
        x = jnp.concatenate(
            [ins[s // 4][(s % 4) * N + 16 * g : (s % 4) * N + 16 * g + 16, :] for s in range(16)], axis=0
        )
        y = dot(swap, x).astype(BF)
        if g < 4:
            out_a[256 * g : 256 * g + 256, :] = y
        else:
            out_b[256 * (g - 4) : 256 * (g - 4) + 256, :] = y
    for first, lines, row in BLOCKS:
        for s in range(16):
            at = (s % 4) * N + first
            out_b[row + s * lines : row + (s + 1) * lines, :] = ins[s // 4][at : at + lines, :]


def join_kernel(a, b, c, d, out):
    for r, ref in enumerate((a, b, c, d)):
        out[r * RA : (r + 1) * RA, :] = ref[...]


def gather(shard, tokens, early):
    one = jnp.concatenate([shard] + [send(shard, 0, r) for r in (1, 2, 3)], axis=0)
    t1, t0 = (lax.ppermute(tokens, ("y", "x"), behind(k)) for k in (1, 2))
    two = [one] + [send(one, 1, r) for r in (1, 2, 3)]
    two[0], t0, t1, *early = lax.optimization_barrier((two[0], t0, t1, *early))
    piece_a, piece_b = call(asm_kernel, [sds((RA, 128), BF), sds((RB, 128), BF)], two, name="asm", mem=24, us=0)
    mine_a = [piece_a] + [send(piece_a, 2, r) for r in (1, 2, 3)]
    mine_a = call(join_kernel, sds((4 * RA, 128), BF), mine_a, name="join", mem=24, us=0)
    theirs_a = other_core(mine_a)
    mine_b = [piece_b] + [send(piece_b, 2, r) for r in (1, 2, 3)]
    return mine_a, theirs_a, mine_b, other_core(piece_b), t0, t1, early


def rs1_kernel(a, b, *outs):
    for r in range(4):
        outs[r][...] = (a[r].astype(F32) + b[r].astype(F32)).astype(BF)


def total4(refs, at, rows):
    t = refs[0][at : at + rows, :].astype(F32)
    for ref in refs[1:]:
        t = t + ref[at : at + rows, :].astype(F32)
    return t


def add_kernel(a, b, out):
    out[...] = (a[...].astype(F32) + b[...].astype(F32)).astype(BF)


def rs2_kernel(*refs):
    a, b, outs = refs[:4], refs[4:9], refs[9:]
    swap = swap_matrix()
    for g in range((INT_A + INT_B) // 16):
        t = total4(a, 256 * g, 256) if g < 4 else total4(b, 256 * (g - 4), 256)
        y = dot(swap, t.astype(BF)).astype(BF)
        for s in range(16):
            at = (s % 4) * N + 16 * g
            outs[s // 4][at : at + 16, :] = y[16 * s : 16 * s + 16]
    for first, lines, row in BLOCKS:
        for s in range(16):
            at = (s % 4) * N + first
            outs[s // 4][at : at + lines, :] = total4(b, row + s * lines, lines).astype(BF)


def rs3_kernel(*refs):
    ins, outs = refs[:4], refs[4:]
    for r in range(4):
        outs[r][...] = total4(ins, r * N, N).astype(BF)


def rs4_kernel(a0, a1, a2, a3, q, kv, gate, up, down, o, *small):
    t = total4((a0, a1, a2, a3), 0, N)
    for cb in range(8):
        q[:, cb * 128 : cb * 128 + 128] = t[cb * 5 : cb * 5 + 5]
    for cb in range(4):
        kv[:, cb * 128 : cb * 128 + 128] = t[40 + cb * 5 : 45 + cb * 5]
    at = 0
    for ref in small[:6]:
        ref[...] = t[60, at : at + ref.shape[0]]
        at += ref.shape[0]
    for g in range(4):
        small[6][g : g + 1, :] = t[60:61, at + 5 * g : at + 5 * g + 5]
    for cb in range(16):
        gate[:, cb * 128 : cb * 128 + 128] = t[64 + cb * 5 : 69 + cb * 5]
        up[:, cb * 128 : cb * 128 + 128] = t[144 + cb * 5 : 149 + cb * 5]
    for cb in range(5):
        down[:, cb * 128 : cb * 128 + 128] = t[224 + cb * 16 : 240 + cb * 16]
        o[:, cb * 128 : cb * 128 + 128] = t[304 + cb * 8 : 312 + cb * 8]


def first_hop(mine, got, rows, grid, us):
    block = rows // grid
    parts = pl.pallas_call(
        rs1_kernel,
        grid=(grid,),
        out_shape=[sds((rows, 128), BF)] * 4,
        in_specs=[pl.BlockSpec((4, block, 128), lambda i: (0, i, 0))] * 2,
        out_specs=[pl.BlockSpec((block, 128), lambda i: (i, 0))] * 4,
        compiler_params=pltpu.CompilerParams(vmem_limit_bytes=24 << 20),
        cost_estimate=cost_of(us),
        name=f"rs1_{rows}",
    )(mine.reshape(4, rows, 128), got.reshape(4, rows, 128))
    return [parts[0]] + [send(parts[r], 2, -r) for r in (1, 2, 3)]


def scatter(a, b, out_shape):
    parts = call(rs2_kernel, [sds((4 * N, 128), BF)] * 4, a + b, name="rs2", mem=24, us=0)
    parts = [parts[0]] + [send(parts[r], 1, -r) for r in (1, 2, 3)]
    parts = call(rs3_kernel, [sds((N, 128), BF)] * 4, parts, name="rs3", mem=24, us=0)
    parts = [parts[0]] + [send(parts[r], 0, -r) for r in (1, 2, 3)]
    return call(rs4_kernel, out_shape, parts, name="rs4", mem=24, us=0)


def pack_kernel(q, kv, o, gate, up, down, sq, skv, so, sg, su, sd, gains, out, wide):
    for cb in range(8):
        wide[cb * 5 : cb * 5 + 5, :] = q[:, cb * 128 : cb * 128 + 128].astype(F32)
    for cb in range(4):
        wide[40 + cb * 5 : 45 + cb * 5, :] = kv[:, cb * 128 : cb * 128 + 128].astype(F32)
    row = [ref[...].reshape(1, -1) for ref in (sq, skv, so, sg, su, sd)] + [gains[g : g + 1, :] for g in range(4)]
    v = jnp.concatenate(row + [jnp.zeros((1, 54), F32)], axis=1)
    hi = v.astype(BF).astype(F32)
    mid = (v - hi).astype(BF).astype(F32)
    wide[60:61, :] = hi
    wide[61:62, :] = mid
    wide[62:63, :] = v - hi - mid
    wide[63:64, :] = jnp.zeros((1, 128), F32)
    for cb in range(16):
        wide[64 + cb * 5 : 69 + cb * 5, :] = gate[:, cb * 128 : cb * 128 + 128].astype(F32)
        wide[144 + cb * 5 : 149 + cb * 5, :] = up[:, cb * 128 : cb * 128 + 128].astype(F32)
    for cb in range(5):
        wide[224 + cb * 16 : 240 + cb * 16, :] = down[:, cb * 128 : cb * 128 + 128].astype(F32)
        wide[304 + cb * 8 : 312 + cb * 8, :] = o[:, cb * 128 : cb * 128 + 128].astype(F32)
    wide[344:352, :] = jnp.zeros((8, 128), F32)
    out[...] = wide[...].astype(BF)


def piece(mine, theirs, p, rows):
    return (mine if p < 4 else theirs), (p % 4) * rows


def perm_matrix(dk):
    return (lax.broadcasted_iota(jnp.int32, (D, D), 0) == dk).astype(BF)


def steps_of(b):
    step = jnp.where(b == 0, 1.0, jnp.where(b == 1, 16.0, 64.0)).astype(F32)
    inv = jnp.where(b == 0, 1.0, jnp.where(b == 1, 1.0 / 16, 1.0 / 64)).astype(F32)
    return step, inv


def level_maker(b, rows=16, dtype=BF):
    step, inv = steps_of(b)
    step_v = jnp.full((rows, 128), step, F32)
    inv_v = jnp.full((rows, 128), inv, F32).astype(dtype)
    half_v = (step_v * 0.5).astype(dtype)
    step_v = step_v.astype(dtype)
    return lambda c: jnp.floor(c * inv_v) * step_v + half_v


def dequant_a(b, mine, theirs, lq, lkv):
    level = level_maker(b)
    for p in range(8):
        ref, base = piece(mine, theirs, p, RA)
        for j in range(5):
            for cb in range(8):
                at = base + (cb * 5 + j) * 16
                lq[j * 128 + p * 16 : j * 128 + p * 16 + 16, cb * 128 : cb * 128 + 128] = level(ref[at : at + 16, :])
            for cb in range(4):
                at = base + (40 + cb * 5 + j) * 16
                lkv[j * 128 + p * 16 : j * 128 + p * 16 + 16, cb * 128 : cb * 128 + 128] = level(ref[at : at + 16, :])


def column(row):
    n = row.shape[1]
    eye = lax.broadcasted_iota(jnp.int32, (n, n), 0) == lax.broadcasted_iota(jnp.int32, (n, n), 1)
    return jnp.sum(jnp.where(eye, row.astype(F32), 0.0), axis=1, keepdims=True).astype(jnp.int32)


def make_mask(segk, mask):
    for t in range(2):
        mine = column(segk[:, WINDOW + t * 128 : WINDOW + t * 128 + 128])
        r = lax.broadcasted_iota(jnp.int32, (128, 640), 0)
        c = lax.broadcasted_iota(jnp.int32, (128, 640), 1)
        ok = (c <= WINDOW + r) & (c > r)
        ok = ok & (mine == segk[:, t * 128 : t * 128 + 640])
        mask[t] = ok.astype(F32)


def rope(v, cos, sin):
    a, b = v[:, :128], v[:, 128:]
    return jnp.concatenate([a * cos - b * sin, b * cos + a * sin], axis=1)


def unrope(v, cos, sin):
    a, b = v[:, :128], v[:, 128:]
    return jnp.concatenate([a * cos + b * sin, b * cos - a * sin], axis=1)


TANH_IN = 1.0 / (16.0 * 50.0)
EXP2_IN = 50.0 * math.log2(math.e)


def first_kernel(
    run, mine, theirs, dev_row, lane_of, dev_of, t0, t1, t2, dk, cos, sin, segk,
    par, h1p, q_out, kv_out, mix_out, lq, lkv, mask, sc, ex,
):
    lines = []
    for l in (60, 61, 62):
        refs = [piece(mine, theirs, p, RA) for p in range(8)]
        lines.append(jnp.concatenate([ref[at + l * 16 : at + l * 16 + 16, :] for ref, at in refs], axis=0))
    lines = jnp.concatenate(lines, axis=1)
    devs = column(dev_row[...])
    row = lax.broadcasted_iota(jnp.int32, (128, 256), 0)
    for i in range(NP // 256):
        cols = slice(i * 256, i * 256 + 256)
        one_hot = (row == lane_of[:, cols]).astype(BF)
        t = dot(lines, jnp.concatenate([one_hot] * 3, axis=0))
        t = jnp.where(devs == dev_of[:, cols], t, 0.0)
        par[:, cols] = jnp.sum(t, axis=0, keepdims=True)
    perm = perm_matrix(dk[...])
    gain = par[:, ON : ON + D]
    for k, t in enumerate((t0, t1, t2)):
        v = t[...].astype(F32)
        h = v * lax.rsqrt(jnp.mean(v * v, axis=-1, keepdims=True) + EPS) * gain
        h1p[k * 256 : k * 256 + 256, :] = dot(h.astype(BF), perm).astype(BF)
    make_mask(segk, mask)

    def width(b, carry):
        @pl.when(run[b] == 0)
        def _():
            mix_out[b] = jnp.zeros((TOK, HEADS * HD), BF)

        @pl.when(run[b] > 0)
        def _():
            dequant_a(b, mine, theirs, lq, lkv)
            own = h1p[512:768, :]
            co, so = cos[512:768, :], sin[512:768, :]
            for h in range(4):
                scale = par[:, OQ + h * 256 : OQ + h * 256 + 256] * U_D
                q = rope(dot(own, lq[:, h * 256 : h * 256 + 256]) * scale, co, so).astype(BF)
                for t in range(2):
                    q_out[b, t, h * 128 : h * 128 + 128, :] = q[t * 128 : t * 128 + 128]
            for k in range(3):
                rows = h1p[k * 256 : k * 256 + 256, :]
                cw, sw = cos[k * 256 : k * 256 + 256, :], sin[k * 256 : k * 256 + 256, :]
                key = dot(rows, lkv[:, :256]) * (par[:, OKV : OKV + 256] * U_D)
                kv_out[b, k * 256 : k * 256 + 256, 0:256] = rope(key, cw, sw).astype(BF)
                val = dot(rows, lkv[:, 256:]) * (par[:, OKV + 256 : OKV + 512] * U_D)
                kv_out[b, k * 256 : k * 256 + 256, 256:512] = val.astype(BF)
            ones = jnp.ones((640, 128), BF)
            for t in range(2):
                sc[t] = dot_t(q_out[b, t], kv_out[b, t * 128 : t * 128 + 640, 0:256])
            for t in range(2):
                for i in range(16):
                    rows = slice(i * 32, i * 32 + 32)
                    m = mask[t, (i % 4) * 32 : (i % 4) * 32 + 32, :]
                    ex[t, rows, :] = (jnp.exp2(jnp.tanh(sc[t, rows, :] * TANH_IN) * EXP2_IN) * m).astype(BF)
                e = ex[t]
                inv = 1.0 / dot(e, ones)
                mixed = dot(e, kv_out[b, t * 128 : t * 128 + 640, 256:512]) * jnp.concatenate([inv, inv], axis=1)
                for h in range(4):
                    mix_out[b, t * 128 : t * 128 + 128, h * 256 : h * 256 + 256] = mixed[h * 128 : h * 128 + 128].astype(BF)

        return carry

    lax.fori_loop(0, 3, width, 0)


def mean_of(v):
    return jnp.mean(v, axis=-1, keepdims=True)


C_G = math.sqrt(2.0 / math.pi)
C_3 = C_G * 0.044715
PARTS = ((O_ROW, 768), (0, 2560), (DOWN_ROW, 1280))


def middle_kernel(
    run, inat, mix, tok, cot, b0, b1, b2, b3, b4, b5, b6, b7, par, dk,
    out, rest, gmix, g0, g1_, g2_, g3_, g4, g5, g6, g7, gpar,
    pcs, lgu, ld, lo, onat, gu32, gate, up, aa, bb, hid, gg, gu, h2s, gbr, gat, att, mid, acc, perm, outv,
    in_sem, gu_sem, do_sem, out_sem,
):
    dwd, dwo = ld, onat
    loads = [
        [
            pltpu.make_async_copy(ref.at[pl.ds(first, rows)], pcs.at[p, pl.ds(first, rows)], in_sem.at[k, p])
            for p, ref in enumerate((b0, b1, b2, b3, b4, b5, b6, b7))
        ]
        for k, (first, rows) in enumerate(PARTS)
    ]
    for group in loads:
        for copy in group:
            copy.start()
    perm[...] = perm_matrix(dk[...])
    rest[...] = jnp.zeros_like(rest)
    gpar[...] = jnp.zeros_like(gpar)
    for copy in loads[0]:
        copy.wait()
    for p in range(8):
        for s in range(16):
            at = O_ROW + s * 48
            block = pcs[p, at : at + 48, :].astype(F32)
            row = pl.multiple_of(inat[p * 16 + s] * 8, 8)
            for cb in range(5):
                onat[pl.ds(row, 8), cb * 128 : cb * 128 + 128] = block[cb * 8 : cb * 8 + 8]
    def width(b, carry):
        rows = pl.ds(pl.multiple_of(b * TOK, TOK), TOK)

        @pl.when(run[b] == 0)
        def _():
            outv[b] = jnp.zeros((TOK, D), F32)
            hid[rows, :] = jnp.zeros((TOK, FF), BF)
            gg[rows, :] = jnp.zeros((TOK, FF), BF)
            gu[rows, :] = jnp.zeros((TOK, FF), BF)
            h2s[rows, :] = jnp.zeros((TOK, D), BF)
            gbr[rows, :] = jnp.zeros((TOK, D), BF)
            gat[rows, :] = jnp.zeros((TOK, D), BF)

        @pl.when(run[b] > 0)
        def _():
            level = level_maker(b)
            wide = level_maker(b, 8, F32)
            for r in range(64):
                for cb in range(5):
                    two = [wide(onat[r * 16 + k * 8 : r * 16 + k * 8 + 8, cb * 128 : cb * 128 + 128]) for k in (0, 1)]
                    lo[r * 16 : r * 16 + 16, cb * 128 : cb * 128 + 128] = jnp.concatenate(two, axis=0).astype(BF)
            s_o = par[:, OO : OO + D] * U_O
            s_d = par[:, OD : OD + D] * U_F
            g1, g2, g3 = (par[:, ON + k * D : ON + (k + 1) * D] for k in (1, 2, 3))
            attended = dot(mix[b], lo[...]) * s_o
            att[...] = attended
            r1 = lax.rsqrt(mean_of(attended * attended) + EPS)
            middle = tok[...].astype(F32) + attended * r1 * g1
            mid[...] = middle
            r2 = lax.rsqrt(mean_of(middle * middle) + EPS)
            h2 = (middle * r2 * g2).astype(BF)
            h2p = dot(h2, perm[...]).astype(BF)
            h2s[rows, :] = h2p

            @pl.when(carry == 0)
            def _():
                for copy in loads[1] + loads[2]:
                    copy.wait()

            def gate_up(f):
                for half in range(2):
                    cb = f * 2 + half
                    for first, to in ((0, f * 512), (80, f * 512 + 256)):
                        for j in range(5):
                            for p in range(8):
                                at = (first + cb * 5 + j) * 16
                                k = j * 128 + p * 16
                                col = to + half * 128
                                lgu[k : k + 16, col : col + 128] = level(pcs[p, at : at + 16, :])
                gu32[f % 2] = dot(h2p, lgu[:, f * 512 : f * 512 + 512])

            gate_up(0)
            for p in range(8):
                for s in range(16):
                    row = pl.multiple_of(inat[p * 16 + s] * 16, 16)
                    for cb in range(5):
                        at = DOWN_ROW + s * 80 + cb * 16
                        ld[pl.ds(row, 16), cb * 128 : cb * 128 + 128] = level(pcs[p, at : at + 16, :])
            for f in range(8):
                if f < 7:
                    gate_up(f + 1)
                cols = slice(f * 256, f * 256 + 256)
                s_g, s_u = par[:, OG + f * 256 : OG + f * 256 + 256] * U_D, par[:, OU + f * 256 : OU + f * 256 + 256] * U_D
                parts = []
                for rc in range(8):
                    rr = slice(rc * 32, rc * 32 + 32)
                    x = gu32[f % 2, rr, 0:256] * s_g
                    u = gu32[f % 2, rr, 256:512] * s_u
                    gate[rr, cols] = x.astype(BF)
                    up[rr, cols] = u.astype(BF)
                    x2 = x * x
                    hf = 0.5 * jnp.tanh(x * (C_G + C_3 * x2)) + 0.5
                    gl = x * hf
                    aa[rr, cols] = u * (hf + (gl - gl * hf) * (2 * C_G + (6 * C_3) * x2))
                    bb[rr, cols] = gl
                    parts.append((gl * u).astype(BF))
                h = jnp.concatenate(parts, axis=0)
                hid[rows, cols] = h
                add = dot(h, ld[cols, :])
                acc[...] = add if f == 0 else acc[...] + add
            branch = acc[...] * s_d
            r3 = lax.rsqrt(mean_of(branch * branch) + EPS)
            outv[b] = mid[...] + branch * r3 * g3
            gy = cot[b].astype(F32)
            gpar[:, ON + 3 * D : ON + 4 * D] += jnp.sum(gy * branch * r3, axis=0, keepdims=True)
            w = g3 * gy
            gb = r3 * w - branch * (r3 * r3 * r3 * mean_of(w * branch))
            gpar[:, OD : OD + D] += jnp.sum(gb * branch, axis=0, keepdims=True)
            gb = (gb * s_d).astype(BF)
            gbr[rows, :] = gb

            def grad_hidden(f):
                gu32[f % 2, :, 0:256] = dot_t(gb, ld[f * 256 : f * 256 + 256, :])

            ones = jnp.ones((8, TOK), BF)
            grad_hidden(0)
            for f in range(8):
                if f < 7:
                    grad_hidden(f + 1)
                cols = slice(f * 256, f * 256 + 256)
                col_g, col_u = slice(OG + f * 256, OG + f * 256 + 256), slice(OU + f * 256, OU + f * 256 + 256)
                s_g, s_u = par[:, col_g] * U_D, par[:, col_u] * U_D
                parts, prods = [], []
                for rc in range(8):
                    rr = slice(rc * 32, rc * 32 + 32)
                    g = gu32[f % 2, rr, 0:256]
                    gg_b = (g * aa[rr, cols] * s_g).astype(BF)
                    gu_b = (g * bb[rr, cols] * s_u).astype(BF)
                    parts.append(jnp.concatenate([gg_b, gu_b], axis=1))
                    prods.append(jnp.concatenate([gg_b * gate[rr, cols], gu_b * up[rr, cols]], axis=1))
                both = jnp.concatenate(parts, axis=0)
                gg[rows, cols] = both[:, 0:256]
                gu[rows, cols] = both[:, 256:512]
                sums = dot(ones, jnp.concatenate(prods, axis=0))
                gpar[:, col_g] += sums[0:1, 0:256]
                gpar[:, col_u] += sums[0:1, 256:512]
                add = dot_t(both, lgu[:, f * 512 : f * 512 + 512])
                acc[...] = add if f == 0 else acc[...] + add
            g_h2 = dot_t(acc[...].astype(BF), perm[...])
            middle = mid[...]
            attended = att[...]
            gpar[:, ON + 2 * D : ON + 3 * D] += jnp.sum(g_h2 * middle * r2, axis=0, keepdims=True)
            w = g2 * g_h2
            gmid = cot[b].astype(F32) + r2 * w - middle * (r2 * r2 * r2 * mean_of(w * middle))
            rest[...] += gmid
            gpar[:, ON + D : ON + 2 * D] += jnp.sum(gmid * attended * r1, axis=0, keepdims=True)
            w = g1 * gmid
            ga = r1 * w - attended * (r1 * r1 * r1 * mean_of(w * attended))
            gpar[:, OO : OO + D] += jnp.sum(ga * attended, axis=0, keepdims=True)
            ga = (ga * s_o).astype(BF)
            gat[rows, :] = ga
            gmix[b] = dot_t(ga, lo[...]).astype(BF)

        return carry + run[b]

    lax.fori_loop(0, 3, width, 0)
    out_copy = pltpu.make_async_copy(outv, out, out_sem)
    out_copy.start()
    gpar[:, OO : OO + D] = gpar[:, OO : OO + D] / par[:, OO : OO + D]
    for at in (OG, OU):
        scale = par[:, at : at + FF]
        gpar[:, at : at + FF] = gpar[:, at : at + FF] / (scale * scale * U_D)
    gpar[:, OD : OD + D] = gpar[:, OD : OD + D] / par[:, OD : OD + D]

    stores = []

    def leave(p, first, rows, sem):
        to = (g0, g1_, g2_, g3_, g4, g5, g6, g7)[p]
        copy = pltpu.make_async_copy(pcs.at[p, pl.ds(first, rows)], to.at[pl.ds(first, rows)], sem)
        copy.start()
        stores.append(copy)

    g_all = gbr[...]
    for f in range(8):
        cols = slice(f * 256, f * 256 + 256)
        dwd[cols, :] = t_dot(hid[:, cols], g_all).astype(BF)
    for p in range(8):
        for s in range(16):
            row = pl.multiple_of(inat[p * 16 + s] * 16, 16)
            for cb in range(5):
                at = DOWN_ROW + s * 80 + cb * 16
                pcs[p, at : at + 16, :] = dwd[pl.ds(row, 16), cb * 128 : cb * 128 + 128]
        leave(p, DOWN_ROW, 1280, do_sem.at[0, p])
    for h in range(4):
        w = jnp.zeros((256, D), F32)
        for b in range(3):
            w = w + t_dot(mix[b, :, h * 256 : h * 256 + 256], gat[b * TOK : (b + 1) * TOK, :])
        dwo[h * 256 : h * 256 + 256, :] = w
    for p in range(8):
        for s in range(16):
            row = pl.multiple_of(inat[p * 16 + s] * 8, 8)
            parts = [dwo[pl.ds(row, 8), cb * 128 : cb * 128 + 128] for cb in range(5)] + [jnp.zeros((8, 128), F32)]
            at = O_ROW + s * 48
            pcs[p, at : at + 48, :] = jnp.concatenate(parts, axis=0).astype(BF)
        leave(p, O_ROW, 768, do_sem.at[1, p])
    h2t = h2s[...]
    for f in range(8):
        cols = slice(f * 256, f * 256 + 256)
        for k, (first, ref) in enumerate(((0, gg), (80, gu))):
            w = t_dot(h2t, ref[:, cols]).astype(BF)
            for half in range(2):
                for j in range(5):
                    for p in range(8):
                        at = (first + (f * 2 + half) * 5 + j) * 16
                        r = j * 128 + p * 16
                        pcs[p, at : at + 16, :] = w[r : r + 16, half * 128 : half * 128 + 128]
            if f % 2:
                for p in range(8):
                    leave(p, (first + (f - 1) * 10) * 16, 320, gu_sem.at[f // 2, k, p])
    for copy in stores:
        copy.wait()
    out_copy.wait()


def back_kernel(
    run, par, cos, sin, segk, gpar_in, dk, dev_row, lane_of, dev_of,
    q_far, kv_far, gmix_far, mine_far, theirs_far, h1p_far, t0_far, t1_far, t2_far,
    own, back1, back2, g_mine, g_theirs,
    q, kv, gmix, mine, theirs, h1p, toks, mask, sc, gp, ex, wt, pb, gz, gq, gkv, gq_sum, gkv_sum, gqb, gkvb, lq, lkv, gh1, gpar,
    sem, sem_late,
):
    loads = [
        [pltpu.make_async_copy(far.at[b], near.at[b], sem.at[b, k]) for k, (far, near) in enumerate(((q_far, q), (kv_far, kv), (gmix_far, gmix)))]
        for b in range(3)
    ]
    late = [
        pltpu.make_async_copy(far, near, sem_late.at[k])
        for k, (far, near) in enumerate(((mine_far, mine), (theirs_far, theirs), (h1p_far, h1p)))
    ]
    last = [pltpu.make_async_copy(far, toks.at[k], sem_late.at[3 + k]) for k, far in enumerate((t0_far, t1_far, t2_far))]
    for copy in loads[0] + late + loads[1] + loads[2] + last:
        copy.start()
    for t in range(2):
        k = lax.broadcasted_iota(jnp.int32, (640, 128), 0)
        r = lax.broadcasted_iota(jnp.int32, (640, 128), 1)
        ok = (k <= WINDOW + r) & (k > r)
        keys = jnp.concatenate([column(segk[:, (t + i) * 128 : (t + i + 1) * 128]) for i in range(5)], axis=0)
        ok = ok & (keys == segk[:, WINDOW + t * 128 : WINDOW + t * 128 + 128])
        mask[t] = ok.astype(F32)
    gpar[...] = gpar_in[...]
    gh1[...] = jnp.zeros_like(gh1)
    gq_sum[...] = jnp.zeros_like(gq_sum)
    gkv_sum[...] = jnp.zeros_like(gkv_sum)

    def width(b, seen):
        for k, (far, near) in enumerate(((q_far, q), (kv_far, kv), (gmix_far, gmix))):
            pltpu.make_async_copy(far.at[b], near.at[b], sem.at[b, k]).wait()

        @pl.when(run[b] > 0)
        def _():
            gkv[...] = jnp.zeros_like(gkv)
            gms = []
            for t in range(2):
                gm = jnp.concatenate(
                    [gmix[b, t * 128 : t * 128 + 128, h * 256 : h * 256 + 256] for h in range(4)], axis=0
                )
                gms.append(gm)
                sc[t] = dot_t(kv[b, t * 128 : t * 128 + 640, 0:256], q[b, t])
                gp[t] = dot_t(kv[b, t * 128 : t * 128 + 640, 256:512], gm)
            for t in range(2):
                for h in range(4):
                    cols = slice(h * 128, h * 128 + 128)
                    total, dot_sum = jnp.zeros((16, 128), F32), jnp.zeros((16, 128), F32)
                    for i in range(40):
                        rows = slice(i * 16, i * 16 + 16)
                        th = jnp.tanh(sc[t, rows, cols] * TANH_IN)
                        e = jnp.exp2(th * EXP2_IN) * mask[t, rows, :]
                        ex[t, rows, cols] = e
                        wt[t, rows, cols] = 1.0 - th * th
                        total = total + e
                        dot_sum = dot_sum + e * gp[t, rows, cols]
                    inv = 1.0 / jnp.sum(total, axis=0, keepdims=True)
                    dd = jnp.sum(dot_sum, axis=0, keepdims=True) * inv
                    inv, dd = jnp.broadcast_to(inv, (16, 128)), jnp.broadcast_to(dd, (16, 128))
                    for i in range(40):
                        rows = slice(i * 16, i * 16 + 16)
                        p = ex[t, rows, cols] * inv
                        pb[t, rows, cols] = p.astype(BF)
                        gz[t, rows, cols] = (p * (gp[t, rows, cols] - dd) * wt[t, rows, cols]).astype(BF)
                win = slice(t * 128, t * 128 + 640)
                gkv[win, 256:512] += dot(pb[t], gms[t])
                gkv[win, 0:256] += dot(gz[t], q[b, t]) * (1.0 / 16)
                gq[t] = t_dot(gz[t], kv[b, win, 0:256]) * (1.0 / 16)

            @pl.when(seen == 0)
            def _():
                for copy in late:
                    copy.wait()

            dequant_a(b, mine, theirs, lq, lkv)
            co, so = cos[512:768, :], sin[512:768, :]
            for h in range(4):
                cols = slice(h * 256, h * 256 + 256)
                g = unrope(jnp.concatenate([gq[t, h * 128 : h * 128 + 128, :] for t in (0, 1)], axis=0), co, so)
                raw = jnp.concatenate([q[b, t, h * 128 : h * 128 + 128, :] for t in (0, 1)], axis=0)
                raw = unrope(raw.astype(F32), co, so)
                gpar[:, OQ + h * 256 : OQ + h * 256 + 256] += jnp.sum(g * raw, axis=0, keepdims=True)
                g = g * (par[:, OQ + h * 256 : OQ + h * 256 + 256] * U_D)
                gq_sum[:, cols] += g
                gqb[:, cols] = g.astype(BF)
            for w in range(3):
                rows = slice(w * 256, w * 256 + 256)
                cw, sw = cos[rows, :], sin[rows, :]
                for half in range(2):
                    cols = slice(half * 256, half * 256 + 256)
                    g = gkv[rows, cols]
                    raw = kv[b, rows, cols].astype(F32)
                    if half == 0:
                        g, raw = unrope(g, cw, sw), unrope(raw, cw, sw)
                    at = OKV + half * 256
                    gpar[:, at : at + 256] += jnp.sum(g * raw, axis=0, keepdims=True)
                    g = g * (par[:, at : at + 256] * U_D)
                    gkv_sum[rows, cols] += g
                    gkvb[rows, cols] = g.astype(BF)
            gh1[512:768, :] += dot_t(gqb[...], lq[...])
            for k in range(3):
                gh1[k * 256 : k * 256 + 256, :] += dot_t(gkvb[k * 256 : k * 256 + 256, :], lkv[...])

        return seen + run[b]

    lax.fori_loop(0, 3, width, 0)
    gpar[:, OQ : OQ + 1536] = gpar[:, OQ : OQ + 1536] / par[:, OQ : OQ + 1536]

    def put(w, first):
        for half in range(2):
            for j in range(5):
                for p in range(8):
                    to, base = piece(g_mine, g_theirs, p, RA)
                    at = base + (first + half * 5 + j) * 16
                    k = j * 128 + p * 16
                    to[at : at + 16, :] = w[k : k + 16, half * 128 : half * 128 + 128]

    gqb[...] = gq_sum[...].astype(BF)
    gkvb[...] = gkv_sum[...].astype(BF)
    for f in range(4):
        put(t_dot(h1p[512:768, :], gqb[:, f * 256 : f * 256 + 256]).astype(BF), f * 10)
    for f in range(2):
        put(t_dot(h1p[...], gkvb[:, f * 256 : f * 256 + 256]).astype(BF), 40 + f * 10)

    for copy in last:
        copy.wait()
    perm = perm_matrix(dk[...])
    gain_sum = jnp.zeros((1, D), F32)
    for k, to in enumerate((back2, back1, own)):
        g = dot_t(gh1[k * 256 : k * 256 + 256, :].astype(BF), perm)
        v = toks[k].astype(F32)
        r = lax.rsqrt(mean_of(v * v) + EPS)
        gain_sum = gain_sum + jnp.sum(g * v * r, axis=0, keepdims=True)
        to[...] = g.astype(to.dtype)
    gpar[:, ON : ON + D] = gain_sum

    devs = column(dev_row[...])
    sums = jnp.zeros((128, 128), F32)
    row = lax.broadcasted_iota(jnp.int32, (128, 256), 0)
    for i in range(NP // 256):
        cols = slice(i * 256, i * 256 + 256)
        one_hot = (row == lane_of[:, cols]).astype(BF)
        sums = sums + dot_t(jnp.where(devs == dev_of[:, cols], gpar[:, cols], 0.0).astype(BF), one_hot)
    sums = sums.astype(BF)
    for p in range(8):
        to, base = piece(g_mine, g_theirs, p, RA)
        to[base + 960 : base + 976, :] = sums[p * 16 : p * 16 + 16]
        to[base + 976 : base + 1024, :] = jnp.zeros((48, 128), BF)


def end_kernel(own, got1, got2, tok, rest, par, out):
    g = own[...] + got1[...].astype(F32) + got2[...].astype(F32)
    v = tok[...].astype(F32)
    r = lax.rsqrt(mean_of(v * v) + EPS)
    w = par[:, ON : ON + D] * g
    out[...] = rest[...] + r * w - v * (r * r * r * mean_of(w * v))


def run_first(args):
    return call(
        first_kernel,
        [
            sds((1, NP), F32), sds((WIN, D), BF),
            sds((3, 2, 512, HD), BF), sds((3, WIN, 2 * HD), BF), sds((3, TOK, HEADS * HD), BF),
        ],
        args,
        scratch=[
            pltpu.VMEM((D, 1024), BF), pltpu.VMEM((D, 512), BF), pltpu.VMEM((2, 128, 640), F32),
            pltpu.VMEM((2, 512, 640), F32), pltpu.VMEM((2, 512, 640), BF),
        ],
        in_specs=[SMEM] + [VMEM] * 12, mem=30, name="first", us=20,
    )


def run_middle(args):
    out_shape = [
        sds((3, TOK, D), F32), sds((TOK, D), F32), sds((3, TOK, HEADS * HD), BF),
        *[sds((RB, 128), BF)] * 8, sds((1, NP), F32),
    ]
    any_ = pl.BlockSpec(memory_space=pl.ANY)
    return pl.pallas_call(
        middle_kernel,
        out_shape=out_shape,
        in_specs=[SMEM, SMEM] + [VMEM] * 3 + [any_] * 8 + [VMEM] * 2,
        out_specs=[any_, VMEM, VMEM] + [any_] * 8 + [VMEM],
        scratch_shapes=[
            pltpu.VMEM((8, RB, 128), BF), pltpu.VMEM((D, 2 * FF), BF), pltpu.VMEM((FF, D), BF), pltpu.VMEM((1024, D), BF),
            pltpu.VMEM((1024, D), F32), pltpu.VMEM((2, TOK, 512), F32),
            pltpu.VMEM((TOK, FF), BF), pltpu.VMEM((TOK, FF), BF), pltpu.VMEM((TOK, FF), F32), pltpu.VMEM((TOK, FF), F32),
            pltpu.VMEM((3 * TOK, FF), BF), pltpu.VMEM((3 * TOK, FF), BF), pltpu.VMEM((3 * TOK, FF), BF),
            pltpu.VMEM((3 * TOK, D), BF), pltpu.VMEM((3 * TOK, D), BF), pltpu.VMEM((3 * TOK, D), BF),
            pltpu.VMEM((TOK, D), F32), pltpu.VMEM((TOK, D), F32), pltpu.VMEM((TOK, D), F32),
            pltpu.VMEM((D, D), BF), pltpu.VMEM((3, TOK, D), F32),
            pltpu.SemaphoreType.DMA((3, 8)), pltpu.SemaphoreType.DMA((4, 2, 8)), pltpu.SemaphoreType.DMA((2, 8)),
            pltpu.SemaphoreType.DMA,
        ],
        compiler_params=pltpu.CompilerParams(vmem_limit_bytes=55 << 20),
        cost_estimate=cost_of(70),
        name="middle",
    )(*args)


def run_back(args):
    return call(
        back_kernel,
        [
            sds((TOK, D), F32), sds((TOK, D), BF), sds((TOK, D), BF),
            sds((4 * RA, 128), BF), sds((4 * RA, 128), BF),
        ],
        args,
        scratch=[
            pltpu.VMEM((3, 2, 512, HD), BF), pltpu.VMEM((3, WIN, 512), BF), pltpu.VMEM((3, TOK, 1024), BF),
            pltpu.VMEM((4 * RA, 128), BF), pltpu.VMEM((4 * RA, 128), BF), pltpu.VMEM((WIN, D), BF), pltpu.VMEM((3, TOK, D), BF),
            pltpu.VMEM((2, 640, 128), F32), pltpu.VMEM((2, 640, 512), F32), pltpu.VMEM((2, 640, 512), F32),
            pltpu.VMEM((2, 640, 512), F32), pltpu.VMEM((2, 640, 512), F32),
            pltpu.VMEM((2, 640, 512), BF), pltpu.VMEM((2, 640, 512), BF),
            pltpu.VMEM((2, 512, HD), F32), pltpu.VMEM((WIN, 512), F32),
            pltpu.VMEM((TOK, 1024), F32), pltpu.VMEM((WIN, 512), F32), pltpu.VMEM((TOK, 1024), BF), pltpu.VMEM((WIN, 512), BF),
            pltpu.VMEM((D, 1024), BF), pltpu.VMEM((D, 512), BF), pltpu.VMEM((WIN, D), F32), pltpu.VMEM((1, NP), F32),
            pltpu.SemaphoreType.DMA((3, 3)), pltpu.SemaphoreType.DMA((6,)),
        ],
        in_specs=[SMEM] + [VMEM] * 9 + [pl.BlockSpec(memory_space=pl.ANY)] * 9, mem=40, name="back", us=30,
    )


def per_device(
    tokens, cotangent, segment_ids, width_mask,
    q_codes, kv_codes, o_codes, gate_codes, up_codes, down_codes,
    q_scale, kv_scale, o_scale, gate_scale, up_scale, down_scale, norm_gains,
):
    c, x, y = lax.axis_index("c"), lax.axis_index("x"), lax.axis_index("y")
    zl, zh = lax.axis_index("zl"), lax.axis_index("zh")
    z = zh * 2 + zl
    lane_of, dev_of = lane_tables()

    p, s = jnp.arange(128, dtype=jnp.int32) // 16, jnp.arange(128, dtype=jnp.int32) % 16
    shift = (s % 4, s // 4, p % 4)
    core = jnp.where(p < 4, c, 1 - c)
    sx, sy, sz = (
        (at - jnp.where(core == 0, shift[ORDER[0].index(a)], shift[ORDER[1].index(a)])) % 4 for at, a in ((x, "x"), (y, "y"), (z, "z"))
    )
    inat = ((((sz % 2) * 2 + core) * 2 + sz // 2) * 4 + sy) * 4 + sx
    dk = (5 * inat[None, :] + jnp.arange(5, dtype=jnp.int32)[:, None]).reshape(1, D)
    dev_row = inat[None, :]

    place = (y % 2) * 4 + x
    seq = zh * 2 + y // 2
    segs = lax.dynamic_slice_in_dim(segment_ids, seq, 1, 0)
    run = lax.dynamic_slice_in_dim(width_mask, seq, 1, 0)[0]
    padded = jnp.concatenate([jnp.full((1, WINDOW), -1, jnp.int32), segs], axis=1)
    segk = lax.dynamic_slice_in_dim(padded, place * TOK, WIN, 1)
    pos = (place * TOK - WINDOW + jnp.arange(WIN, dtype=jnp.int32)).astype(F32)
    inverse = 10000.0 ** (-2.0 * jnp.arange(HD // 2).astype(F32) / HD)
    angles = pos[:, None] * inverse[None, :]
    cos, sin = jnp.cos(angles), jnp.sin(angles)

    shard = call(
        pack_kernel, sds((N, 128), BF),
        (q_codes, kv_codes, o_codes, gate_codes, up_codes, down_codes, q_scale, kv_scale, o_scale, gate_scale, up_scale, down_scale, norm_gains.T),
        scratch=[pltpu.VMEM((N, 128), F32)], name="pack", us=0,
    )
    early = (run, inat, dk, dev_row, segk, cos, sin)
    mine_a, theirs_a, mine_b, their_first, t0, t1, early = gather(shard, tokens, early)
    run, inat, dk, dev_row, segk, cos, sin = early

    par, h1p, q, kv, mix = run_first((run, mine_a, theirs_a, dev_row, lane_of, dev_of, t0, t1, tokens, dk, cos, sin, segk))
    mix, *late = lax.optimization_barrier((mix, *mine_b[1:]))
    pieces_b = [mine_b[0], *late, their_first] + [other_core(b) for b in late]
    out, rest, gmix, *g_b, gpar = run_middle((run, inat, mix, tokens, cotangent, *pieces_b, par, dk))
    got_b = {r: other_core(g_b[4 + r]) for r in (2, 1, 3, 0)}
    hop = {r: call(add_kernel, sds((RB, 128), BF), (g_b[r], got_b[r]), name=f"add{r}", mem=24, us=0) for r in (2, 1, 3)}
    gpar, *hops = lax.optimization_barrier((gpar, hop[1], hop[2], hop[3]))
    hops = [send(a, 2, -r) for r, a in zip((1, 2, 3), hops)]
    own, back1, back2, gm_a, gt_a = run_back(
        (run, par, cos, sin, segk, gpar, dk, dev_row, lane_of, dev_of, q, kv, gmix, mine_a, theirs_a, h1p, t0, t1, tokens)
    )
    forth = lambda k: [(j, i) for i, j in behind(k)]
    gt_a, *hops = lax.optimization_barrier((gt_a, *hops))
    got1 = lax.ppermute(back1, ("y", "x"), forth(1))
    got2 = lax.ppermute(back2, ("y", "x"), forth(2))
    parts_a = first_hop(gm_a, other_core(gt_a), RA, 1, 0)
    gq, gkv, gate, up, down, o, *small = scatter(
        parts_a, [g_b[0], got_b[0], *hops],
        [sds((5, 1024), F32), sds((5, 512), F32), sds((5, FF), F32), sds((5, FF), F32), sds((16, D), F32), sds((8, D), F32),
         sds((8,), F32), sds((4,), F32), sds((5,), F32), sds((16,), F32), sds((16,), F32), sds((5,), F32), sds((4, 5), F32)],
    )
    grad_tokens = call(end_kernel, sds((TOK, D), F32), (own, got1, got2, tokens, rest, par), name="end", mem=24, us=0)

    return (out, grad_tokens, gq, gkv, o, gate, up, down, *small[:6], small[6].T)


def solution(mesh):
    fine = Mesh(mesh.devices.reshape(2, 2, 2, 4, 4), AX)
    rows, seqs = P(AX, None), P(("zl", "c"), None)
    wide = P(None, AX, None)
    return jax.shard_map(
        per_device,
        mesh=fine,
        in_specs=(rows, wide, seqs, seqs) + (rows,) * 6 + (P(AX),) * 6 + (rows,),
        out_specs=(wide, rows) + (rows,) * 6 + (P(AX),) * 6 + (rows,),
        check_vma=False,
    )
```
